32 devices in a mesh: dp: 8 (over z, core), ctx: 4 (over y, x).
Axes of the slice: x: 2, y: 2, z: 4, core: 2. Of those that a mesh axis runs over, the one named last changes fastest.
Arguments:
- tokens: bfloat16 [8, 1024, 1024], P('dp', 'ctx'), may hold values from -6 to 6
- cotangent: bfloat16 [8, 1024, 1024], P('dp', 'ctx'), may hold values from -6 to 6
- routes: int32 [8, 1024, 1], P('dp', 'ctx'), may hold values from 0 to 1; in each aligned block of 256 rows (0 to 255, 256 to 511, ..., all dimensions but the last counted through in order) at most 160 rows name the same one
- ln1_gain: bfloat16 [1024], P(('dp', 'ctx')), may hold values from 0.5 to 1.5
- ln1_bias: bfloat16 [1024], P(('dp', 'ctx')), may hold values from -4 to 4
- qkv_weight: bfloat16 [1024, 3072], P(('dp', 'ctx')), may hold values from -0.1875 to 0.1875
- qv_bias: bfloat16 [2048], P(('dp', 'ctx')), may hold values from -4 to 4
- out_weight: bfloat16 [1024, 1024], P(('dp', 'ctx')), may hold values from -3 to 3
- out_bias: bfloat16 [1024], P(('dp', 'ctx')), may hold values from -4 to 4
- ln2_gain: bfloat16 [1024], P(('dp', 'ctx')), may hold values from 0.5 to 1.5
- ln2_bias: bfloat16 [1024], P(('dp', 'ctx')), may hold values from -4 to 4
- up_weight: bfloat16 [1024, 4096], P(('dp', 'ctx')), may hold values from -0.1875 to 0.1875
- up_bias: bfloat16 [4096], P(('dp', 'ctx')), may hold values from -4 to 4
- down_weight: bfloat16 [4096, 1024], P(('dp', 'ctx')), may hold values from -0.25 to 0.25
- down_bias: bfloat16 [1024], P(('dp', 'ctx')), may hold values from -4 to 4
- router_weight: bfloat16 [1024, 2], P(('dp', 'ctx')), may hold values from -0.375 to 0.375
- mix_weight: bfloat16 [1024, 2], P(('dp', 'ctx')), may hold values from -0.4375 to 0.4375
- expert_up: bfloat16 [2, 1024, 4096], P(None, ('dp', 'ctx')), may hold values from -0.1875 to 0.1875
- expert_up_bias: bfloat16 [2, 4096], P(None, ('dp', 'ctx')), may hold values from -4 to 4
- expert_down: bfloat16 [2, 4096, 1024], P(None, ('dp', 'ctx')), may hold values from -0.375 to 0.375
- expert_down_bias: bfloat16 [2, 1024], P(None, ('dp', 'ctx')), may hold values from -4 to 4
Outputs:
- result: float32 [8, 1024, 1024], P('dp', 'ctx')
- tokens_grad: float32 [8, 1024, 1024], P('dp', 'ctx')
- ln1_gain_grad: float32 [1024], P(('dp', 'ctx'))
- ln1_bias_grad: float32 [1024], P(('dp', 'ctx'))
- qkv_weight_grad: float32 [1024, 3072], P(('dp', 'ctx'))
- qv_bias_grad: float32 [2048], P(('dp', 'ctx'))
- out_weight_grad: float32 [1024, 1024], P(('dp', 'ctx'))
- out_bias_grad: float32 [1024], P(('dp', 'ctx'))
- ln2_gain_grad: float32 [1024], P(('dp', 'ctx'))
- ln2_bias_grad: float32 [1024], P(('dp', 'ctx'))
- up_weight_grad: float32 [1024, 4096], P(('dp', 'ctx'))
- up_bias_grad: float32 [4096], P(('dp', 'ctx'))
- down_weight_grad: float32 [4096, 1024], P(('dp', 'ctx'))
- down_bias_grad: float32 [1024], P(('dp', 'ctx'))
- router_weight_grad: float32 [1024, 2], P(('dp', 'ctx'))
- mix_weight_grad: float32 [1024, 2], P(('dp', 'ctx'))
- expert_up_grad: float32 [2, 1024, 4096], P(None, ('dp', 'ctx'))
- expert_up_bias_grad: float32 [2, 4096], P(None, ('dp', 'ctx'))
- expert_down_grad: float32 [2, 4096, 1024], P(None, ('dp', 'ctx'))
- expert_down_bias_grad: float32 [2, 1024], P(None, ('dp', 'ctx'))
The draws below stay inside these ranges and needn't reach their ends.
Inputs may be any that keep to these rules, and one draw needn't show every extreme that they name: `routes`: in each aligned block of 256 tokens (one sequence's tokens on one device) each expert is named by at most 160 tokens, and in some blocks exactly 160.
All inputs are finite; a program needn't handle non-finite values.
Results may differ from the reference program's by a relative error of at most 0.01.
The reference program's roundings to bfloat16 on the way count: a program that leaves them out, or rounds other values in their place, can miss the bound.
Values may be sent and summed in bfloat16 or wider, within the bound.
No kernel may reach another device: no remote copies, remote signals or barrier semaphores. Data moves between devices by JAX's collectives and lax.ppermute only.
A program may use at most 320 MiB of HBM per device.

```python
import math
import jax
import jax.numpy as jnp
import numpy as np
from jax import lax

D = 1024
HEADS = 16
HEAD_DIM = 64
FF = 4096
EXPERTS = 2
LEN = 1024
ROWS = 256
CAP = 160
SEQS = 8


def block_levels(own_key, extent, shards, low, high):
    def one(position, parts):
        steps = jax.random.uniform(jax.random.fold_in(jax.random.fold_in(own_key, 6), position), (parts,), jnp.float32, low / len(shards), high / len(shards))
        return jnp.repeat(jnp.exp(steps), extent[position] // parts).reshape((-1,) + (1,) * (len(extent) - position - 1))

    loudness = one(*shards[0])
    for cut in shards[1:]:
        loudness = loudness * one(*cut)
    return loudness


def assign_block(own_key, own, number, rows, amount, top, bound, skew):
    order = jax.random.permutation(own_key, amount)
    heavy_load, common = load_shares(amount, rows * top, bound, skew, True), load_shares(amount, rows * top, bound, skew, False)
    places = jnp.arange(amount)

    def named(sizes, rotation):
        used = int((sizes > 0).sum())
        fixed = max(1, used // 4)
        shifted = fixed + (places - fixed + rotation * (used - fixed)) % max(1, amount - fixed)
        return jnp.zeros((amount,), jnp.int32).at[order[jnp.where(places < fixed, places, shifted)]].set(jnp.asarray(sizes, jnp.int32))

    sizes = jnp.where(number % 4 == 0, named(heavy_load, number // 4), named(common, number - number // 4 - 1))
    mixed = jax.random.permutation(jax.random.fold_in(own, 3), amount)
    giver, receiver = mixed[0:amount // 2 * 2:2], mixed[1:amount // 2 * 2:2]
    room = jnp.minimum(sizes[giver] - 1, bound - sizes[receiver]) // 2
    room = jnp.where((giver == order[0]) | (receiver == order[0]) | (sizes[receiver] == 0), 0, jnp.maximum(room, 0))
    shifted = jax.random.randint(jax.random.fold_in(own, 4), (amount // 2,), 0, 1 << 20) % (room + 1)
    sizes = sizes.at[giver].add(-shifted).at[receiver].add(shifted)
    labels = jnp.searchsorted(jnp.cumsum(sizes), jnp.arange(rows * top), side="right").astype(jnp.int32)
    grid = labels.reshape(top, rows).T
    grid = grid[jax.random.permutation(jax.random.fold_in(own, 1), rows)]
    rotation = jax.random.randint(jax.random.fold_in(own, 2), (rows, 1), 0, top)
    return jnp.take_along_axis(grid, (jnp.arange(top)[None, :] + rotation) % top, axis=1)


def load_shares(number_of, total, bound, skew, full):
    portions = [(1 << 20) // math.isqrt(rank ** skew) + 1 for rank in range(1, number_of + 1)]
    largest = bound if full else min(bound, max(-(-total // number_of), total * portions[0] // sum(portions)))
    least = 1 if total - largest >= number_of - 1 else 0
    counts, spare = [largest] + [least] * (number_of - 1), total - largest - least * (number_of - 1)
    while spare > 0:
        free = [i for i in range(1, number_of) if counts[i] < largest] or [i for i in range(1, number_of) if counts[i] < bound]
        pool, left = sum([portions[i] for i in free]), spare
        for i in free:
            more = min(bound - counts[i], max(1, left * portions[i] // pool), spare)
            counts[i] = counts[i] + more
            spare = spare - more
    return np.array(counts)


def gaussian(stream_key, extent, deviation, limit, cuts=(), kind=jnp.bfloat16):
    values = deviation * jax.random.normal(stream_key, extent, jnp.float32)
    if cuts:
        values = values * block_levels(stream_key, extent, cuts, -0.22, 0.18)
    return jnp.clip(values, -limit, limit).astype(kind)


def setup_inputs(seed: int = 0) -> dict:
    splits = jax.random.split(jax.random.key(seed), 22)
    tokens = gaussian(splits[0], (SEQS, LEN, D), 1.0, 6.0, ((0, 8), (1, 4)))
    cotangent = gaussian(splits[1], (SEQS, LEN, D), 1.0, 6.0, ((0, 8), (1, 4)))
    routes_keys = jax.random.split(jax.random.fold_in(splits[2], 1), SEQS * LEN // ROWS)
    routes_turns = jax.random.permutation(jax.random.fold_in(splits[2], 3), SEQS * LEN // ROWS)
    routes = jax.vmap(lambda own, number: assign_block(jax.random.fold_in(splits[2], 2), own, number, ROWS, EXPERTS, 1, CAP, 0))(routes_keys, routes_turns).reshape((SEQS, LEN, 1))
    ln1_gain = jnp.clip(1.0 + 0.1 * jax.random.normal(splits[3], (D,), jnp.float32), 0.5, 1.5).astype(jnp.bfloat16)
    ln1_bias = gaussian(splits[4], (D,), 0.3, 4.0, ((0, 32),))
    qkv_weight = gaussian(splits[5], (D, 3 * D), D ** -0.5, 0.1875, ((0, 32),))
    qv_bias = gaussian(splits[6], (2 * D,), 0.3, 4.0, ((0, 32),))
    out_weight = gaussian(splits[7], (D, D), (max(1, D // 256)) ** -0.5, 3.0, ((0, 32),))
    out_bias = gaussian(splits[8], (D,), 0.3, 4.0, ((0, 32),))
    ln2_gain = jnp.clip(1.0 + 0.1 * jax.random.normal(splits[9], (D,), jnp.float32), 0.5, 1.5).astype(jnp.bfloat16)
    ln2_bias = gaussian(splits[10], (D,), 0.3, 4.0, ((0, 32),))
    up_weight = gaussian(splits[11], (D, FF), D ** -0.5, 0.1875, ((0, 32),))
    up_bias = gaussian(splits[12], (FF,), 0.3, 4.0, ((0, 32),))
    down_weight = gaussian(splits[13], (FF, D), (FF // 8) ** -0.5, 0.25, ((0, 32),))
    down_bias = gaussian(splits[14], (D,), 0.3, 4.0, ((0, 32),))
    router_weight = gaussian(splits[15], (D, EXPERTS), 0.025, 0.375, ((0, 32),))
    mix_weight = gaussian(splits[16], (D, 2), 0.03, 0.4375, ((0, 32),))
    expert_up = gaussian(splits[17], (EXPERTS, D, FF), D ** -0.5, 0.1875, ((1, 32),))
    expert_up_bias = gaussian(splits[18], (EXPERTS, FF), 0.3, 4.0, ((1, 32),))
    expert_down = gaussian(splits[19], (EXPERTS, FF, D), (FF // 16) ** -0.5, 0.375, ((1, 32),))
    expert_down_bias = gaussian(splits[20], (EXPERTS, D), 0.3, 4.0, ((1, 32),))
    return {"tokens": tokens, "cotangent": cotangent, "routes": routes, "ln1_gain": ln1_gain, "ln1_bias": ln1_bias, "qkv_weight": qkv_weight, "qv_bias": qv_bias, "out_weight": out_weight, "out_bias": out_bias, "ln2_gain": ln2_gain, "ln2_bias": ln2_bias, "up_weight": up_weight, "up_bias": up_bias, "down_weight": down_weight, "down_bias": down_bias, "router_weight": router_weight, "mix_weight": mix_weight, "expert_up": expert_up, "expert_up_bias": expert_up_bias, "expert_down": expert_down, "expert_down_bias": expert_down_bias}


highest = lax.Precision.HIGHEST

@jax.custom_vjp
def low(v):
    return lax.optimization_barrier(v.astype(jnp.bfloat16)).astype(jnp.float32)

@jax.custom_vjp
def low_back(v):
    return v

def low_keep(v):
    return (low(v), None)

def low_pass(kept, grad):
    return (grad,)

def back_keep(v):
    return (v, None)

def back_low(kept, grad):
    return (low(grad),)
low.defvjp(low_keep, low_pass)
low_back.defvjp(back_keep, back_low)

def matmul(left_op, right_op):
    return jnp.dot(left_op, right_op, precision=highest, preferred_element_type=jnp.float32)

def layer_norm(values, gain, shift):
    row_mean = lax.optimization_barrier(jnp.mean(values, -1, keepdims=True))
    centred = values - row_mean
    inverse = lax.rsqrt(lax.optimization_barrier(jnp.mean(centred * centred, -1, keepdims=True)) + 1e-05)
    return centred * inverse * gain + shift

def group_forward(layer_weights, tok_group, route_group):
    gain_one, shift_one, qkv_weight, qv_bias, out_weight, out_bias, gain_two, shift_two, up_weight, up_bias, down_weight, down_bias, router_weight, mix_weight, expert_up, expert_up_bias, expert_down, expert_down_bias = layer_weights
    seq_count = tok_group.shape[0]
    length = tok_group.shape[1]
    flat_rows = tok_group.reshape(seq_count * length, D)
    attn_in = low(layer_norm(flat_rows, gain_one, shift_one))
    qkv_out = matmul(attn_in, qkv_weight)
    queries = low(low_back(qkv_out[:, :D] + qv_bias[:D])).reshape(seq_count, length, HEADS, HEAD_DIM)
    keys = low(low_back(qkv_out[:, D:2 * D])).reshape(seq_count, length, HEADS, HEAD_DIM)
    values = low(low_back(qkv_out[:, 2 * D:] + qv_bias[D:])).reshape(seq_count, length, HEADS, HEAD_DIM)
    raw_scores = low_back(jnp.einsum('sqhd,skhd->shqk', queries, keys, precision=highest) * HEAD_DIM ** (-0.5))
    positions = jnp.arange(length)
    allowed = positions[None, :] <= positions[:, None]
    masked = jnp.where(allowed, raw_scores, -1e+30)
    attn_probs = low(jax.nn.softmax(masked, axis=-1))
    attended = jnp.einsum('shqk,skhd->sqhd', attn_probs, values, precision=highest).reshape(seq_count * length, D)
    attended = low(low_back(attended))
    hidden_state = flat_rows + low_back(matmul(attended, out_weight) + out_bias)
    ffn_in = low(layer_norm(hidden_state, gain_two, shift_two))
    route_probs = jax.nn.softmax(matmul(ffn_in, router_weight), axis=-1)
    route_hot = (route_group.reshape(-1, 1) == jnp.arange(EXPERTS)[None, :]).astype(jnp.float32)
    gate_value = lax.optimization_barrier(jnp.sum(route_probs * route_hot, -1))
    mix_coef = jax.nn.softmax(matmul(ffn_in, mix_weight), axis=-1)
    up_dense = low_back(matmul(ffn_in, up_weight) + up_bias)
    out_dense = low_back(matmul(low(jax.nn.gelu(up_dense, approximate=True)), down_weight) + down_bias)
    moe_out = jnp.zeros_like(flat_rows)
    for expert in range(EXPERTS):
        exp_up = low_back(matmul(ffn_in, expert_up[expert]) + expert_up_bias[expert])
        exp_act = low(jax.nn.gelu(exp_up, approximate=True))
        exp_out = low_back(matmul(exp_act, expert_down[expert]) + expert_down_bias[expert])
        moe_out = moe_out + route_hot[:, expert:expert + 1] * exp_out
    branch_coef = mix_coef[:, 1] * gate_value
    result = hidden_state + mix_coef[:, 0:1] * out_dense + branch_coef[:, None] * moe_out
    return result.reshape(tok_group.shape)

def reference(tokens, cotangent, routes, ln1_gain, ln1_bias, qkv_weight, qv_bias, out_weight, out_bias, ln2_gain, ln2_bias, up_weight, up_bias, down_weight, down_bias, router_weight, mix_weight, expert_up, expert_up_bias, expert_down, expert_down_bias):
    layer_weights = tuple((weight_arg.astype(jnp.float32) for weight_arg in (ln1_gain, ln1_bias, qkv_weight, qv_bias, out_weight, out_bias, ln2_gain, ln2_bias, up_weight, up_bias, down_weight, down_bias, router_weight, mix_weight, expert_up, expert_up_bias, expert_down, expert_down_bias)))
    group_size = min(SEQS, max(1, 4096 // LEN))
    group_count = SEQS // group_size
    tok_groups = tokens.astype(jnp.float32).reshape(group_count, group_size, LEN, D)
    route_groups = routes.reshape(group_count, group_size, LEN)
    checked = jax.checkpoint(group_forward)

    def whole_layer(weight_set, tok_set):

        def scan_step(carry_val, pieces):
            return (carry_val, checked(weight_set, pieces[0], pieces[1]))
        unused, outputs = lax.scan(scan_step, jnp.zeros((), jnp.float32), (tok_set, route_groups))
        return outputs
    outputs, pull_back = jax.vjp(whole_layer, layer_weights, tok_groups)
    weight_grads, token_grads = pull_back(cotangent.astype(jnp.float32).reshape(outputs.shape))
    return (outputs.reshape(SEQS, LEN, D), token_grads.reshape(SEQS, LEN, D), weight_grads[0], weight_grads[1], weight_grads[2], weight_grads[3], weight_grads[4], weight_grads[5], weight_grads[6], weight_grads[7], weight_grads[8], weight_grads[9], weight_grads[10], weight_grads[11], weight_grads[12], weight_grads[13], weight_grads[14], weight_grads[15], weight_grads[16], weight_grads[17])
```

```python
import functools

import jax
import jax.numpy as jnp
from jax import lax
from jax.experimental import pallas as pl
from jax.experimental.pallas import tpu as pltpu
from jax.sharding import PartitionSpec as P

HEAD_DIM = 64
EPSILON = 1e-05
f32 = jnp.float32
bf16 = jnp.bfloat16
highest = lax.Precision.HIGHEST


def product(left_op, right_op):
    return jnp.dot(left_op, right_op, preferred_element_type=f32)


def left_product(left_op, right_op):
    return lax.dot_general(left_op, right_op, (((0,), (0,)), ((), ())), preferred_element_type=f32)


def right_product(left_op, right_op):
    return lax.dot_general(left_op, right_op, (((1,), (1,)), ((), ())), preferred_element_type=f32)


def layer_stats(values):
    row_mean = jnp.mean(values, -1, keepdims=True)
    centred = values - row_mean
    inverse = lax.rsqrt(jnp.mean(centred * centred, -1, keepdims=True) + EPSILON)
    return (centred * inverse, inverse)


def norm_back(grad_norm, normed, inverse, gain):
    scaled = grad_norm * gain
    return inverse * (
        scaled
        - jnp.mean(scaled, -1, keepdims=True)
        - normed * jnp.mean(scaled * normed, -1, keepdims=True)
    )


def gelu(pre_act):
    return jax.nn.gelu(pre_act, approximate=True)


def gelu_grad(pre_act, grad_act):
    return jax.vjp(gelu, pre_act)[1](grad_act)[0]


def score_parts(q_part, k_ref, column, step, block):
    scale = HEAD_DIM ** (-0.5)
    parts = []
    if step:
        parts.append(right_product(q_part, k_ref[0 : step * block, column]) * scale)
    diagonal = right_product(q_part, k_ref[step * block : (step + 1) * block, column]) * scale
    rows = lax.broadcasted_iota(jnp.int32, (block, block), 0)
    keys = lax.broadcasted_iota(jnp.int32, (block, block), 1)
    parts.append(jnp.where(keys <= rows, diagonal, -1e30))
    return parts


def softmax_of(parts):
    row_max = functools.reduce(jnp.maximum, [jnp.max(part, -1, keepdims=True) for part in parts])
    terms = [jnp.exp(part - row_max) for part in parts]
    total = functools.reduce(jnp.add, [jnp.sum(term, -1, keepdims=True) for term in terms])
    inverse = 1.0 / total
    return [term * inverse for term in terms]


def key_spans(step, block):
    spans = [slice(0, step * block)] if step else []
    return spans + [slice(step * block, (step + 1) * block)]


def attention_forward_kernel(heads, block, q_ref, k_ref, v_ref, out_ref):
    for head in range(heads):
        column = slice(head * HEAD_DIM, (head + 1) * HEAD_DIM)
        for step in range(q_ref.shape[0] // block):
            rows = slice(step * block, (step + 1) * block)
            probs = softmax_of(score_parts(q_ref[rows, column], k_ref, column, step, block))
            mixed = functools.reduce(
                jnp.add,
                [
                    product(prob.astype(bf16), v_ref[span, column])
                    for prob, span in zip(probs, key_spans(step, block))
                ],
            )
            out_ref[rows, column] = mixed.astype(bf16)


def attention_backward_kernel(
    heads, block, q_ref, k_ref, v_ref, o_ref, dq_ref, dk_ref, dv_ref, k_acc, v_acc
):
    scale = HEAD_DIM ** (-0.5)
    for head in range(heads):
        column = slice(head * HEAD_DIM, (head + 1) * HEAD_DIM)
        for step in reversed(range(q_ref.shape[0] // block)):
            rows = slice(step * block, (step + 1) * block)
            spans = key_spans(step, block)
            q_part, o_part = q_ref[rows, column], o_ref[rows, column]
            probs = softmax_of(score_parts(q_part, k_ref, column, step, block))
            prob_grads = [right_product(o_part, v_ref[span, column]) for span in spans]
            delta = functools.reduce(
                jnp.add,
                [jnp.sum(p * g, -1, keepdims=True) for p, g in zip(probs, prob_grads)],
            )
            score_grads = [(p * (g - delta)).astype(bf16) for p, g in zip(probs, prob_grads)]
            q_grad = functools.reduce(
                jnp.add,
                [product(s, k_ref[span, column]) for s, span in zip(score_grads, spans)],
            )
            dq_ref[rows, column] = (q_grad * scale).astype(bf16)
            first = step == q_ref.shape[0] // block - 1
            for span, score_grad, prob in zip(spans, score_grads, probs):
                key_grad = left_product(score_grad, q_part)
                value_grad = left_product(prob.astype(bf16), o_part)
                k_acc[span, column] = key_grad if first else k_acc[span, column] + key_grad
                v_acc[span, column] = value_grad if first else v_acc[span, column] + value_grad
    dk_ref[...] = (k_acc[...] * scale).astype(bf16)
    dv_ref[...] = v_acc[...].astype(bf16)


def attention_plan(qkv, width):
    length = qkv.shape[0]
    heads = min(2, width // HEAD_DIM)
    block = min(256, length)
    lanes = heads * HEAD_DIM
    steps = width // lanes

    whole = lanes % 128 == 0
    joined = [qkv] * 3 if whole else [qkv[:, i * width : (i + 1) * width] for i in range(3)]

    def spec(part):
        first = part * steps if whole else 0
        return pl.BlockSpec((length, lanes), lambda step: (0, first + step))

    params = pltpu.CompilerParams(
        dimension_semantics=("arbitrary",), vmem_limit_bytes=48 * 1024 * 1024
    )
    return length, heads, block, lanes, steps, spec, params, joined


def attention_forward(qkv, width):
    length, heads, block, lanes, steps, spec, params, joined = attention_plan(qkv, width)
    return pl.pallas_call(
        functools.partial(attention_forward_kernel, heads, block),
        grid=(steps,),
        in_specs=[spec(0), spec(1), spec(2)],
        out_specs=spec(0),
        out_shape=jax.ShapeDtypeStruct((length, width), bf16),
        compiler_params=params,
        cost_estimate=pl.CostEstimate(
            flops=2 * length * length * width,
            bytes_accessed=8 * length * width,
            transcendentals=length * length * width // HEAD_DIM // 2,
        ),
        name="attention_forward",
    )(*joined)


def attention_backward(qkv, grad_attended, width):
    length, heads, block, lanes, steps, spec, params, joined = attention_plan(qkv, width)
    shape = jax.ShapeDtypeStruct((length, width), bf16)
    return pl.pallas_call(
        functools.partial(attention_backward_kernel, heads, block),
        grid=(steps,),
        in_specs=[spec(0), spec(1), spec(2), spec(0)],
        out_specs=[spec(0), spec(0), spec(0)],
        out_shape=[shape, shape, shape],
        scratch_shapes=[pltpu.VMEM((length, lanes), f32), pltpu.VMEM((length, lanes), f32)],
        compiler_params=params,
        cost_estimate=pl.CostEstimate(
            flops=5 * length * length * width,
            bytes_accessed=14 * length * width,
            transcendentals=length * length * width // HEAD_DIM // 2,
        ),
        name="attention_backward",
    )(*joined, grad_attended)


def layer(
    dp,
    ctx,
    tokens,
    cotangent,
    routes,
    ln1_gain,
    ln1_bias,
    qkv_weight,
    qv_bias,
    out_weight,
    out_bias,
    ln2_gain,
    ln2_bias,
    up_weight,
    up_bias,
    down_weight,
    down_bias,
    router_weight,
    mix_weight,
    expert_up,
    expert_up_bias,
    expert_down,
    expert_down_bias,
):
    rows, width = tokens.shape[0] * tokens.shape[1], tokens.shape[2]
    experts, share, hidden = expert_up.shape
    own_hidden = hidden // ctx
    own_width = width // ctx
    length = rows * ctx
    capacity = rows * 5 // 8
    me = lax.axis_index("ctx")
    shifts = range(1, ctx)

    def swap(array, shift):
        return lax.ppermute(array, "ctx", [(i, i ^ shift) for i in range(ctx)])

    def gather_ctx(array):
        return [array] + [swap(array, s) for s in shifts]

    def exchange(pieces):
        own = [lax.dynamic_index_in_dim(pieces, me ^ s, 0, keepdims=False) for s in range(ctx)]
        return [own[0]] + [swap(own[s], s) for s in shifts]

    def natural(pieces, axis=0):
        size = pieces[0].shape[axis]
        shape = list(pieces[0].shape)
        shape[axis] = size * ctx
        whole = jnp.zeros(shape, pieces[0].dtype)
        for s, piece in enumerate(pieces):
            whole = lax.dynamic_update_slice_in_dim(whole, piece, (me ^ s) * size, axis)
        return whole

    def gather_dp(array, axis=0):
        return lax.all_gather(array, "dp", axis=axis, tiled=True)

    def scatter_dp(array, axis=0):
        return lax.psum_scatter(
            array.astype(bf16), "dp", scatter_dimension=axis, tiled=True
        )

    def total(pieces):
        return functools.reduce(jnp.add, [piece.astype(f32) for piece in pieces])

    tokens = tokens.reshape(rows, width)
    cotangent = cotangent.reshape(rows, width)
    routes = routes.reshape(rows)
    first_hot = routes == 0
    first_count = jnp.sum(first_hot.astype(f32))
    smalls = [
        ln1_gain,
        ln1_bias,
        qv_bias,
        out_bias,
        ln2_gain,
        ln2_bias,
        down_bias,
        router_weight,
        mix_weight,
        expert_down_bias,
        up_bias,
        expert_up_bias,
        first_count[None].astype(bf16),
    ]
    sizes = [small.size for small in smalls]
    packed = jnp.concatenate([small.reshape(-1) for small in smalls])
    plane_small = lax.all_gather(packed, "ctx", axis=0)
    all_small = lax.all_gather(plane_small, "dp", axis=0)
    unpacked, at = [], 0
    for size in sizes:
        unpacked.append(all_small[:, :, at : at + size])
        at += size
    (gain_one, shift_one, full_qv, full_outb, gain_two, shift_two, full_downb) = [
        part.reshape(-1).astype(f32) for part in unpacked[:7]
    ]
    full_router = unpacked[7].reshape(width, -1)
    full_mix = unpacked[8].reshape(width, -1)
    full_expert_downb = (
        unpacked[9].reshape(dp, ctx, experts, -1).transpose(2, 0, 1, 3).reshape(experts, width)
    ).astype(f32)
    own_upb = lax.dynamic_index_in_dim(unpacked[10], me, 1, keepdims=False).reshape(-1).astype(f32)
    own_expert_upb = (
        lax.dynamic_index_in_dim(unpacked[11], me, 1, keepdims=False)
        .reshape(dp, experts, -1)
        .transpose(1, 0, 2)
        .reshape(experts, own_hidden)
        .astype(f32)
    )
    counts = plane_small[:, -1].astype(f32)

    token_all = natural(gather_ctx(tokens))
    qkv_cut = qkv_weight.reshape(share, 3, ctx, own_width).transpose(2, 0, 1, 3)
    own_qkv = gather_dp(natural(exchange(qkv_cut.reshape(ctx, share, 3 * own_width))))
    out_parts = gather_dp(out_weight)
    full_out = natural(
        [part.reshape(dp, share, width) for part in gather_ctx(out_parts)], 1
    ).reshape(width, width)

    unit = hidden // (dp * ctx)
    ups = jnp.concatenate([up_weight[None], expert_up], 0)
    ups_cut = ups.reshape(experts + 1, share, dp, ctx, unit).transpose(3, 0, 1, 2, 4)
    ups_cut = ups_cut.reshape(ctx, experts + 1, share, own_hidden)
    ups_rows = natural(exchange(ups_cut), 1)
    own_up = gather_dp(ups_rows[0])
    own_down = gather_dp(down_weight)
    own_expert_up = [gather_dp(ups_rows[e + 1]) for e in range(experts)]
    own_expert_down = [gather_dp(expert_down[e]) for e in range(experts)]

    normed_all, _ = layer_stats(token_all.astype(f32))
    attn_in = (normed_all * gain_one + shift_one).astype(bf16)
    own_q_bias = lax.dynamic_slice_in_dim(full_qv, me * own_width, own_width)
    own_v_bias = lax.dynamic_slice_in_dim(full_qv, width + me * own_width, own_width)
    own_bias = jnp.concatenate([own_q_bias, jnp.zeros_like(own_q_bias), own_v_bias])
    qkv = (product(attn_in, own_qkv) + own_bias).astype(bf16)
    attended_heads = attention_forward(qkv, own_width)
    attended = natural(exchange(attended_heads.reshape(ctx, rows, own_width)), 1)

    inputs = tokens.astype(f32)
    hidden_state = inputs + (product(attended, full_out) + full_outb)
    normed_two, inverse_two = layer_stats(hidden_state)
    ffn_in = (normed_two * gain_two + shift_two).astype(bf16)

    order = jnp.arange(rows).astype(f32)
    counted = jnp.cumsum(first_hot.astype(f32))
    place = jnp.where(first_hot, counted - 1.0, first_count + order - counted)
    sort_t = (place[:, None] == order[None, :]).astype(bf16)
    sort = (place[None, :] == order[:, None]).astype(bf16)
    grad_rows = jnp.concatenate(gather_ctx(product(sort, cotangent).astype(bf16)))
    ffn_rows = jnp.concatenate(gather_ctx(product(sort, ffn_in).astype(bf16)))
    row_counts = jnp.stack([counts[me ^ s] for s in range(ctx)])
    first_mask = order[None, :] < row_counts[:, None]

    def router(values):
        return (
            jax.nn.softmax(product(values, full_router), axis=-1),
            jax.nn.softmax(product(values, full_mix), axis=-1),
        )

    route_rows, mix_rows = router(ffn_rows)
    gate_rows = jnp.where(first_mask.reshape(-1), route_rows[:, 0], route_rows[:, 1])
    mix_zero = mix_rows[:, 0:1]
    branch = (mix_rows[:, 1] * gate_rows)[:, None]

    up_dense = product(ffn_rows, own_up) + own_upb
    act_dense = gelu(up_dense).astype(bf16)
    out_dense = product(act_dense, own_down)
    ffn_blocks = ffn_rows.reshape(ctx, rows, width)
    spans = (slice(0, capacity), slice(rows - capacity, rows))
    masks = (first_mask, ~first_mask)
    caches = []
    for e in range(experts):
        slot_in = ffn_blocks[:, spans[e]].reshape(ctx * capacity, width)
        slot_up = product(slot_in, own_expert_up[e]) + own_expert_upb[e]
        slot_act = gelu(slot_up).astype(bf16)
        slot_out = product(slot_act, own_expert_down[e]).reshape(ctx, capacity, width)
        caches.append((slot_in, slot_up, slot_act, slot_out))
    edge = rows - capacity
    overlap = capacity - edge
    moe = jnp.concatenate(
        [
            caches[0][3][:, :edge],
            jnp.where(
                first_mask[:, edge:capacity, None],
                caches[0][3][:, edge:],
                caches[1][3][:, :overlap],
            ),
            caches[1][3][:, overlap:],
        ],
        1,
    ).reshape(length, width)
    grad_f = grad_rows.astype(f32)
    dots = jnp.stack([jnp.sum(grad_f * out_dense, -1), jnp.sum(grad_f * moe, -1)], -1)
    mixed_out = (mix_zero * out_dense + branch * moe).astype(bf16)

    def scatter_ctx(array):
        blocks = array.reshape(ctx, rows, array.shape[-1])
        return [blocks[0]] + [swap(blocks[s], s) for s in shifts]

    sort_t_all = jnp.concatenate([sort_t] * ctx, 1)

    def back_in_order(pieces):
        return product(sort_t_all, jnp.concatenate(pieces, 0))

    grad_dense_out = (grad_f * mix_zero).astype(bf16)
    grad_moe = (grad_f * branch).astype(bf16).reshape(ctx, rows, width)
    grad_w_down = left_product(act_dense, grad_dense_out)
    grad_act = right_product(grad_dense_out, own_down)
    grad_up_dense = gelu_grad(up_dense, grad_act).astype(bf16)
    grad_w_up = left_product(ffn_rows, grad_up_dense)
    grad_b_up = jnp.sum(grad_up_dense.astype(f32), 0)
    grad_ffn_rows = right_product(grad_up_dense, own_up).reshape(ctx, rows, width)
    down_grad = scatter_dp(grad_w_down).astype(f32)
    up_part = scatter_dp(grad_w_up)
    expert_down_grads, expert_up_parts, expert_upb_grads, slot_grads = [], [], [], []
    for e in range(experts):
        slot_in, slot_up, slot_act, _ = caches[e]
        grad_slot = jnp.where(masks[e][:, spans[e], None], grad_moe[:, spans[e]], 0)
        grad_slot = grad_slot.reshape(ctx * capacity, width)
        expert_down_grads.append(scatter_dp(left_product(slot_act, grad_slot)).astype(f32))
        grad_slot_act = right_product(grad_slot, own_expert_down[e])
        grad_slot_up = gelu_grad(slot_up, grad_slot_act).astype(bf16)
        expert_up_parts.append(scatter_dp(left_product(slot_in, grad_slot_up)))
        expert_upb_grads.append(jnp.sum(grad_slot_up.astype(f32), 0))
        grad_slot_in = right_product(grad_slot_up, own_expert_up[e])
        slot_grads.append(grad_slot_in.reshape(ctx, capacity, width))
    grad_ffn_rows = jnp.concatenate(
        [
            grad_ffn_rows[:, :edge] + slot_grads[0][:, :edge],
            grad_ffn_rows[:, edge:capacity]
            + (slot_grads[0][:, edge:] + slot_grads[1][:, :overlap]),
            grad_ffn_rows[:, capacity:] + slot_grads[1][:, overlap:],
        ],
        1,
    ).reshape(length, width)
    grad_ffn = back_in_order(scatter_ctx(grad_ffn_rows.astype(bf16)))
    own_dots = jnp.dot(sort_t.astype(f32), total(scatter_ctx(dots)), precision=highest)
    mlp_out = back_in_order(scatter_ctx(mixed_out))

    route_probs, mix_coef = router(ffn_in)
    hot = jnp.stack([first_hot, ~first_hot], -1).astype(f32)
    gate_value = jnp.sum(route_probs * hot, -1)
    branch_coef = mix_coef[:, 1] * gate_value
    bias_moe = jnp.where(first_hot[:, None], full_expert_downb[0], full_expert_downb[1])
    result = (
        hidden_state
        + mlp_out
        + mix_coef[:, 0:1] * full_downb
        + branch_coef[:, None] * bias_moe
    )
    grad_out = cotangent.astype(f32)
    dense_dot = own_dots[:, 0] + jnp.sum(grad_out * full_downb, -1)
    moe_dot = own_dots[:, 1] + jnp.sum(grad_out * bias_moe, -1)
    grad_mixc = jnp.stack([dense_dot, moe_dot * gate_value], -1)
    grad_gate = moe_dot * mix_coef[:, 1]
    grad_mix_logits = mix_coef * (grad_mixc - jnp.sum(mix_coef * grad_mixc, -1, keepdims=True))
    grad_probs = hot * grad_gate[:, None]
    grad_router_logits = route_probs * (
        grad_probs - jnp.sum(route_probs * grad_probs, -1, keepdims=True)
    )
    grad_small = jnp.concatenate([grad_router_logits, grad_mix_logits], -1)
    small_weights = jnp.concatenate([full_router, full_mix], 1).astype(f32)
    grad_small_w = jnp.einsum("nd,ne->de", ffn_in.astype(f32), grad_small, precision=highest)
    grad_ffn = grad_ffn + jnp.einsum("ne,de->nd", grad_small, small_weights, precision=highest)
    own_grad_dense = (grad_out * mix_coef[:, 0:1]).astype(bf16).astype(f32)
    own_grad_moe = (grad_out * branch_coef[:, None]).astype(bf16).astype(f32)
    grad_b_down = jnp.sum(own_grad_dense, 0)
    grad_b_expert_down = jnp.stack(
        [jnp.sum(own_grad_moe * hot[:, e : e + 1], 0) for e in range(experts)]
    )
    grad_gain_two = jnp.sum(grad_ffn * normed_two, 0)
    grad_shift_two = jnp.sum(grad_ffn, 0)
    grad_hidden = grad_out + norm_back(grad_ffn, normed_two, inverse_two, gain_two)
    grad_proj = grad_hidden.astype(bf16)
    grad_b_out = jnp.sum(grad_proj.astype(f32), 0)
    grad_attended = right_product(grad_proj, full_out).astype(bf16)
    grad_cut = grad_attended.reshape(rows, ctx, own_width).transpose(1, 0, 2)
    grad_heads = natural(exchange(grad_cut))
    grad_w_out = left_product(attended, grad_proj).astype(bf16)
    grad_w_out = grad_w_out.reshape(dp, ctx, share, width).transpose(1, 0, 2, 3)
    out_part = total(exchange(grad_w_out.reshape(ctx, dp * share, width)))
    out_grad = scatter_dp(out_part).astype(f32)

    grad_qkv = jnp.concatenate(attention_backward(qkv, grad_heads, own_width), 1)
    qkv_part = scatter_dp(left_product(attn_in, grad_qkv))
    grad_b_qkv = jnp.sum(grad_qkv.astype(f32), 0)
    grad_attn_rows = right_product(grad_qkv, own_qkv).astype(bf16)
    grad_attn_in = total(exchange(grad_attn_rows.reshape(ctx, rows, width)))
    normed_one, inverse_one = layer_stats(inputs)
    grad_gain_one = jnp.sum(grad_attn_in * normed_one, 0)
    grad_shift_one = jnp.sum(grad_attn_in, 0)
    grad_inputs = grad_hidden + norm_back(grad_attn_in, normed_one, inverse_one, gain_one)

    up_parts = jnp.stack([up_part] + expert_up_parts)
    up_cut = up_parts.reshape(experts + 1, ctx, share, own_hidden).transpose(1, 0, 2, 3)
    up_grads = natural(
        [p.reshape(experts + 1, share, dp, 1, unit) for p in exchange(up_cut)], 3
    )
    up_grads = up_grads.reshape(experts + 1, share, hidden).astype(f32)
    qkv_cut = qkv_part.reshape(ctx, share, 3 * own_width)
    qkv_grad = natural([p.reshape(share, 3, own_width) for p in exchange(qkv_cut)], 2)
    qkv_grad = qkv_grad.reshape(share, 3 * width).astype(f32)

    zero_qv = jnp.zeros((2, width), f32)
    grad_qv = lax.dynamic_update_slice(
        zero_qv,
        jnp.stack([grad_b_qkv[:own_width], grad_b_qkv[2 * own_width :]]),
        (0, me * own_width),
    )

    def own_columns(array):
        whole = jnp.zeros((dp, ctx, array.shape[-1]), f32)
        return lax.dynamic_update_slice_in_dim(whole, array[:, None], me, 1)

    expert_upb = jnp.stack(expert_upb_grads).reshape(experts, dp, unit).transpose(1, 0, 2)
    small_grads = [
        grad_gain_one,
        grad_shift_one,
        grad_qv,
        grad_b_out,
        grad_gain_two,
        grad_shift_two,
        grad_b_down,
        grad_small_w[:, :experts],
        grad_small_w[:, experts:],
        grad_b_expert_down.reshape(experts, dp, ctx, share).transpose(1, 2, 0, 3),
        own_columns(grad_b_up.reshape(dp, unit)),
        own_columns(expert_upb.reshape(dp, experts * unit)),
    ]
    small_sum = jnp.concatenate([g.reshape(dp, ctx, -1) for g in small_grads], -1)
    small_sum = total(exchange(small_sum.transpose(1, 0, 2)))
    place_dp = lax.axis_index("dp")
    own = [
        lax.dynamic_index_in_dim(small_sum, place_dp ^ s, 0, keepdims=False) for s in range(dp)
    ]
    small_sum = total(
        [own[0]]
        + [lax.ppermute(own[s], "dp", [(i, i ^ s) for i in range(dp)]) for s in range(1, dp)]
    )
    outs, at = [], 0
    for size in sizes[:-1]:
        outs.append(small_sum[at : at + size])
        at += size
    return (
        result[None],
        grad_inputs[None],
        outs[0],
        outs[1],
        qkv_grad,
        outs[2],
        out_grad,
        outs[3],
        outs[4],
        outs[5],
        up_grads[0],
        outs[10],
        down_grad,
        outs[6],
        outs[7].reshape(router_weight.shape),
        outs[8].reshape(mix_weight.shape),
        up_grads[1:],
        outs[11].reshape(expert_up_bias.shape),
        jnp.stack(expert_down_grads),
        outs[9].reshape(expert_down_bias.shape),
    )


def solution(mesh):
    both = ("dp", "ctx")
    data = P("dp", "ctx", None)
    vector = P(both)
    matrix = P(both, None)
    expert_matrix = P(None, both, None)
    expert_vector = P(None, both)
    weights = (
        vector,
        vector,
        matrix,
        vector,
        matrix,
        vector,
        vector,
        vector,
        matrix,
        vector,
        matrix,
        vector,
        matrix,
        matrix,
        expert_matrix,
        expert_vector,
        expert_matrix,
        expert_vector,
    )
    return jax.shard_map(
        functools.partial(layer, mesh.shape["dp"], mesh.shape["ctx"]),
        mesh=mesh,
        in_specs=(data, data, data) + weights,
        out_specs=(data, data) + weights,
        check_vma=False,
    )
```

```python
import functools

import jax
import jax.numpy as jnp
from jax import lax
from jax.experimental import pallas as pl
from jax.experimental.pallas import tpu as pltpu
from jax.sharding import PartitionSpec as P

HEAD_DIM = 64
EPSILON = 1e-05
ROOT = 0.7978845608028654
CUBE = 0.044715
LANES = 128
f32 = jnp.float32
bf16 = jnp.bfloat16

ROUTER, MIX, GAIN_ONE, SHIFT_ONE, QV, OUT_BIAS, GAIN_TWO, SHIFT_TWO, DOWN_BIAS, EXPERT_DOWN, COUNT = (
    0,
    2,
    4,
    5,
    6,
    8,
    9,
    10,
    11,
    12,
    14,
)
UP_BIAS = 15
SMALL_ROWS = 24

anywhere = pl.BlockSpec(memory_space=pl.ANY)
inside = pl.BlockSpec(memory_space=pltpu.VMEM)
scalar = pl.BlockSpec(memory_space=pltpu.SMEM)


def product(left_op, right_op):
    return jnp.dot(left_op, right_op, preferred_element_type=f32)


def left_product(left_op, right_op):
    return lax.dot_general(left_op, right_op, (((0,), (0,)), ((), ())), preferred_element_type=f32)


def right_product(left_op, right_op):
    return lax.dot_general(left_op, right_op, (((1,), (1,)), ((), ())), preferred_element_type=f32)


def layer_stats(values):
    row_mean = jnp.mean(values, -1, keepdims=True)
    centred = values - row_mean
    inverse = lax.rsqrt(jnp.mean(centred * centred, -1, keepdims=True) + EPSILON)
    return (centred * inverse, inverse)


def norm_back(grad_norm, normed, inverse, gain):
    scaled = grad_norm * gain
    return inverse * (
        scaled
        - jnp.mean(scaled, -1, keepdims=True)
        - normed * jnp.mean(scaled * normed, -1, keepdims=True)
    )


def sigmoid_pair(low, high):
    return 1.0 / (1.0 + jnp.exp(high - low))


def three_parts(values):
    high = values.astype(bf16)
    rest = values - high.astype(f32)
    middle = rest.astype(bf16)
    return high, middle, (rest - middle.astype(f32)).astype(bf16)


def aligned(index, size):
    return pl.ds(pl.multiple_of(index * size, size), size)


def run(kernel, name, inputs, specs, outs, out_specs, scratch, grid=()):
    return pl.pallas_call(
        kernel,
        grid=grid,
        in_specs=specs,
        out_specs=out_specs,
        out_shape=[jax.ShapeDtypeStruct(shape, kind) for shape, kind in outs],
        scratch_shapes=scratch,
        compiler_params=pltpu.CompilerParams(
            dimension_semantics=("arbitrary",) * len(grid), vmem_limit_bytes=56 * 1024 * 1024
        ),
        cost_estimate=pl.CostEstimate(flops=1024, bytes_accessed=1024, transcendentals=0),
        name=name,
    )(*inputs)


def start_all(copies):
    for copy in copies:
        copy.start()
    return copies


def wait_all(copies):
    for copy in copies:
        copy.wait()


def unpack_kernel(plan, places, *refs):
    dp, ctx, share, own, experts = plan
    parts, (by_row, by_column, out_ref), (held, sems) = refs[:dp], refs[dp : dp + 3], refs[dp + 3 :]
    size = parts[0].shape[0]
    wait_all(
        start_all(
            [
                pltpu.make_async_copy(part, held.at[aligned(places[i], size)], sems.at[i])
                for i, part in enumerate(parts)
            ]
        )
    )
    small = held[:, 4 * own :]
    by_row[...] = small
    turned = jnp.transpose(small.astype(f32))
    by_column[...] = turned[:SMALL_ROWS]
    for block in range(dp):
        for piece in range(ctx):
            at = block * size + piece * share
            out_ref[block * share : (block + 1) * share, piece * own : (piece + 1) * own] = held[
                at : at + share, 3 * own : 4 * own
            ]


def unpack(places, parts, plan):
    dp, ctx, share, own, experts = plan
    size = parts[0].shape[0]
    width = dp * size
    return run(
        functools.partial(unpack_kernel, plan),
        "unpack",
        [places] + parts,
        [scalar] + [anywhere] * dp,
        [((width, LANES), bf16), ((SMALL_ROWS, width), f32), ((dp * share, ctx * own), bf16)],
        [inside] * 3,
        [pltpu.VMEM((width, 4 * own + LANES), bf16), pltpu.SemaphoreType.DMA((dp,))],
    )


def qkv_kernel(plan, scalars, small_ref, *refs):
    dp, ctx, rows, own, share = plan
    parts, tokens = refs[:dp], refs[dp : dp + ctx]
    qkv_ref, norm_ref, weight_ref, sems = refs[dp + ctx :]
    size = parts[0].shape[0]
    moves = [
        pltpu.make_async_copy(token, norm_ref.at[aligned(scalars[dp + i], rows)], sems.at[i])
        for i, token in enumerate(tokens)
    ] + [
        pltpu.make_async_copy(part, weight_ref.at[aligned(scalars[i], size)], sems.at[ctx + i])
        for i, part in enumerate(parts)
    ]
    start_all(moves)
    width = small_ref.shape[1]
    column = lax.broadcasted_iota(jnp.int32, (width, own), 1) + scalars[dp] * own
    source = lax.broadcasted_iota(jnp.int32, (width, own), 0)
    rank, inner = column // (2 * share), column % (2 * share)
    pair = small_ref[QV : QV + 2, :].astype(bf16)
    biases = []
    for part in range(2):
        picks = [
            (source == (rank + part * (width // (2 * share))) * share + inner - half * share)
            & (inner // share == half)
            for half in range(2)
        ]
        biases.append(
            sum(product(pair[half : half + 1], picks[half].astype(bf16)) for half in range(2))
        )
    bias = jnp.concatenate([biases[0], jnp.zeros_like(biases[0]), biases[1]], 1)
    gain, shift = small_ref[GAIN_ONE : GAIN_ONE + 1, :], small_ref[SHIFT_ONE : SHIFT_ONE + 1, :]
    wait_all(moves)
    tile = min(256, ctx * rows)
    for at in range(0, ctx * rows, tile):
        span = slice(at, at + tile)
        normed, _ = layer_stats(norm_ref[span, :].astype(f32))
        low = (normed * gain + shift).astype(bf16)
        norm_ref[span, :] = low
        qkv_ref[span, :] = (product(low, weight_ref[:, : 3 * own]) + bias).astype(bf16)


def make_qkv(scalars, small, parts, tokens, plan):
    dp, ctx, rows, own, share = plan
    width = tokens[0].shape[1]
    return run(
        functools.partial(qkv_kernel, plan),
        "norm_qkv",
        [scalars, small] + parts + tokens,
        [scalar, inside] + [anywhere] * (dp + ctx),
        [
            ((ctx * rows, 3 * own), bf16),
            ((ctx * rows, width), bf16),
            ((width, parts[0].shape[1]), bf16),
        ],
        [inside] * 3,
        [pltpu.SemaphoreType.DMA((dp + ctx,))],
    )


def score_parts(q_part, k_ref, column, step, block):
    scale = HEAD_DIM ** (-0.5)
    parts = []
    if step:
        parts.append(right_product(q_part, k_ref[0 : step * block, column]) * scale)
    diagonal = right_product(q_part, k_ref[step * block : (step + 1) * block, column]) * scale
    rows = lax.broadcasted_iota(jnp.int32, (block, block), 0)
    keys = lax.broadcasted_iota(jnp.int32, (block, block), 1)
    parts.append(jnp.where(keys <= rows, diagonal, -1e30))
    return parts


def softmax_of(parts):
    row_max = functools.reduce(jnp.maximum, [jnp.max(part, -1, keepdims=True) for part in parts])
    terms = [jnp.exp(part - row_max) for part in parts]
    total = functools.reduce(jnp.add, [jnp.sum(term, -1, keepdims=True) for term in terms])
    inverse = 1.0 / total
    return [term * inverse for term in terms]


def key_spans(step, block):
    spans = [slice(0, step * block)] if step else []
    return spans + [slice(step * block, (step + 1) * block)]


def attention_forward_kernel(heads, block, q_ref, k_ref, v_ref, out_ref):
    for head in range(heads):
        column = slice(head * HEAD_DIM, (head + 1) * HEAD_DIM)
        for step in range(q_ref.shape[0] // block):
            rows = slice(step * block, (step + 1) * block)
            probs = softmax_of(score_parts(q_ref[rows, column], k_ref, column, step, block))
            mixed = functools.reduce(
                jnp.add,
                [
                    product(prob.astype(bf16), v_ref[span, column])
                    for prob, span in zip(probs, key_spans(step, block))
                ],
            )
            out_ref[rows, column] = mixed.astype(bf16)


def attention_backward_kernel(
    heads, block, rows, scalars, q_ref, k_ref, v_ref, *refs
):
    scale = HEAD_DIM ** (-0.5)
    pieces, (dq_ref, dk_ref, dv_ref, held, k_acc, v_acc, sems) = refs[:-7], refs[-7:]
    step_now, lanes = pl.program_id(0), dq_ref.shape[1]

    @pl.when(step_now == 0)
    def _():
        wait_all(
            start_all(
                [
                    pltpu.make_async_copy(piece, held.at[aligned(scalars[i], rows)], sems.at[i])
                    for i, piece in enumerate(pieces)
                ]
            )
        )

    grads = held[...] if held.shape[1] == lanes else held[:, aligned(step_now, lanes)]
    for head in range(heads):
        column = slice(head * HEAD_DIM, (head + 1) * HEAD_DIM)
        for step in reversed(range(q_ref.shape[0] // block)):
            span_rows = slice(step * block, (step + 1) * block)
            spans = key_spans(step, block)
            q_part, o_part = q_ref[span_rows, column], grads[span_rows, column]
            probs = softmax_of(score_parts(q_part, k_ref, column, step, block))
            prob_grads = [right_product(o_part, v_ref[span, column]) for span in spans]
            delta = functools.reduce(
                jnp.add,
                [jnp.sum(p * g, -1, keepdims=True) for p, g in zip(probs, prob_grads)],
            )
            score_grads = [(p * (g - delta)).astype(bf16) for p, g in zip(probs, prob_grads)]
            q_grad = functools.reduce(
                jnp.add,
                [product(s, k_ref[span, column]) for s, span in zip(score_grads, spans)],
            )
            dq_ref[span_rows, column] = (q_grad * scale).astype(bf16)
            first = step == q_ref.shape[0] // block - 1
            for span, score_grad, prob in zip(spans, score_grads, probs):
                key_grad = left_product(score_grad, q_part)
                value_grad = left_product(prob.astype(bf16), o_part)
                k_acc[span, column] = key_grad if first else k_acc[span, column] + key_grad
                v_acc[span, column] = value_grad if first else v_acc[span, column] + value_grad
    dk_ref[...] = (k_acc[...] * scale).astype(bf16)
    dv_ref[...] = v_acc[...].astype(bf16)


def attention_plan(qkv, width):
    length = qkv.shape[0]
    heads = min(2, width // HEAD_DIM)
    block = min(256, length)
    lanes = heads * HEAD_DIM
    steps = width // lanes
    whole = lanes % LANES == 0
    joined = [qkv] * 3 if whole else [qkv[:, i * width : (i + 1) * width] for i in range(3)]

    def spec(part):
        first = part * steps if whole else 0
        return pl.BlockSpec((length, lanes), lambda step: (0, first + step))

    return length, heads, block, lanes, steps, spec, joined


def attention_forward(qkv, width):
    length, heads, block, lanes, steps, spec, joined = attention_plan(qkv, width)
    return run(
        functools.partial(attention_forward_kernel, heads, block),
        "attention_forward",
        joined,
        [spec(0), spec(1), spec(2)],
        [((length, width), bf16)],
        [spec(0)],
        [],
        (steps,),
    )[0]


def attention_backward(scalars, qkv, pieces, width):
    length, heads, block, lanes, steps, spec, joined = attention_plan(qkv, width)
    return run(
        functools.partial(attention_backward_kernel, heads, block, pieces[0].shape[0]),
        "attention_backward",
        [scalars] + joined + pieces,
        [scalar, spec(0), spec(1), spec(2)] + [anywhere] * len(pieces),
        [((length, width), bf16)] * 3,
        [spec(0)] * 3,
        [
            pltpu.VMEM((length, width), bf16),
            pltpu.VMEM((length, lanes), f32),
            pltpu.VMEM((length, lanes), f32),
            pltpu.SemaphoreType.DMA((len(pieces),)),
        ],
        (steps,),
    )


def hidden_kernel(ctx, scalars, small_ref, out_ref, tokens_ref, sort_ref, *refs):
    pieces, (hidden_ref, norm_ref, sorted_ref) = refs[:ctx], refs[ctx:]
    own = pieces[0].shape[1]
    hidden = tokens_ref[...].astype(f32) + (
        sum(
            product(piece[...], out_ref[aligned(scalars[i], own), :])
            for i, piece in enumerate(pieces)
        )
        + small_ref[OUT_BIAS : OUT_BIAS + 1, :]
    )
    hidden_ref[...] = hidden
    normed, _ = layer_stats(hidden)
    low = (
        normed * small_ref[GAIN_TWO : GAIN_TWO + 1, :] + small_ref[SHIFT_TWO : SHIFT_TWO + 1, :]
    ).astype(bf16)
    norm_ref[...] = low
    sorted_ref[...] = product(sort_ref[...], low).astype(bf16)


def make_hidden(scalars, small, full_out, tokens, sort, pieces):
    shape = tokens.shape
    return run(
        functools.partial(hidden_kernel, len(pieces)),
        "hidden",
        [scalars, small, full_out, tokens, sort] + pieces,
        [scalar] + [inside] * (4 + len(pieces)),
        [(shape, f32), (shape, bf16), (shape, bf16)],
        [inside] * 3,
        [],
    )


def mlp_kernel(plan, scalars, small_ref, by_column, *refs):
    dp, ctx, rows, start, count, expert, merged, last = plan
    depth = dp // 2
    refs = list(refs)

    def take(number):
        taken = refs[:number]
        del refs[:number]
        return taken

    x_parts, g_parts = take(ctx), take(ctx)
    parts = take(dp if merged else 2 * dp)
    sums = take(6) if last else []
    if last:
        y_refs, gx_refs = take(ctx), take(ctx)
    else:
        y_ref, gx_ref, dots_out = take(3)
    (gb_ref,) = take(1)
    mine, other = take(1 if merged else 2), take(1 if merged else 2)
    up, down, x_all, g_all, act_all, go_all, gu_all, up_grad, down_grad = take(9)
    held = take(6) if last else []
    in_sems, x_sems, out_sems, held_sems = take(4)
    width, hidden = up.shape
    up_rows, down_rows = width // dp, hidden // dp
    tile = min(256, hidden)
    tiles = [slice(at, at + tile) for at in range(0, hidden, tile)]
    total = ctx * count

    def loads(target, size, which):
        return [
            pltpu.make_async_copy(
                parts[i].at[which] if merged else parts[which * dp + i],
                target.at[aligned(scalars[i], size)],
                in_sems.at[which * dp + i],
            )
            for i in range(dp)
        ]

    def rows_of(block):
        return slice(block * count, (block + 1) * count)

    tokens = [
        pltpu.make_async_copy(
            part.at[start : start + count], x_all.at[rows_of(i)], x_sems.at[i]
        )
        for i, part in enumerate(x_parts)
    ]
    grads = [
        pltpu.make_async_copy(
            part.at[start : start + count], g_all.at[rows_of(i)], x_sems.at[ctx + i]
        )
        for i, part in enumerate(g_parts)
    ]
    ups, downs = loads(up, up_rows, 0), loads(down, down_rows, 1)
    start_all(tokens + ups + grads + downs)
    gathered = [
        pltpu.make_async_copy(ref, held[i], held_sems.at[i]) for i, ref in enumerate(sums)
    ]
    start_all(gathered)
    wait_all(tokens)
    logits = product(x_all[...], small_ref[...])
    route_zero, route_one = logits[:, ROUTER : ROUTER + 1], logits[:, ROUTER + 1 : ROUTER + 2]
    mix_zero, mix_one = logits[:, MIX : MIX + 1], logits[:, MIX + 1 : MIX + 2]
    if expert is None:
        mask = None
        coef = sigmoid_pair(mix_zero, mix_one)
    else:
        place = lax.broadcasted_iota(jnp.int32, (count, 1), 0) + start
        firsts = [place < scalars[dp + block] for block in range(ctx)]
        masks = [(first if expert == 0 else ~first).astype(f32) for first in firsts]
        mask = jnp.concatenate(masks, 0)
        gate = (
            sigmoid_pair(route_zero, route_one)
            if expert == 0
            else sigmoid_pair(route_one, route_zero)
        )
        coef = sigmoid_pair(mix_one, mix_zero) * gate * mask
    wait_all(grads)
    go_all[...] = (g_all[...].astype(f32) * coef).astype(bf16)
    wait_all(ups)

    def forward(cut):
        pre = product(x_all[...], up[:, cut]) + by_column[:, cut]
        square = pre * pre
        bend = jnp.tanh(ROOT * (pre + CUBE * (square * pre)))
        half = 0.5 * (1.0 + bend)
        act_all[:, cut] = (pre * half).astype(bf16)
        return half + (0.5 * ROOT) * pre * (1.0 - bend * bend) * (1.0 + (3.0 * CUBE) * square)

    for number, cut in enumerate(tiles):
        slope = forward(cut)
        if number == 0:
            wait_all(downs)
        grad_act = right_product(go_all[...], down[cut, :])
        grad_up = (grad_act * slope).astype(bf16)
        gu_all[:, cut] = grad_up
        gb_ref[:, cut] = jnp.sum(grad_up.astype(f32), 0, keepdims=True)
        down_grad[cut, :] = left_product(act_all[:, cut], go_all[...]).astype(bf16)
        up_grad[:, cut] = left_product(x_all[...], grad_up).astype(bf16)

    def stores(grad, size, which):
        targets = [
            (mine[0].at[i, which] if merged else mine[which].at[i])
            if i < depth
            else (other[0].at[i - depth, which] if merged else other[which].at[i - depth])
            for i in range(dp)
        ]
        return [
            pltpu.make_async_copy(
                grad.at[aligned(scalars[i], size)], target, out_sems.at[which * dp + i]
            )
            for i, target in enumerate(targets)
        ]

    saved = start_all(stores(up_grad, up_rows, 0) + stores(down_grad, down_rows, 1))
    wait_all(gathered)
    for block in range(ctx):
        span = rows_of(block)
        out = product(act_all[span, :], down[...])
        grad_x = right_product(gu_all[span, :], up[...])
        dot = jnp.sum(g_all[span, :].astype(f32) * out, -1, keepdims=True)
        out = out * coef[span]
        if not last:
            y_ref[span, :], gx_ref[span, :] = out, grad_x
            dots_out[span, :] = dot if mask is None else dot * mask[span]
            continue
        y_dense, gx_dense, dots_dense, y_first, gx_first, dots_first = held
        whole = slice(block * rows, (block + 1) * rows)
        sets = ((y_dense, y_first, out, y_refs), (gx_dense, gx_first, grad_x, gx_refs))
        for dense, first, own, target in sets:
            early = dense[whole, :][:start] + first[span, :][:start]
            middle = dense[whole, :][start:count] + (first[span, :][start:] + own[: count - start])
            late = dense[whole, :][count:] + own[count - start :]
            target[block][0:start, 0:width] = early.astype(bf16)
            target[block][start:count, 0:width] = middle.astype(bf16)
            target[block][count:rows, 0:width] = late.astype(bf16)
        own_dot = dot * mask[span]
        first_dot = dots_first[span, :]
        moe = jnp.concatenate(
            [
                first_dot[:start],
                first_dot[start:] + own_dot[: count - start],
                own_dot[count - start :],
            ],
            0,
        )
        lane = lax.broadcasted_iota(jnp.int32, (rows, LANES), 1)
        both = jnp.where(lane % 2 == 0, dots_dense[whole, :], moe)
        high, middle, low = three_parts(both)
        extra = jnp.where(lane < 2, high.astype(f32), jnp.where(lane < 4, middle.astype(f32), low.astype(f32)))
        gx_refs[block][:, width:] = jnp.where(lane < 6, extra, 0.0).astype(bf16)
    wait_all(saved)


def mlp(scalars, small, bias, x, g, parts, expert, merged, sums):
    ctx = len(x)
    rows, width = x[0].shape
    dp = len(parts) if merged else len(parts) // 2
    depth = dp // 2
    hidden = bias.shape[1]
    count = rows if expert is None else rows * 5 // 8
    start = 0 if expert in (None, 0) else rows - count
    total = ctx * count
    last = expert == 1
    if merged:
        halves = [((depth,) + parts[0].shape, bf16)]
    else:
        halves = [((depth,) + parts[0].shape, bf16), ((depth,) + parts[dp].shape, bf16)]
    if last:
        outs = [((rows, width), bf16)] * ctx + [((rows, width + LANES), bf16)] * ctx
    else:
        outs = [((total, width), f32), ((total, width), f32), ((total, 1), f32)]
    outs = outs + [((1, hidden), f32)] + halves + halves
    small_outs = len(outs) - 2 * len(halves)
    held = [pltpu.VMEM(ref.shape, f32) for ref in sums]
    return run(
        functools.partial(mlp_kernel, (dp, ctx, rows, start, count, expert, merged, last)),
        "mlp",
        [scalars, small, bias] + x + g + parts + sums,
        [scalar, inside, inside] + [anywhere] * (2 * ctx + len(parts) + len(sums)),
        outs,
        [inside] * small_outs + [anywhere] * (2 * len(halves)),
        [
            pltpu.VMEM((width, hidden), bf16),
            pltpu.VMEM((hidden, width), bf16),
            pltpu.VMEM((total, width), bf16),
            pltpu.VMEM((total, width), bf16),
            pltpu.VMEM((total, hidden), bf16),
            pltpu.VMEM((total, width), bf16),
            pltpu.VMEM((total, hidden), bf16),
            pltpu.VMEM((width, hidden), bf16),
            pltpu.VMEM((hidden, width), bf16),
        ]
        + held
        + [
            pltpu.SemaphoreType.DMA((2 * dp,)),
            pltpu.SemaphoreType.DMA((2 * ctx,)),
            pltpu.SemaphoreType.DMA((2 * dp,)),
            pltpu.SemaphoreType.DMA((max(1, len(sums)),)),
        ],
    )


def middle_kernel(
    ctx, scalars, by_row, by_column, out_ref, hidden_ref, norm_ref, g_ref, first_ref, unsort_ref, *refs
):
    gx, pieces = refs[:ctx], refs[ctx : 2 * ctx]
    outs = refs[2 * ctx :]
    base_ref, grad_hidden_ref, out_grad_ref, rows_ref, router_ref = outs[:5]
    grad_pieces = outs[5:]
    rows, width = hidden_ref.shape
    own = pieces[0].shape[1]
    unsort = unsort_ref[...]
    gathered = sum(product(unsort, piece[...]) for piece in gx)
    grad_norm = gathered[:, :width]
    extra = gathered[:, width:]
    dense_dot = extra[:, 0:1] + (extra[:, 2:3] + extra[:, 4:5])
    moe_dot = extra[:, 1:2] + (extra[:, 3:4] + extra[:, 5:6])
    grad_out = g_ref[...].astype(f32)
    first = first_ref[...]
    down_bias = by_column[DOWN_BIAS : DOWN_BIAS + 1, :]
    moe_bias = jnp.where(
        first > 0.5,
        by_column[EXPERT_DOWN : EXPERT_DOWN + 1, :],
        by_column[EXPERT_DOWN + 1 : EXPERT_DOWN + 2, :],
    )
    dense_dot = dense_dot + jnp.sum(grad_out * down_bias, -1, keepdims=True)
    moe_dot = moe_dot + jnp.sum(grad_out * moe_bias, -1, keepdims=True)
    norm = norm_ref[...]
    logits = product(norm, by_row[...])
    route = [
        sigmoid_pair(logits[:, a : a + 1], logits[:, b : b + 1])
        for a, b in ((ROUTER, ROUTER + 1), (ROUTER + 1, ROUTER))
    ]
    mix = [
        sigmoid_pair(logits[:, a : a + 1], logits[:, b : b + 1])
        for a, b in ((MIX, MIX + 1), (MIX + 1, MIX))
    ]
    hot = [first, 1.0 - first]
    gate = route[0] * hot[0] + route[1] * hot[1]
    branch = mix[1] * gate
    hidden = hidden_ref[...]
    base_ref[...] = hidden + (mix[0] * down_bias + branch * moe_bias)
    grad_mix = [dense_dot, moe_dot * gate]
    mean_mix = mix[0] * grad_mix[0] + mix[1] * grad_mix[1]
    grad_gate = moe_dot * mix[1]
    grad_route = [hot[0] * grad_gate, hot[1] * grad_gate]
    mean_route = route[0] * grad_route[0] + route[1] * grad_route[1]
    lane = lax.broadcasted_iota(jnp.int32, (rows, LANES), 1)
    columns = [route[i] * (grad_route[i] - mean_route) for i in range(2)]
    columns += [mix[i] * (grad_mix[i] - mean_mix) for i in range(2)]
    logit_grads = jnp.zeros((rows, LANES), f32)
    for i, column in enumerate(columns):
        logit_grads = jnp.where(lane == i, column, logit_grads)
    split = three_parts(logit_grads)
    weights = by_row[...]
    for part in split:
        grad_norm = grad_norm + right_product(part, weights)
    router_ref[...] = sum(left_product(norm, part) for part in split)
    grad_dense = (grad_out * mix[0]).astype(bf16).astype(f32)
    grad_moe = (grad_out * branch).astype(bf16).astype(f32)
    normed, inverse = layer_stats(hidden)
    gain = by_column[GAIN_TWO : GAIN_TWO + 1, :]
    grad_hidden = grad_out + norm_back(grad_norm, normed, inverse, gain)
    grad_hidden_ref[...] = grad_hidden
    low = grad_hidden.astype(bf16)

    def total(values):
        return jnp.sum(values, 0, keepdims=True)

    sums = [
        total(low.astype(f32)),
        total(grad_norm * normed),
        total(grad_norm),
        total(grad_dense),
        total(grad_moe * hot[0]),
        total(grad_moe * hot[1]),
        jnp.zeros((2, width), f32),
    ]
    rows_ref[...] = jnp.concatenate(sums, 0)
    for i, (piece, target) in enumerate(zip(pieces, grad_pieces)):
        span = aligned(scalars[i], own)
        target[...] = right_product(low, out_ref[span, :]).astype(bf16)
        out_grad_ref[span, :] = left_product(piece[...], low).astype(bf16)


def make_middle(scalars, by_row, by_column, full_out, hidden, norm, g, first, unsort, gx, pieces):
    ctx = len(gx)
    rows, width = hidden.shape
    own = pieces[0].shape[1]
    return run(
        functools.partial(middle_kernel, ctx),
        "middle",
        [scalars, by_row, by_column, full_out, hidden, norm, g, first, unsort] + gx + pieces,
        [scalar] + [inside] * (8 + 2 * ctx),
        [
            ((rows, width), f32),
            ((rows, width), f32),
            ((width, width), bf16),
            ((8, width), f32),
            ((width, LANES), f32),
        ]
        + [((rows, own), bf16)] * ctx,
        [inside] * (5 + ctx),
        [],
    )


def qkv_back_kernel(plan, scalars, norm_ref, dq_ref, dk_ref, dv_ref, weight_ref, *refs):
    dp, ctx, rows, own = plan
    depth = dp // 2
    gn_refs, (mine, other, bias_ref, grad, weight_grad, gn, sems, gn_sems) = refs[:ctx], refs[ctx:]
    width = norm_ref.shape[1]
    size = width // dp
    for part, ref in enumerate((dq_ref, dk_ref, dv_ref)):
        grad[:, part * own : (part + 1) * own] = ref[...]
    tile = min(256, ctx * rows)
    weight = weight_ref[:, : 3 * own]
    for at in range(0, ctx * rows, tile):
        gn[at : at + tile, :] = right_product(grad[at : at + tile, :], weight).astype(bf16)
    sent = start_all(
        [
            pltpu.make_async_copy(gn.at[aligned(scalars[dp + i], rows)], ref, gn_sems.at[i])
            for i, ref in enumerate(gn_refs)
        ]
    )
    step = min(256, width)
    for at in range(0, width, step):
        weight_grad[at : at + step, :] = left_product(norm_ref[:, at : at + step], grad[...]).astype(
            bf16
        )
    saved = start_all(
        [
            pltpu.make_async_copy(
                weight_grad.at[aligned(scalars[i], size)],
                mine.at[i] if i < depth else other.at[i - depth],
                sems.at[i],
            )
            for i in range(dp)
        ]
    )
    bias_ref[...] = jnp.sum(grad[...].astype(f32), 0, keepdims=True)
    wait_all(sent + saved)


def qkv_back(scalars, norm, grads, weight, plan):
    dp, ctx, rows, own = plan
    length, width = norm.shape
    half = ((dp // 2, width // dp, 3 * own), bf16)
    return run(
        functools.partial(qkv_back_kernel, plan),
        "qkv_back",
        [scalars, norm] + list(grads) + [weight],
        [scalar] + [inside] * 5,
        [((rows, width), bf16)] * ctx + [half, half, ((1, 3 * own), f32)],
        [anywhere] * (ctx + 2) + [inside],
        [
            pltpu.VMEM((length, 3 * own), bf16),
            pltpu.VMEM((width, 3 * own), bf16),
            pltpu.VMEM((length, width), bf16),
            pltpu.SemaphoreType.DMA((dp,)),
            pltpu.SemaphoreType.DMA((ctx,)),
        ],
    )


def final_kernel(ctx, by_column, tokens_ref, grad_hidden_ref, *refs):
    pieces, (grad_ref, rows_ref) = refs[:ctx], refs[ctx:]
    grad_norm = sum(piece[...].astype(f32) for piece in pieces)
    normed, inverse = layer_stats(tokens_ref[...].astype(f32))
    gain = by_column[GAIN_ONE : GAIN_ONE + 1, :]
    grad_ref[...] = grad_hidden_ref[...] + norm_back(grad_norm, normed, inverse, gain)
    rows_ref[0:1, :] = jnp.sum(grad_norm * normed, 0, keepdims=True)
    rows_ref[1:2, :] = jnp.sum(grad_norm, 0, keepdims=True)


def make_final(by_column, tokens, grad_hidden, pieces):
    return run(
        functools.partial(final_kernel, len(pieces)),
        "final",
        [by_column, tokens, grad_hidden] + pieces,
        [inside] * (3 + len(pieces)),
        [(tokens.shape, f32), ((2, tokens.shape[1]), f32)],
        [inside] * 2,
        [],
    )


def result_kernel(ctx, base_ref, unsort_ref, *refs):
    pieces, (out_ref,) = refs[:ctx], refs[ctx:]
    unsort = unsort_ref[...]
    out_ref[...] = base_ref[...] + sum(product(unsort, piece[...]) for piece in pieces)


def make_result(base, unsort, pieces):
    return run(
        functools.partial(result_kernel, len(pieces)),
        "result",
        [base, unsort] + pieces,
        [inside] * (2 + len(pieces)),
        [(base.shape, f32)],
        [inside],
        [],
    )[0]


def layer(
    dp,
    ctx,
    tokens,
    cotangent,
    routes,
    ln1_gain,
    ln1_bias,
    qkv_weight,
    qv_bias,
    out_weight,
    out_bias,
    ln2_gain,
    ln2_bias,
    up_weight,
    up_bias,
    down_weight,
    down_bias,
    router_weight,
    mix_weight,
    expert_up,
    expert_up_bias,
    expert_down,
    expert_down_bias,
):
    rows, width = tokens.shape[0] * tokens.shape[1], tokens.shape[2]
    experts, share, hidden = expert_up.shape
    own_hidden = hidden // ctx
    own_width = width // ctx
    unit = hidden // (dp * ctx)
    me = lax.axis_index("ctx")
    place_dp = lax.axis_index("dp")
    core = place_dp % 2
    depth = dp // 2
    shifts = range(1, ctx)
    ring_pairs = [(i, (i + 2) % dp) for i in range(dp)]
    core_pairs = [(i, i ^ 1) for i in range(dp)]
    places = jnp.stack(
        [
            ((place_dp // 2 + depth - t) % depth) * 2 + c
            for c in (core, 1 - core)
            for t in range(depth)
        ]
    ).astype(jnp.int32)
    peers = jnp.stack([me ^ s for s in range(ctx)]).astype(jnp.int32)

    def swap(array, shift):
        return lax.ppermute(array, "ctx", [(i, i ^ shift) for i in range(ctx)])

    def gather_ctx(array):
        return [array] + [swap(array, s) for s in shifts]

    def trade(pieces):
        return [pieces[0]] + [swap(pieces[s], s) for s in shifts]

    def exchange(pieces):
        return trade(
            [lax.dynamic_index_in_dim(pieces, me ^ s, 0, keepdims=False) for s in range(ctx)]
        )

    def natural(pieces):
        whole = jnp.zeros((ctx,) + pieces[0].shape, pieces[0].dtype)
        for s, piece in enumerate(pieces):
            whole = lax.dynamic_update_slice_in_dim(whole, piece[None], me ^ s, 0)
        return whole

    def ring(array):
        return lax.ppermute(array, "dp", ring_pairs)

    def swap_core(array):
        return lax.ppermute(array, "dp", core_pairs)

    def chunks(array):
        size = array.shape[0] // dp
        cut = [
            lax.dynamic_slice_in_dim(array, places[i] * size, size, 0) for i in range(dp)
        ]
        return jnp.stack(cut[:depth]), jnp.stack(cut[depth:])

    def after(array, *others):
        return lax.optimization_barrier((array,) + others)[0]

    tokens = tokens.reshape(rows, width)
    cotangent = cotangent.reshape(rows, width)
    first_hot = routes.reshape(rows) == 0
    first_float = first_hot.astype(f32)
    first_count = jnp.sum(first_float)

    def column(vector):
        return vector.reshape(-1, share).T

    def bias_column(vector):
        return jnp.pad(vector.reshape(unit, 1), ((0, ctx * share - unit), (0, 0)))

    small = jnp.concatenate(
        [
            router_weight,
            mix_weight,
            column(ln1_gain),
            column(ln1_bias),
            column(qv_bias),
            column(out_bias),
            column(ln2_gain),
            column(ln2_bias),
            column(down_bias),
            expert_down_bias.T,
            jnp.broadcast_to(first_count.astype(bf16), (share, 1)),
        ],
        1,
    )
    small = jnp.pad(small, ((0, 0), (0, LANES - small.shape[1])))
    qkv_cut = qkv_weight.reshape(share, 3, ctx, own_width).transpose(2, 0, 1, 3)
    first_cut = jnp.concatenate(
        [
            qkv_cut.reshape(ctx, share, 3 * own_width),
            jnp.broadcast_to(small[None], (ctx, share, LANES)),
        ],
        -1,
    )
    first_rows = natural(exchange(first_cut)).reshape(ctx * share, 3 * own_width + LANES)
    qkv_rows = first_rows[:, : 3 * own_width]
    small_rows = first_rows[:, 3 * own_width :]
    counts = small_rows[::share, COUNT]
    bias_lanes = jnp.concatenate(
        [bias_column(up_bias)] + [bias_column(expert_up_bias[e]) for e in range(experts)], 1
    )
    lane = jnp.arange(LANES)[None, :]
    bias_lanes = jnp.pad(bias_lanes, ((0, 0), (UP_BIAS, LANES - UP_BIAS - bias_lanes.shape[1])))
    small_rows = jnp.where((lane >= UP_BIAS) & (lane < UP_BIAS + experts + 1), bias_lanes, small_rows)
    out_rows = out_weight.reshape(share, ctx, own_width).transpose(1, 0, 2)
    out_rows = out_rows.reshape(ctx * share, own_width)
    first_group = jnp.concatenate([qkv_rows, out_rows, small_rows], 1)

    def gather_dp(streams):
        parts = [[array] for array in streams]
        for _ in range(1, depth):
            for part in parts:
                part.append(ring(part[-1]))
        return parts

    def with_cores(parts):
        return parts + [swap_core(part) for part in parts]

    (first_ring,) = gather_dp([first_group])
    token_parts = gather_ctx(tokens)
    first_parts = with_cores(first_ring)
    plan = (dp, ctx, share, own_width, experts)
    by_row, by_column, out_own = unpack(places, first_parts, plan)
    out_pieces = natural(gather_ctx(out_own))
    full_out = out_pieces.reshape(ctx, dp, share, width).transpose(1, 0, 2, 3).reshape(width, width)

    unit_rows = ctx * share
    ups = jnp.concatenate([up_weight[None], expert_up], 0)
    ups_cut = ups.reshape(experts + 1, share, dp, ctx, unit).transpose(3, 0, 1, 2, 4)
    ups_cut = after(ups_cut.reshape(ctx, experts + 1, share, own_hidden), first_rows)
    ups_rows = natural(exchange(ups_cut)).transpose(1, 0, 2, 3)
    ups_rows = ups_rows.reshape(experts + 1, unit_rows, own_hidden)
    downs = [down_weight] + [expert_down[e] for e in range(experts)]
    merged = downs[0].shape == ups_rows.shape[1:]
    streams = []
    for which in range(experts + 1):
        pair = [ups_rows[which], downs[which]]
        streams += [jnp.stack(pair)] if merged else pair
    streams = list(lax.optimization_barrier(tuple(streams) + (first_ring[-1],)))[:-1]
    rings = [[stream, ring(stream)] for stream in streams]

    order = jnp.arange(rows).astype(f32)
    counted = jnp.cumsum(first_float)
    place = jnp.where(first_hot, counted - 1.0, first_count + order - counted)
    unsort = (place[:, None] == order[None, :]).astype(bf16)
    sort = (place[None, :] == order[:, None]).astype(bf16)
    sorted_grad = product(sort, cotangent).astype(bf16)

    scalars = jnp.concatenate([places, peers])
    qkv, attn_in, own_qkv = make_qkv(
        scalars, by_column, first_parts, token_parts, (dp, ctx, rows, own_width, share)
    )
    attended_heads = attention_forward(qkv, own_width)
    attended = exchange(attended_heads.reshape(ctx, rows, own_width))
    hidden_state, ffn_in, sorted_in = make_hidden(peers, by_column, full_out, tokens, sort, attended)
    ffn_parts = gather_ctx(sorted_in)
    grad_parts = gather_ctx(after(sorted_grad, attended[-1]))

    for _ in range(2, depth):
        stepped = lax.optimization_barrier(tuple(parts[-1] for parts in rings) + (sorted_in,))
        for parts, part in zip(rings, stepped):
            parts.append(ring(part))
    if merged:
        weight_parts = [with_cores(parts) for parts in rings]
    else:
        weight_parts = [
            with_cores(rings[2 * w]) + with_cores(rings[2 * w + 1]) for w in range(experts + 1)
        ]

    row_counts = jnp.stack([counts[me ^ s] for s in range(ctx)]).astype(jnp.int32)
    mlp_scalars = jnp.concatenate([places, row_counts])
    up_biases = by_column[UP_BIAS : UP_BIAS + experts + 1]
    up_biases = up_biases.reshape(experts + 1, dp, -1)[:, :, :unit].reshape(experts + 1, own_hidden)

    class Scatter:
        def __init__(self, mine, other):
            self.mine, self.got, self.step, self.sent = mine, swap_core(other), 0, None

        def move(self, *others):
            if self.step == 0:
                self.got = after(self.got, *others)
            carried = None if self.step == 0 else after(ring(self.sent), *others)
            self.step += 1
            part = self.mine[self.step % depth].astype(f32) + self.got[self.step % depth].astype(f32)
            if carried is not None:
                part = part + carried.astype(f32)
            self.sent = part.astype(bf16) if self.step < depth else part
            return self.sent

        def finish(self, *others):
            while self.step < depth:
                self.move(*others)
            return self.sent

    class Joint:
        def __init__(self, halves):
            half = len(halves) // 2
            self.parts = [Scatter(m, o) for m, o in zip(halves[:half], halves[half:])]

        def move(self, *others):
            return [part.move(*others) for part in self.parts]

        def finish(self, *others):
            done = [part.finish(*others) for part in self.parts]
            return done if len(done) == 2 else [done[0][0], done[0][1]]

    def run_mlp(which, held, sums):
        return mlp(
            held,
            by_row,
            up_biases[which][None],
            ffn_parts,
            grad_parts,
            weight_parts[which],
            which - 1 if which else None,
            merged,
            list(sums),
        )

    dense = run_mlp(0, mlp_scalars, [])
    sum_dense = Joint(dense[4:])
    first = run_mlp(1, after(mlp_scalars, dense[3]), [])
    sum_first = Joint(first[4:])
    sent = sum_dense.move(first[3])
    second = run_mlp(2, after(mlp_scalars, first[3], *sent), dense[:3] + first[:3])
    gb_second = second[2 * ctx]
    grad_pieces = trade(second[ctx : 2 * ctx])
    sum_second = Joint(second[2 * ctx + 1 :])
    sent = sum_first.move(gb_second)
    sent = sum_dense.move(*sent) + sum_second.move(*sent)

    base, grad_hidden, out_grad, middle_rows, router_grad, *att_grads = make_middle(
        after(peers, *sent),
        by_row,
        by_column,
        full_out,
        hidden_state,
        ffn_in,
        cotangent,
        first_float[:, None],
        unsort,
        grad_pieces,
        attended,
    )
    att_grads = trade(att_grads)
    result_pieces = trade([after(piece, att_grads[-1]) for piece in second[:ctx]])
    sent = sum_first.move(middle_rows) + sum_dense.move(middle_rows)

    grad_heads = attention_backward(after(peers, *sent), qkv, att_grads, own_width)
    sent = sum_second.move(grad_heads[0])
    *norm_grads, qkv_mine, qkv_other, grad_b_qkv = qkv_back(
        after(scalars, *sent), attn_in, grad_heads, own_qkv, (dp, ctx, rows, own_width)
    )
    norm_pieces = trade(norm_grads)
    sum_qkv = Scatter(qkv_mine, qkv_other)
    sent = sum_first.move(grad_b_qkv)
    sent = sent + [sum_qkv.move(*sent)]
    dense_sums = sum_dense.finish(*sent)
    grad_inputs, final_rows = make_final(
        after(by_column, *dense_sums, *sent), tokens, grad_hidden, norm_pieces
    )
    sent = sum_second.move(final_rows)
    result = make_result(base, unsort, result_pieces)
    out_grad = out_grad.reshape(dp, ctx, share, width).transpose(1, 0, 2, 3)
    out_grad = after(out_grad.reshape(ctx, dp * share, width), norm_pieces[-1])
    out_part = sum(p.astype(f32) for p in exchange(out_grad))
    out_grad = Scatter(*chunks(out_part.astype(bf16))).finish()
    qkv_part = sum_qkv.finish()
    first_sums, second_sums = sum_first.finish(), sum_second.finish()
    up_sums = [dense_sums[0], first_sums[0], second_sums[0]]
    down_sums = [dense_sums[1], first_sums[1], second_sums[1]]
    upb_grads = [dense[3][0], first[3][0], gb_second[0]]

    def to_owners(part, groups):
        size = part.shape[1] // groups
        pieces = exchange(part.astype(bf16).reshape(ctx, share, part.shape[1]))
        whole = natural(pieces).reshape(ctx, share, groups, size).transpose(1, 2, 0, 3)
        return whole.reshape(share, ctx * part.shape[1]).astype(f32)

    up_grads = [to_owners(part, dp) for part in up_sums]
    qkv_grad = to_owners(qkv_part, 3)

    zero_qv = jnp.zeros((2, width), f32)
    grad_qv = lax.dynamic_update_slice(
        zero_qv,
        jnp.concatenate([grad_b_qkv[:, :own_width], grad_b_qkv[:, 2 * own_width :]], 0),
        (0, me * own_width),
    )

    def own_columns(array):
        whole = jnp.zeros((dp, ctx, array.shape[-1]), f32)
        return lax.dynamic_update_slice_in_dim(whole, array[:, None], me, 1)

    expert_upb = jnp.stack(upb_grads[1:]).reshape(experts, dp, unit).transpose(1, 0, 2)
    small_grads = [
        final_rows[0],
        final_rows[1],
        grad_qv,
        middle_rows[0],
        middle_rows[1],
        middle_rows[2],
        middle_rows[3],
        router_grad[:, :experts],
        router_grad[:, experts : 2 * experts],
        middle_rows[4 : 4 + experts].reshape(experts, dp, ctx, share).transpose(1, 2, 0, 3),
        own_columns(upb_grads[0].reshape(dp, unit)),
        own_columns(expert_upb.reshape(dp, experts * unit)),
    ]
    sizes = [grad.size // (dp * ctx) for grad in small_grads]
    small_sum = jnp.concatenate([g.reshape(dp, ctx, -1) for g in small_grads], -1)
    small_sum = sum(exchange(small_sum.transpose(1, 0, 2)))
    small_sum = small_sum.reshape(dp, 1, -1)[places]
    small_sum = small_sum[:depth] + swap_core(small_sum[depth:])
    pairs = [[(i, (i + dp - 2 * t) % dp) for i in range(dp)] for t in range(depth)]
    small_sum = sum(
        [small_sum[0]] + [lax.ppermute(small_sum[t], "dp", pairs[t]) for t in range(1, depth)]
    )[0]
    outs, at = [], 0
    for size in sizes:
        outs.append(small_sum[at : at + size])
        at += size
    return (
        result[None],
        grad_inputs[None],
        outs[0],
        outs[1],
        qkv_grad,
        outs[2],
        out_grad,
        outs[3],
        outs[4],
        outs[5],
        up_grads[0],
        outs[10],
        down_sums[0],
        outs[6],
        outs[7].reshape(router_weight.shape),
        outs[8].reshape(mix_weight.shape),
        jnp.stack(up_grads[1:]),
        outs[11].reshape(expert_up_bias.shape),
        jnp.stack(down_sums[1:]),
        outs[9].reshape(expert_down_bias.shape),
    )


def solution(mesh):
    both = ("dp", "ctx")
    data = P("dp", "ctx", None)
    vector = P(both)
    matrix = P(both, None)
    expert_matrix = P(None, both, None)
    expert_vector = P(None, both)
    weights = (
        vector,
        vector,
        matrix,
        vector,
        matrix,
        vector,
        vector,
        vector,
        matrix,
        vector,
        matrix,
        vector,
        matrix,
        matrix,
        expert_matrix,
        expert_vector,
        expert_matrix,
        expert_vector,
    )
    return jax.shard_map(
        functools.partial(layer, mesh.shape["dp"], mesh.shape["ctx"]),
        mesh=mesh,
        in_specs=(data, data, data) + weights,
        out_specs=(data, data) + weights,
        check_vma=False,
    )
```

```python
import functools

import jax
import jax.numpy as jnp
from jax import lax
from jax.experimental import pallas as pl
from jax.experimental.pallas import tpu as pltpu
from jax.sharding import PartitionSpec as P

HEAD_DIM = 64
EPSILON = 1e-05
ROOT = 0.7978845608028654
CUBE = 0.044715
LANES = 128
f32 = jnp.float32
bf16 = jnp.bfloat16

ROUTER, MIX, GAIN_ONE, SHIFT_ONE, QV, OUT_BIAS, GAIN_TWO, SHIFT_TWO, DOWN_BIAS, EXPERT_DOWN, COUNT = (
    0,
    2,
    4,
    5,
    6,
    8,
    9,
    10,
    11,
    12,
    14,
)
UP_BIAS = 15
SMALL_ROWS = 24

anywhere = pl.BlockSpec(memory_space=pl.ANY)
inside = pl.BlockSpec(memory_space=pltpu.VMEM)
scalar = pl.BlockSpec(memory_space=pltpu.SMEM)


def product(left_op, right_op):
    return jnp.dot(left_op, right_op, preferred_element_type=f32)


def left_product(left_op, right_op):
    return lax.dot_general(left_op, right_op, (((0,), (0,)), ((), ())), preferred_element_type=f32)


def right_product(left_op, right_op):
    return lax.dot_general(left_op, right_op, (((1,), (1,)), ((), ())), preferred_element_type=f32)


def layer_stats(values):
    row_mean = jnp.mean(values, -1, keepdims=True)
    centred = values - row_mean
    inverse = lax.rsqrt(jnp.mean(centred * centred, -1, keepdims=True) + EPSILON)
    return (centred * inverse, inverse)


def norm_back(grad_norm, normed, inverse, gain):
    scaled = grad_norm * gain
    return inverse * (
        scaled
        - jnp.mean(scaled, -1, keepdims=True)
        - normed * jnp.mean(scaled * normed, -1, keepdims=True)
    )


def sigmoid_pair(low, high):
    return 1.0 / (1.0 + jnp.exp(high - low))


def three_parts(values):
    high = values.astype(bf16)
    rest = values - high.astype(f32)
    middle = rest.astype(bf16)
    return high, middle, (rest - middle.astype(f32)).astype(bf16)


def aligned(index, size):
    return pl.ds(pl.multiple_of(index * size, size), size)


def run(kernel, name, micros, inputs, specs, outs, out_specs, scratch, grid=()):
    return pl.pallas_call(
        kernel,
        grid=grid,
        in_specs=specs,
        out_specs=out_specs,
        out_shape=[jax.ShapeDtypeStruct(shape, kind) for shape, kind in outs],
        scratch_shapes=scratch,
        compiler_params=pltpu.CompilerParams(
            dimension_semantics=("arbitrary",) * len(grid), vmem_limit_bytes=56 * 1024 * 1024
        ),
        cost_estimate=pl.CostEstimate(
            flops=int(micros * 10**9), bytes_accessed=1024, transcendentals=0
        ),
        name=name,
    )(*inputs)


def gate_kernel(*refs):
    in_ref, out_ref = refs[0], refs[-1]
    for i in range(in_ref.shape[0]):
        out_ref[i] = in_ref[i]


def gate(scalars, *others):
    return pl.pallas_call(
        gate_kernel,
        in_specs=[scalar] + [anywhere] * len(others),
        out_specs=scalar,
        out_shape=jax.ShapeDtypeStruct(scalars.shape, scalars.dtype),
        cost_estimate=pl.CostEstimate(flops=3 * 10**10, bytes_accessed=1024, transcendentals=0),
        name="gate",
    )(scalars, *others)


def start_all(copies):
    for copy in copies:
        copy.start()
    return copies


def wait_all(copies):
    for copy in copies:
        copy.wait()


def unpack_kernel(plan, places, *refs):
    dp, ctx, share, own, experts = plan
    parts, (by_row, by_column, out_ref), (held, sems) = refs[:dp], refs[dp : dp + 3], refs[dp + 3 :]
    size = parts[0].shape[0]
    wait_all(
        start_all(
            [
                pltpu.make_async_copy(part, held.at[aligned(places[i], size)], sems.at[i])
                for i, part in enumerate(parts)
            ]
        )
    )
    small = held[:, 4 * own :]
    by_row[...] = small
    turned = jnp.transpose(small.astype(f32))
    by_column[...] = turned[:SMALL_ROWS]
    for block in range(dp):
        for piece in range(ctx):
            at = block * size + piece * share
            out_ref[block * share : (block + 1) * share, piece * own : (piece + 1) * own] = held[
                at : at + share, 3 * own : 4 * own
            ]


def unpack(places, parts, plan):
    dp, ctx, share, own, experts = plan
    size = parts[0].shape[0]
    width = dp * size
    return run(
        functools.partial(unpack_kernel, plan),
        "unpack",
        3,
        [places] + parts,
        [scalar] + [anywhere] * dp,
        [((width, LANES), bf16), ((SMALL_ROWS, width), f32), ((dp * share, ctx * own), bf16)],
        [inside] * 3,
        [pltpu.VMEM((width, 4 * own + LANES), bf16), pltpu.SemaphoreType.DMA((dp,))],
    )


def qkv_kernel(plan, scalars, small_ref, *refs):
    dp, ctx, rows, own, share = plan
    parts, tokens = refs[:dp], refs[dp : dp + ctx]
    qkv_ref, norm_ref, weight_ref, sems = refs[dp + ctx :]
    size = parts[0].shape[0]
    moves = [
        pltpu.make_async_copy(token, norm_ref.at[aligned(scalars[dp + i], rows)], sems.at[i])
        for i, token in enumerate(tokens)
    ] + [
        pltpu.make_async_copy(part, weight_ref.at[aligned(scalars[i], size)], sems.at[ctx + i])
        for i, part in enumerate(parts)
    ]
    start_all(moves)
    width = small_ref.shape[1]
    column = lax.broadcasted_iota(jnp.int32, (width, own), 1) + scalars[dp] * own
    source = lax.broadcasted_iota(jnp.int32, (width, own), 0)
    rank, inner = column // (2 * share), column % (2 * share)
    pair = small_ref[QV : QV + 2, :].astype(bf16)
    biases = []
    for part in range(2):
        picks = [
            (source == (rank + part * (width // (2 * share))) * share + inner - half * share)
            & (inner // share == half)
            for half in range(2)
        ]
        biases.append(
            sum(product(pair[half : half + 1], picks[half].astype(bf16)) for half in range(2))
        )
    bias = jnp.concatenate([biases[0], jnp.zeros_like(biases[0]), biases[1]], 1)
    gain, shift = small_ref[GAIN_ONE : GAIN_ONE + 1, :], small_ref[SHIFT_ONE : SHIFT_ONE + 1, :]
    wait_all(moves)
    tile = min(256, ctx * rows)
    for at in range(0, ctx * rows, tile):
        span = slice(at, at + tile)
        normed, _ = layer_stats(norm_ref[span, :].astype(f32))
        low = (normed * gain + shift).astype(bf16)
        norm_ref[span, :] = low
        qkv_ref[span, :] = (product(low, weight_ref[:, : 3 * own]) + bias).astype(bf16)


def make_qkv(scalars, small, parts, tokens, plan):
    dp, ctx, rows, own, share = plan
    width = tokens[0].shape[1]
    return run(
        functools.partial(qkv_kernel, plan),
        "norm_qkv",
        8,
        [scalars, small] + parts + tokens,
        [scalar, inside] + [anywhere] * (dp + ctx),
        [
            ((ctx * rows, 3 * own), bf16),
            ((ctx * rows, width), bf16),
            ((width, parts[0].shape[1]), bf16),
        ],
        [inside] * 3,
        [pltpu.SemaphoreType.DMA((dp + ctx,))],
    )


def score_parts(q_part, k_ref, column, step, block):
    scale = HEAD_DIM ** (-0.5)
    parts = []
    if step:
        parts.append(right_product(q_part, k_ref[0 : step * block, column]) * scale)
    diagonal = right_product(q_part, k_ref[step * block : (step + 1) * block, column]) * scale
    rows = lax.broadcasted_iota(jnp.int32, (block, block), 0)
    keys = lax.broadcasted_iota(jnp.int32, (block, block), 1)
    parts.append(jnp.where(keys <= rows, diagonal, -1e30))
    return parts


def softmax_of(parts):
    row_max = functools.reduce(jnp.maximum, [jnp.max(part, -1, keepdims=True) for part in parts])
    terms = [jnp.exp(part - row_max) for part in parts]
    total = functools.reduce(jnp.add, [jnp.sum(term, -1, keepdims=True) for term in terms])
    inverse = 1.0 / total
    return [term * inverse for term in terms]


def key_spans(step, block):
    spans = [slice(0, step * block)] if step else []
    return spans + [slice(step * block, (step + 1) * block)]


def attention_forward_kernel(heads, block, q_ref, k_ref, v_ref, out_ref):
    for head in range(heads):
        column = slice(head * HEAD_DIM, (head + 1) * HEAD_DIM)
        for step in range(q_ref.shape[0] // block):
            rows = slice(step * block, (step + 1) * block)
            probs = softmax_of(score_parts(q_ref[rows, column], k_ref, column, step, block))
            mixed = functools.reduce(
                jnp.add,
                [
                    product(prob.astype(bf16), v_ref[span, column])
                    for prob, span in zip(probs, key_spans(step, block))
                ],
            )
            out_ref[rows, column] = mixed.astype(bf16)


def attention_backward_kernel(
    heads, block, rows, scalars, q_ref, k_ref, v_ref, *refs
):
    scale = HEAD_DIM ** (-0.5)
    pieces, (dq_ref, dk_ref, dv_ref, held, k_acc, v_acc, sems) = refs[:-7], refs[-7:]
    step_now, lanes = pl.program_id(0), dq_ref.shape[1]

    @pl.when(step_now == 0)
    def _():
        wait_all(
            start_all(
                [
                    pltpu.make_async_copy(piece, held.at[aligned(scalars[i], rows)], sems.at[i])
                    for i, piece in enumerate(pieces)
                ]
            )
        )

    grads = held[...] if held.shape[1] == lanes else held[:, aligned(step_now, lanes)]
    for head in range(heads):
        column = slice(head * HEAD_DIM, (head + 1) * HEAD_DIM)
        for step in reversed(range(q_ref.shape[0] // block)):
            span_rows = slice(step * block, (step + 1) * block)
            spans = key_spans(step, block)
            q_part, o_part = q_ref[span_rows, column], grads[span_rows, column]
            probs = softmax_of(score_parts(q_part, k_ref, column, step, block))
            prob_grads = [right_product(o_part, v_ref[span, column]) for span in spans]
            delta = functools.reduce(
                jnp.add,
                [jnp.sum(p * g, -1, keepdims=True) for p, g in zip(probs, prob_grads)],
            )
            score_grads = [(p * (g - delta)).astype(bf16) for p, g in zip(probs, prob_grads)]
            q_grad = functools.reduce(
                jnp.add,
                [product(s, k_ref[span, column]) for s, span in zip(score_grads, spans)],
            )
            dq_ref[span_rows, column] = (q_grad * scale).astype(bf16)
            first = step == q_ref.shape[0] // block - 1
            for span, score_grad, prob in zip(spans, score_grads, probs):
                key_grad = left_product(score_grad, q_part)
                value_grad = left_product(prob.astype(bf16), o_part)
                k_acc[span, column] = key_grad if first else k_acc[span, column] + key_grad
                v_acc[span, column] = value_grad if first else v_acc[span, column] + value_grad
    dk_ref[...] = (k_acc[...] * scale).astype(bf16)
    dv_ref[...] = v_acc[...].astype(bf16)


def attention_plan(qkv, width):
    length = qkv.shape[0]
    heads = min(2, width // HEAD_DIM)
    block = min(256, length)
    lanes = heads * HEAD_DIM
    steps = width // lanes
    whole = lanes % LANES == 0
    joined = [qkv] * 3 if whole else [qkv[:, i * width : (i + 1) * width] for i in range(3)]

    def spec(part):
        first = part * steps if whole else 0
        return pl.BlockSpec((length, lanes), lambda step: (0, first + step))

    return length, heads, block, lanes, steps, spec, joined


def attention_forward(qkv, width):
    length, heads, block, lanes, steps, spec, joined = attention_plan(qkv, width)
    return run(
        functools.partial(attention_forward_kernel, heads, block),
        "attention_forward",
        10,
        joined,
        [spec(0), spec(1), spec(2)],
        [((length, width), bf16)],
        [spec(0)],
        [],
        (steps,),
    )[0]


def attention_backward(scalars, qkv, pieces, width):
    length, heads, block, lanes, steps, spec, joined = attention_plan(qkv, width)
    return run(
        functools.partial(attention_backward_kernel, heads, block, pieces[0].shape[0]),
        "attention_backward",
        18,
        [scalars] + joined + pieces,
        [scalar, spec(0), spec(1), spec(2)] + [anywhere] * len(pieces),
        [((length, width), bf16)] * 3,
        [spec(0)] * 3,
        [
            pltpu.VMEM((length, width), bf16),
            pltpu.VMEM((length, lanes), f32),
            pltpu.VMEM((length, lanes), f32),
            pltpu.SemaphoreType.DMA((len(pieces),)),
        ],
        (steps,),
    )


def hidden_kernel(ctx, scalars, small_ref, out_ref, tokens_ref, sort_ref, *refs):
    pieces, (hidden_ref, norm_ref, sorted_ref) = refs[:ctx], refs[ctx:]
    own = pieces[0].shape[1]
    hidden = tokens_ref[...].astype(f32) + (
        sum(
            product(piece[...], out_ref[aligned(scalars[i], own), :])
            for i, piece in enumerate(pieces)
        )
        + small_ref[OUT_BIAS : OUT_BIAS + 1, :]
    )
    hidden_ref[...] = hidden
    normed, _ = layer_stats(hidden)
    low = (
        normed * small_ref[GAIN_TWO : GAIN_TWO + 1, :] + small_ref[SHIFT_TWO : SHIFT_TWO + 1, :]
    ).astype(bf16)
    norm_ref[...] = low
    sorted_ref[...] = product(sort_ref[...], low).astype(bf16)


def make_hidden(scalars, small, full_out, tokens, sort, pieces):
    shape = tokens.shape
    return run(
        functools.partial(hidden_kernel, len(pieces)),
        "hidden",
        4,
        [scalars, small, full_out, tokens, sort] + pieces,
        [scalar] + [inside] * (4 + len(pieces)),
        [(shape, f32), (shape, bf16), (shape, bf16)],
        [inside] * 3,
        [],
    )


def mlp_kernel(plan, scalars, small_ref, by_column, *refs):
    dp, ctx, rows, start, count, expert, merged, last = plan
    base = 2 if expert == 1 else 0
    depth = dp // 2
    refs = list(refs)

    def take(number):
        taken = refs[:number]
        del refs[:number]
        return taken

    x_parts, g_parts = take(ctx), take(ctx)
    parts = take(dp if merged else 2 * dp)
    sums = take(6) if last else []
    if last:
        y_refs, gx_refs = take(ctx), take(ctx)
    else:
        y_ref, gx_ref, dots_out = take(3)
    (gb_ref,) = take(1)
    mine, other = take(1 if merged else 2), take(1 if merged else 2)
    up, down, x_all, x_turned, g_all, act_all, go_all, gu_all, up_grad, down_grad = take(10)
    pre_all, back_all = take(2)
    held = take(6) if last else take(2)
    in_sems, x_sems, out_sems, held_sems = take(4)
    width, hidden = up.shape
    up_rows, down_rows = width // dp, hidden // dp
    tile = min(256, hidden)
    tiles = [slice(at, at + tile) for at in range(0, hidden, tile)]
    total = ctx * count

    def loads(target, size, which):
        return [
            pltpu.make_async_copy(
                parts[i].at[base + which] if merged else parts[which * dp + i],
                target.at[aligned(scalars[i], size)],
                in_sems.at[which * dp + i],
            )
            for i in range(dp)
        ]

    def rows_of(block):
        return slice(block * count, (block + 1) * count)

    tokens = [
        pltpu.make_async_copy(
            part.at[start : start + count], x_all.at[rows_of(i)], x_sems.at[i]
        )
        for i, part in enumerate(x_parts)
    ]
    grads = [
        pltpu.make_async_copy(
            part.at[start : start + count], g_all.at[rows_of(i)], x_sems.at[ctx + i]
        )
        for i, part in enumerate(g_parts)
    ]
    ups, downs = loads(up, up_rows, 0), loads(down, down_rows, 1)
    start_all(tokens + ups + grads + downs)
    gathered = [
        pltpu.make_async_copy(ref, held[i], held_sems.at[i]) for i, ref in enumerate(sums)
    ]
    start_all(gathered)
    wait_all(tokens)
    logits = product(x_all[...], small_ref[...])
    route_zero, route_one = logits[:, ROUTER : ROUTER + 1], logits[:, ROUTER + 1 : ROUTER + 2]
    mix_zero, mix_one = logits[:, MIX : MIX + 1], logits[:, MIX + 1 : MIX + 2]
    if expert is None:
        mask = None
        coef = sigmoid_pair(mix_zero, mix_one)
    else:
        place = lax.broadcasted_iota(jnp.int32, (count, 1), 0) + start
        firsts = [place < scalars[dp + block] for block in range(ctx)]
        masks = [(first if expert == 0 else ~first).astype(f32) for first in firsts]
        mask = jnp.concatenate(masks, 0)
        gate = (
            sigmoid_pair(route_zero, route_one)
            if expert == 0
            else sigmoid_pair(route_one, route_zero)
        )
        coef = sigmoid_pair(mix_one, mix_zero) * gate * mask
    x_turned[...] = jnp.transpose(x_all[...])
    wait_all(grads)
    go_all[...] = (g_all[...].astype(f32) * coef).astype(bf16)
    wait_all(ups)

    piece = 64 if total % 64 == 0 else 16

    def activate(cut):
        bias = by_column[:, cut]
        column_sum = jnp.zeros((8, tile), f32)
        for at in range(0, total, piece):
            span = slice(at, at + piece)
            pre = pre_all[span, :] + bias
            square = pre * pre
            bend = jnp.tanh((ROOT * pre) * (1.0 + CUBE * square))
            half = 0.5 + 0.5 * bend
            act_all[span, cut] = (pre * half).astype(bf16)
            slope = half + ((0.5 * ROOT) * pre) * (1.0 - bend * bend) * (
                1.0 + (3.0 * CUBE) * square
            )
            grad_up = (back_all[span, :] * slope).astype(bf16)
            gu_all[span, cut] = grad_up
            column_sum = column_sum + jnp.sum(
                grad_up.astype(f32).reshape(piece // 8, 8, tile), 0
            )
        gb_ref[:, cut] = jnp.sum(column_sum, 0, keepdims=True)

    for number, cut in enumerate(tiles):
        pre_all[...] = product(x_all[...], up[:, cut])
        if number == 0:
            wait_all(downs)
        back_all[...] = right_product(go_all[...], down[cut, :])
        activate(cut)
        down_grad[cut, :] = left_product(act_all[:, cut], go_all[...]).astype(bf16)
        up_grad[:, cut] = product(x_turned[...], gu_all[:, cut]).astype(bf16)

    def stores(grad, size, which):
        targets = [
            (mine[0].at[i, which] if merged else mine[which].at[i])
            if i < depth
            else (other[0].at[i - depth, which] if merged else other[which].at[i - depth])
            for i in range(dp)
        ]
        return [
            pltpu.make_async_copy(
                grad.at[aligned(scalars[i], size)], target, out_sems.at[which * dp + i]
            )
            for i, target in enumerate(targets)
        ]

    saved = start_all(stores(up_grad, up_rows, 0) + stores(down_grad, down_rows, 1))
    wait_all(gathered)
    sums_sent = []
    for block in range(ctx):
        span = rows_of(block)
        out = product(act_all[span, :], down[...])
        grad_x = right_product(gu_all[span, :], up[...])
        dot = jnp.sum(g_all[span, :].astype(f32) * out, -1, keepdims=True)
        out = out * coef[span]
        if not last:
            held[0][span, :], held[1][span, :] = out, grad_x
            for number, target in enumerate((y_ref, gx_ref)):
                copy = pltpu.make_async_copy(
                    held[number].at[span], target.at[span], held_sems.at[2 * block + number]
                )
                copy.start()
                sums_sent.append(copy)
            dots_out[span, :] = dot if mask is None else dot * mask[span]
            continue
        y_dense, gx_dense, dots_dense, y_first, gx_first, dots_first = held
        whole = slice(block * rows, (block + 1) * rows)
        sets = ((y_dense, y_first, out, y_refs), (gx_dense, gx_first, grad_x, gx_refs))
        for dense, first, own, target in sets:
            early = dense[whole, :][:start] + first[span, :][:start]
            middle = dense[whole, :][start:count] + (first[span, :][start:] + own[: count - start])
            late = dense[whole, :][count:] + own[count - start :]
            target[block][0:start, 0:width] = early.astype(bf16)
            target[block][start:count, 0:width] = middle.astype(bf16)
            target[block][count:rows, 0:width] = late.astype(bf16)
        own_dot = dot * mask[span]
        first_dot = dots_first[span, :]
        moe = jnp.concatenate(
            [
                first_dot[:start],
                first_dot[start:] + own_dot[: count - start],
                own_dot[count - start :],
            ],
            0,
        )
        lane = lax.broadcasted_iota(jnp.int32, (rows, LANES), 1)
        both = jnp.where(lane % 2 == 0, dots_dense[whole, :], moe)
        high, middle, low = three_parts(both)
        extra = jnp.where(lane < 2, high.astype(f32), jnp.where(lane < 4, middle.astype(f32), low.astype(f32)))
        gx_refs[block][:, width:] = jnp.where(lane < 6, extra, 0.0).astype(bf16)
    wait_all(saved + sums_sent)


def mlp(scalars, small, bias, x, g, parts, expert, merged, sums):
    ctx = len(x)
    rows, width = x[0].shape
    dp = len(parts) if merged else len(parts) // 2
    depth = dp // 2
    hidden = bias.shape[1]
    count = rows if expert is None else rows * 5 // 8
    start = 0 if expert in (None, 0) else rows - count
    total = ctx * count
    last = expert == 1
    if merged:
        halves = [((depth, 2) + parts[0].shape[1:], bf16)]
    else:
        halves = [((depth,) + parts[0].shape, bf16), ((depth,) + parts[dp].shape, bf16)]
    if last:
        outs = [((rows, width), bf16)] * ctx + [((rows, width + LANES), bf16)] * ctx
    else:
        outs = [((total, width), f32), ((total, width), f32), ((total, 1), f32)]
    outs = outs + [((1, hidden), f32)] + halves + halves
    small_outs = len(outs) - 2 * len(halves)
    held = [pltpu.VMEM(ref.shape, f32) for ref in sums] or [pltpu.VMEM((total, width), f32)] * 2
    tile = min(256, hidden)
    return run(
        functools.partial(mlp_kernel, (dp, ctx, rows, start, count, expert, merged, last)),
        "mlp",
        20 if total % LANES == 0 and expert is None else 18,
        [scalars, small, bias] + x + g + parts + sums,
        [scalar, inside, inside] + [anywhere] * (2 * ctx + len(parts) + len(sums)),
        outs,
        ([] if last else [anywhere] * 2)
        + [inside] * (small_outs if last else small_outs - 2)
        + [anywhere] * (2 * len(halves)),
        [
            pltpu.VMEM((width, hidden), bf16),
            pltpu.VMEM((hidden, width), bf16),
            pltpu.VMEM((total, width), bf16),
            pltpu.VMEM((width, total), bf16),
            pltpu.VMEM((total, width), bf16),
            pltpu.VMEM((total, hidden), bf16),
            pltpu.VMEM((total, width), bf16),
            pltpu.VMEM((total, hidden), bf16),
            pltpu.VMEM((width, hidden), bf16),
            pltpu.VMEM((hidden, width), bf16),
            pltpu.VMEM((total, tile), f32),
            pltpu.VMEM((total, tile), f32),
        ]
        + held
        + [
            pltpu.SemaphoreType.DMA((2 * dp,)),
            pltpu.SemaphoreType.DMA((2 * ctx,)),
            pltpu.SemaphoreType.DMA((2 * dp,)),
            pltpu.SemaphoreType.DMA((max(2 * ctx, len(sums)),)),
        ],
    )


def middle_kernel(
    ctx, scalars, by_row, by_column, out_ref, hidden_ref, norm_ref, g_ref, first_ref, unsort_ref, *refs
):
    gx, pieces = refs[:ctx], refs[ctx : 2 * ctx]
    outs = refs[2 * ctx :]
    base_ref, grad_hidden_ref, rows_ref, router_ref = outs[:4]
    out_grads, grad_pieces = outs[4 : 4 + ctx], outs[4 + ctx : 4 + 2 * ctx]
    out_all, sems = outs[4 + 2 * ctx :]
    rows, width = hidden_ref.shape
    own = pieces[0].shape[1]
    unsort = unsort_ref[...]
    gathered = sum(product(unsort, piece[...]) for piece in gx)
    grad_norm = gathered[:, :width]
    extra = gathered[:, width:]
    dense_dot = extra[:, 0:1] + (extra[:, 2:3] + extra[:, 4:5])
    moe_dot = extra[:, 1:2] + (extra[:, 3:4] + extra[:, 5:6])
    grad_out = g_ref[...].astype(f32)
    first = first_ref[...]
    down_bias = by_column[DOWN_BIAS : DOWN_BIAS + 1, :]
    moe_bias = jnp.where(
        first > 0.5,
        by_column[EXPERT_DOWN : EXPERT_DOWN + 1, :],
        by_column[EXPERT_DOWN + 1 : EXPERT_DOWN + 2, :],
    )
    dense_dot = dense_dot + jnp.sum(grad_out * down_bias, -1, keepdims=True)
    moe_dot = moe_dot + jnp.sum(grad_out * moe_bias, -1, keepdims=True)
    norm = norm_ref[...]
    logits = product(norm, by_row[...])
    route = [
        sigmoid_pair(logits[:, a : a + 1], logits[:, b : b + 1])
        for a, b in ((ROUTER, ROUTER + 1), (ROUTER + 1, ROUTER))
    ]
    mix = [
        sigmoid_pair(logits[:, a : a + 1], logits[:, b : b + 1])
        for a, b in ((MIX, MIX + 1), (MIX + 1, MIX))
    ]
    hot = [first, 1.0 - first]
    gate = route[0] * hot[0] + route[1] * hot[1]
    branch = mix[1] * gate
    hidden = hidden_ref[...]
    base_ref[...] = hidden + (mix[0] * down_bias + branch * moe_bias)
    grad_mix = [dense_dot, moe_dot * gate]
    mean_mix = mix[0] * grad_mix[0] + mix[1] * grad_mix[1]
    grad_gate = moe_dot * mix[1]
    grad_route = [hot[0] * grad_gate, hot[1] * grad_gate]
    mean_route = route[0] * grad_route[0] + route[1] * grad_route[1]
    lane = lax.broadcasted_iota(jnp.int32, (rows, LANES), 1)
    columns = [route[i] * (grad_route[i] - mean_route) for i in range(2)]
    columns += [mix[i] * (grad_mix[i] - mean_mix) for i in range(2)]
    logit_grads = jnp.zeros((rows, LANES), f32)
    for i, column in enumerate(columns):
        logit_grads = jnp.where(lane == i, column, logit_grads)
    split = three_parts(logit_grads)
    weights = by_row[...]
    for part in split:
        grad_norm = grad_norm + right_product(part, weights)
    router_ref[...] = sum(left_product(norm, part) for part in split)
    grad_dense = (grad_out * mix[0]).astype(bf16).astype(f32)
    grad_moe = (grad_out * branch).astype(bf16).astype(f32)
    normed, inverse = layer_stats(hidden)
    gain = by_column[GAIN_TWO : GAIN_TWO + 1, :]
    grad_hidden = grad_out + norm_back(grad_norm, normed, inverse, gain)
    grad_hidden_ref[...] = grad_hidden
    low = grad_hidden.astype(bf16)

    def total(values):
        return jnp.sum(values, 0, keepdims=True)

    sums = [
        total(low.astype(f32)),
        total(grad_norm * normed),
        total(grad_norm),
        total(grad_dense),
        total(grad_moe * hot[0]),
        total(grad_moe * hot[1]),
        jnp.zeros((2, width), f32),
    ]
    rows_ref[...] = jnp.concatenate(sums, 0)
    for i, (piece, target) in enumerate(zip(pieces, grad_pieces)):
        span = aligned(scalars[i], own)
        target[...] = right_product(low, out_ref[span, :]).astype(bf16)
        part = left_product(piece[...], low).astype(bf16)
        share = out_all.shape[3]
        many = own // (ctx * share)
        for c in range(ctx):
            columns = part[:, c * own : (c + 1) * own].reshape(many, ctx, share, own)
            out_all[aligned(scalars[i], many), :, c] = columns
    wait_all(
        start_all(
            [
                pltpu.make_async_copy(out_all.at[:, scalars[i]], target, sems.at[i])
                for i, target in enumerate(out_grads)
            ]
        )
    )


def make_middle(
    scalars, by_row, by_column, full_out, hidden, norm, g, first, unsort, gx, pieces, dp
):
    ctx = len(gx)
    rows, width = hidden.shape
    own = pieces[0].shape[1]
    return run(
        functools.partial(middle_kernel, ctx),
        "middle",
        11,
        [scalars, by_row, by_column, full_out, hidden, norm, g, first, unsort] + gx + pieces,
        [scalar] + [inside] * (8 + 2 * ctx),
        [
            ((rows, width), f32),
            ((rows, width), f32),
            ((8, width), f32),
            ((width, LANES), f32),
        ]
        + [((dp, ctx, width // (dp * ctx), own), bf16)] * ctx
        + [((rows, own), bf16)] * ctx,
        [inside] * 4 + [anywhere] * ctx + [inside] * ctx,
        [
            pltpu.VMEM((dp, ctx, ctx, width // (dp * ctx), own), bf16),
            pltpu.SemaphoreType.DMA((ctx,)),
        ],
    )


def qkv_back_kernel(plan, scalars, norm_ref, dq_ref, dk_ref, dv_ref, weight_ref, *refs):
    dp, ctx, rows, own = plan
    depth = dp // 2
    out_pieces, gn_refs = refs[:ctx], refs[ctx : 2 * ctx]
    mine, other, bias_ref, grad, weight_grad, gn, sems, gn_sems = refs[2 * ctx :]
    width = norm_ref.shape[1]
    size = width // dp
    for part, ref in enumerate((dq_ref, dk_ref, dv_ref)):
        grad[:, part * own : (part + 1) * own] = ref[...]
    tile = min(256, ctx * rows)
    weight = weight_ref[:, : 3 * own]
    for at in range(0, ctx * rows, tile):
        gn[at : at + tile, :] = right_product(grad[at : at + tile, :], weight).astype(bf16)
    sent = start_all(
        [
            pltpu.make_async_copy(gn.at[aligned(scalars[dp + i], rows)], ref, gn_sems.at[i])
            for i, ref in enumerate(gn_refs)
        ]
    )
    step = min(256, width)
    for at in range(0, width, step):
        weight_grad[at : at + step, : 3 * own] = left_product(
            norm_ref[:, at : at + step], grad[...]
        ).astype(bf16)
    weight_grad[:, 3 * own :] = sum(piece[...].astype(f32) for piece in out_pieces).astype(bf16)
    saved = start_all(
        [
            pltpu.make_async_copy(
                weight_grad.at[aligned(scalars[i], size)],
                mine.at[i] if i < depth else other.at[i - depth],
                sems.at[i],
            )
            for i in range(dp)
        ]
    )
    bias_ref[...] = jnp.sum(grad[...].astype(f32), 0, keepdims=True)
    wait_all(sent + saved)


def qkv_back(scalars, norm, grads, weight, out_pieces, plan):
    dp, ctx, rows, own = plan
    length, width = norm.shape
    half = ((dp // 2, width // dp, 4 * own), bf16)
    return run(
        functools.partial(qkv_back_kernel, plan),
        "qkv_back",
        8,
        [scalars, norm] + list(grads) + [weight] + list(out_pieces),
        [scalar] + [inside] * (5 + ctx),
        [((rows, width), bf16)] * ctx + [half, half, ((1, 3 * own), f32)],
        [anywhere] * (ctx + 2) + [inside],
        [
            pltpu.VMEM((length, 3 * own), bf16),
            pltpu.VMEM((width, 4 * own), bf16),
            pltpu.VMEM((length, width), bf16),
            pltpu.SemaphoreType.DMA((dp,)),
            pltpu.SemaphoreType.DMA((ctx,)),
        ],
    )


def final_kernel(ctx, order, by_column, tokens_ref, grad_hidden_ref, *refs):
    pieces, (grad_ref, rows_ref) = refs[:ctx], refs[ctx:]
    grad_norm = sum(piece[...].astype(f32) for piece in pieces)
    normed, inverse = layer_stats(tokens_ref[...].astype(f32))
    gain = by_column[GAIN_ONE : GAIN_ONE + 1, :]
    grad_ref[...] = grad_hidden_ref[...] + norm_back(grad_norm, normed, inverse, gain)
    rows_ref[0:1, :] = jnp.sum(grad_norm * normed, 0, keepdims=True)
    rows_ref[1:2, :] = jnp.sum(grad_norm, 0, keepdims=True)


def make_final(order, by_column, tokens, grad_hidden, pieces):
    return run(
        functools.partial(final_kernel, len(pieces)),
        "final",
        4,
        [order, by_column, tokens, grad_hidden] + pieces,
        [scalar] + [inside] * (3 + len(pieces)),
        [(tokens.shape, f32), ((2, tokens.shape[1]), f32)],
        [inside] * 2,
        [],
    )


def result_kernel(ctx, base_ref, unsort_ref, *refs):
    pieces, (out_ref,) = refs[:ctx], refs[ctx:]
    unsort = unsort_ref[...]
    out_ref[...] = base_ref[...] + sum(product(unsort, piece[...]) for piece in pieces)


def make_result(base, unsort, pieces):
    return run(
        functools.partial(result_kernel, len(pieces)),
        "result",
        3.5,
        [base, unsort] + pieces,
        [inside] * (2 + len(pieces)),
        [(base.shape, f32)],
        [inside],
        [],
    )[0]


def layer(
    dp,
    ctx,
    tokens,
    cotangent,
    routes,
    ln1_gain,
    ln1_bias,
    qkv_weight,
    qv_bias,
    out_weight,
    out_bias,
    ln2_gain,
    ln2_bias,
    up_weight,
    up_bias,
    down_weight,
    down_bias,
    router_weight,
    mix_weight,
    expert_up,
    expert_up_bias,
    expert_down,
    expert_down_bias,
):
    rows, width = tokens.shape[0] * tokens.shape[1], tokens.shape[2]
    experts, share, hidden = expert_up.shape
    own_hidden = hidden // ctx
    own_width = width // ctx
    unit = hidden // (dp * ctx)
    me = lax.axis_index("ctx")
    place_dp = lax.axis_index("dp")
    core = place_dp % 2
    depth = dp // 2
    shifts = range(1, ctx)
    ring_pairs = [(i, (i + 2) % dp) for i in range(dp)]
    core_pairs = [(i, i ^ 1) for i in range(dp)]
    places = jnp.stack(
        [
            ((place_dp // 2 + depth - t) % depth) * 2 + c
            for c in (core, 1 - core)
            for t in range(depth)
        ]
    ).astype(jnp.int32)
    peers = jnp.stack([me ^ s for s in range(ctx)]).astype(jnp.int32)

    def swap(array, shift):
        return lax.ppermute(array, "ctx", [(i, i ^ shift) for i in range(ctx)])

    def gather_ctx(array):
        return [array] + [swap(array, s) for s in shifts]

    def trade(pieces):
        return [pieces[0]] + [swap(pieces[s], s) for s in shifts]

    def by_peer(pieces):
        return [lax.dynamic_index_in_dim(pieces, me ^ s, 0, keepdims=False) for s in range(ctx)]

    def natural(pieces):
        whole = jnp.zeros((ctx,) + pieces[0].shape, pieces[0].dtype)
        for s, piece in enumerate(pieces):
            whole = lax.dynamic_update_slice_in_dim(whole, piece[None], me ^ s, 0)
        return whole

    def ring(array):
        return lax.ppermute(array, "dp", ring_pairs)

    def swap_core(array):
        return lax.ppermute(array, "dp", core_pairs)

    def sync(*trees):
        return lax.optimization_barrier(trees)

    class Rings:
        def __init__(self, arrays):
            self.parts = [list(arrays)]

        def move(self):
            self.parts.append([ring(array) for array in self.parts[-1]])

        def rest(self):
            while len(self.parts) < depth:
                self.move()

        def pieces(self, others, which):
            return [part[which] for part in self.parts] + [part[which] for part in others]

    def swap_cores(part):
        return [swap_core(array) for array in part]

    class Scatter:
        def __init__(self, *halves):
            half = len(halves) // 2
            self.mine, self.step = list(halves[:half]), 0
            self.got = [swap_core(other) for other in halves[half:]]
            self.arrived = self.sent = None

        def receive(self, others):
            if self.sent is None:
                self.got, others = sync(self.got, others)
            else:
                self.arrived, others = sync([ring(part) for part in self.sent], others)
            return others

        def add(self):
            self.step += 1
            at = self.step % depth
            parts = [m[at].astype(f32) + g[at].astype(f32) for m, g in zip(self.mine, self.got)]
            if self.arrived is not None:
                parts = [p + c.astype(f32) for p, c in zip(parts, self.arrived)]
            self.sent = [part.astype(bf16) if at else part for part in parts]

        def move(self, others):
            others = self.receive(others)
            self.add()
            return others

        def close(self):
            self.add()
            while self.step < depth:
                self.arrived = [ring(part) for part in self.sent]
                self.add()

    def pin(value, *sums):
        value, sent = sync(value, [one.sent for one in sums])
        for one, parts in zip(sums, sent):
            one.sent = parts
        return value

    def pair(sums):
        return sums if len(sums) == 2 else [sums[0][0], sums[0][1]]

    tokens = tokens.reshape(rows, width)
    cotangent = cotangent.reshape(rows, width)
    first_hot = routes.reshape(rows) == 0
    first_float = first_hot.astype(f32)
    first_count = jnp.sum(first_float)

    def column(vector):
        return vector.reshape(-1, share).T

    def bias_column(vector):
        return jnp.pad(vector.reshape(unit, 1), ((0, ctx * share - unit), (0, 0)))

    small = jnp.concatenate(
        [
            router_weight,
            mix_weight,
            column(ln1_gain),
            column(ln1_bias),
            column(qv_bias),
            column(out_bias),
            column(ln2_gain),
            column(ln2_bias),
            column(down_bias),
            expert_down_bias.T,
            jnp.broadcast_to(first_count.astype(bf16), (share, 1)),
        ],
        1,
    )
    small = jnp.pad(small, ((0, 0), (0, LANES - small.shape[1])))
    qkv_cut = qkv_weight.reshape(share, 3, ctx, own_width).transpose(2, 0, 1, 3)
    first_cut = jnp.concatenate(
        [
            qkv_cut.reshape(ctx, share, 3 * own_width),
            jnp.broadcast_to(small[None], (ctx, share, LANES)),
        ],
        -1,
    )
    ups = jnp.concatenate([up_weight[None], expert_up], 0)
    ups_cut = ups.reshape(experts + 1, share, dp, ctx, unit).transpose(3, 0, 1, 2, 4)
    ups_sent = by_peer(ups_cut.reshape(ctx, experts + 1, share, own_hidden))
    first_rows, ups_sent = sync(trade(by_peer(first_cut)), ups_sent)
    first_rows = natural(first_rows).reshape(ctx * share, 3 * own_width + LANES)
    qkv_rows = first_rows[:, : 3 * own_width]
    small_rows = first_rows[:, 3 * own_width :]
    counts = small_rows[::share, COUNT]
    bias_lanes = jnp.concatenate(
        [bias_column(up_bias)] + [bias_column(expert_up_bias[e]) for e in range(experts)], 1
    )
    lane = jnp.arange(LANES)[None, :]
    bias_lanes = jnp.pad(bias_lanes, ((0, 0), (UP_BIAS, LANES - UP_BIAS - bias_lanes.shape[1])))
    small_rows = jnp.where((lane >= UP_BIAS) & (lane < UP_BIAS + experts + 1), bias_lanes, small_rows)
    out_rows = out_weight.reshape(share, ctx, own_width).transpose(1, 0, 2)
    out_rows = out_rows.reshape(ctx * share, own_width)
    first = Rings([jnp.concatenate([qkv_rows, out_rows, small_rows], 1)])

    first.move()
    first_others = [swap_cores(first.parts[0])]
    token_parts = gather_ctx(tokens)
    first.parts[1], first_others[0] = sync(first.parts[1], first_others[0])
    first.move()
    first_others.append(swap_cores(first.parts[1]))
    token_parts, first.parts[2], first_others[1], ups_sent = sync(
        token_parts, first.parts[2], first_others[1], ups_sent
    )
    first.rest()
    first_others += [swap_cores(part) for part in first.parts[2:-1]]
    ups_rows, first.parts[-1], first_others = sync(trade(ups_sent), first.parts[-1], first_others)
    ups_rows = natural(ups_rows).transpose(1, 0, 2, 3)
    ups_rows = ups_rows.reshape(experts + 1, ctx * share, own_hidden)
    downs = [down_weight] + [expert_down[e] for e in range(experts)]
    merged = downs[0].shape == ups_rows.shape[1:]
    if merged:
        dense_weights = [jnp.stack([ups_rows[0], downs[0]])]
        expert_weights = [jnp.stack([ups_rows[1], downs[1], ups_rows[2], downs[2]])]
    else:
        dense_weights = [ups_rows[0], downs[0]]
        expert_weights = [ups_rows[1], downs[1], ups_rows[2], downs[2]]
    dense_ring = Rings(dense_weights)
    dense_ring.move()
    first_others.append(swap_cores(first.parts[-1]))
    first_parts = first.pieces(first_others, 0)
    plan = (dp, ctx, share, own_width, experts)
    by_row, by_column, out_own = unpack(places, first_parts, plan)
    expert_weights, by_row = sync(expert_weights, by_row)
    expert_ring = Rings(expert_weights)
    expert_ring.move()
    out_pieces = gather_ctx(out_own)

    order = jnp.arange(rows).astype(f32)
    counted = jnp.cumsum(first_float)
    place = jnp.where(first_hot, counted - 1.0, first_count + order - counted)
    unsort = (place[:, None] == order[None, :]).astype(bf16)
    sort = (place[None, :] == order[:, None]).astype(bf16)
    sorted_grad = product(sort, cotangent).astype(bf16)

    scalars = jnp.concatenate([places, peers])
    qkv, attn_in, own_qkv = make_qkv(
        scalars, by_column, first_parts, token_parts, (dp, ctx, rows, own_width, share)
    )
    qkv, dense_ring.parts[1] = sync(qkv, dense_ring.parts[1])
    dense_ring.move()
    attended_heads = attention_forward(qkv, own_width)
    attended_heads, out_pieces = sync(attended_heads, out_pieces)
    attended = trade(by_peer(attended_heads.reshape(ctx, rows, own_width)))
    full_out = natural(out_pieces).reshape(ctx, dp, share, width).transpose(1, 0, 2, 3)
    full_out = full_out.reshape(width, width)
    hidden_state, ffn_in, sorted_in = make_hidden(
        peers, by_column, full_out, tokens, sort, attended
    )
    sorted_in, expert_ring.parts[1] = sync(sorted_in, expert_ring.parts[1])
    expert_ring.move()
    ffn_parts = gather_ctx(sorted_in)
    late_columns, late_counts, _ = sync(by_column, counts, sorted_in)
    row_counts = jnp.stack([late_counts[me ^ s] for s in range(ctx)]).astype(jnp.int32)
    mlp_scalars = jnp.concatenate([places, row_counts])
    up_biases = late_columns[UP_BIAS : UP_BIAS + experts + 1]
    up_biases = up_biases.reshape(experts + 1, dp, -1)[:, :, :unit].reshape(experts + 1, own_hidden)

    mlp_scalars = gate(mlp_scalars, *dense_ring.parts[2])
    ffn_parts, dense_ring.parts[2], sorted_grad, up_biases, mlp_scalars = sync(
        ffn_parts, dense_ring.parts[2], sorted_grad, up_biases, mlp_scalars
    )
    dense_ring.rest()
    grad_parts = [sorted_grad] + [swap(sorted_grad, s) for s in shifts[:2]]
    expert_ring.parts[2], late_grad = sync(expert_ring.parts[2], sorted_grad)
    expert_ring.rest()
    grad_parts += [swap(late_grad, s) for s in shifts[2:]]
    grad_parts, dense_ring.parts = sync(grad_parts, dense_ring.parts)
    dense_others = [swap_cores(part) for part in dense_ring.parts]
    dense_others, early = sync(dense_others, expert_ring.parts[:-1])
    expert_others = [swap_cores(part) for part in early]

    def run_mlp(which, held, parts, sums):
        return mlp(
            held,
            by_row,
            up_biases[which][None],
            ffn_parts,
            grad_parts,
            parts,
            which - 1 if which else None,
            merged,
            list(sums),
        )

    def weights_of(rings, others, first_array):
        if merged:
            return rings.pieces(others, 0)
        return rings.pieces(others, first_array) + rings.pieces(others, first_array + 1)

    dense = run_mlp(0, mlp_scalars, weights_of(dense_ring, dense_others, 0), [])
    sum_dense = Scatter(*dense[4:])
    expert_last, expert_others, gb_dense = sync(expert_ring.parts[-1], expert_others, dense[3])
    expert_ring.parts[-1] = expert_last
    expert_others = expert_others + [swap_cores(expert_last)]
    gb_dense = sum_dense.move(gb_dense)
    first_mlp = run_mlp(
        1,
        pin(gate(mlp_scalars), sum_dense),
        weights_of(expert_ring, expert_others, 0),
        [],
    )
    sum_first = Scatter(*first_mlp[4:])
    gb_first = sum_dense.move(first_mlp[3])
    second_mlp = run_mlp(
        2,
        pin(mlp_scalars, sum_dense),
        weights_of(expert_ring, expert_others, 2),
        dense[:3] + first_mlp[:3],
    )
    gb_second = sum_first.move(sum_dense.move(second_mlp[2 * ctx]))
    grad_sent = list(second_mlp[ctx : 2 * ctx])
    grad_pieces = trade(grad_sent[:3] + pin(grad_sent[3:], sum_dense, sum_first))
    grad_pieces, halves, result_sent = sync(
        grad_pieces, second_mlp[2 * ctx + 1 :], second_mlp[:ctx]
    )
    grad_pieces = sum_first.move(sum_dense.receive(grad_pieces))
    sum_second = Scatter(*halves)
    result_pieces = [result_sent[0]] + [swap(result_sent[s], s) for s in shifts[:2]]

    middle_peers, sum_dense.arrived = sync(peers, sum_dense.arrived)
    base, grad_hidden, middle_rows, router_grad, *rest = make_middle(
        pin(middle_peers, sum_first),
        by_row,
        by_column,
        full_out,
        hidden_state,
        ffn_in,
        cotangent,
        first_float[:, None],
        unsort,
        grad_pieces,
        attended,
        dp,
    )
    out_sent, att_sent = rest[:ctx], rest[ctx:]
    result_pieces, att_sent = sync(result_pieces, att_sent)
    att_grads, out_sent = sync(trade(att_sent), out_sent)
    out_sent = [piece.reshape(width, own_width) for piece in out_sent]
    out_pieces = trade(out_sent)
    middle_rows = sum_second.move(sum_first.move(middle_rows))

    grad_heads = attention_backward(pin(peers, sum_first, sum_second), qkv, att_grads, own_width)
    grad_heads = sum_second.move(sum_first.receive(grad_heads))
    back_scalars, sum_first.arrived = sync(pin(scalars, sum_second), sum_first.arrived)
    *norm_grads, last_mine, last_other, grad_b_qkv = qkv_back(
        back_scalars,
        attn_in,
        grad_heads,
        own_qkv,
        out_pieces,
        (dp, ctx, rows, own_width),
    )
    sum_last = Scatter(last_mine, last_other)
    norm_pieces = [norm_grads[0]] + [swap(norm_grads[s], s) for s in shifts[:2]]
    norm_pieces, late_grads, grad_b_qkv = sync(norm_pieces, list(norm_grads[3:]), grad_b_qkv)
    norm_pieces += [swap(piece, s) for piece, s in zip(late_grads, shifts[2:])]
    grad_b_qkv = sum_second.move(sum_last.move(grad_b_qkv))
    sum_dense.close()
    sum_first.close()
    grad_b_qkv = sum_last.move(grad_b_qkv)
    order_numbers, sum_second.arrived = sync(peers, [ring(part) for part in sum_second.sent])
    sum_second.close()

    def cut_columns(parts):
        joined = jnp.concatenate([part.astype(bf16) for part in parts], 1)
        return by_peer(joined.reshape(ctx, share, joined.shape[1]))

    def from_columns(pieces, at, size, groups):
        whole = natural([piece[:, at : at + size] for piece in pieces])
        whole = whole.reshape(ctx, share, groups, size // groups).transpose(1, 2, 0, 3)
        return whole.reshape(share, ctx * size).astype(f32)

    norm_pieces = pin(norm_pieces, sum_last, sum_second)
    grad_b_qkv = sum_last.move(grad_b_qkv)
    sums = [pair(one.sent) for one in (sum_dense, sum_first, sum_second)]
    early_sent = cut_columns([one[0] for one in sums])
    norm_pieces, early_sent, result_sent = sync(norm_pieces, early_sent, result_sent)
    early_pieces = trade(early_sent)
    result_pieces = result_pieces + [swap(result_sent[s], s) for s in shifts[2:]]
    grad_inputs, final_rows = make_final(
        order_numbers, by_column, tokens, grad_hidden, norm_pieces
    )
    final_rows, early_pieces = sum_last.receive((final_rows, early_pieces))
    sum_last.close()
    final_rows, result_pieces = pin((final_rows, result_pieces), sum_last)

    zero_qv = jnp.zeros((2, width), f32)
    grad_qv = lax.dynamic_update_slice(
        zero_qv,
        jnp.concatenate([grad_b_qkv[:, :own_width], grad_b_qkv[:, 2 * own_width :]], 0),
        (0, me * own_width),
    )

    def own_columns(array):
        whole = jnp.zeros((dp, ctx, array.shape[-1]), f32)
        return lax.dynamic_update_slice_in_dim(whole, array[:, None], me, 1)

    upb_grads = [gb_dense[0], gb_first[0], gb_second[0]]
    expert_upb = jnp.stack(upb_grads[1:]).reshape(experts, dp, unit).transpose(1, 0, 2)
    small_grads = [
        final_rows[0],
        final_rows[1],
        grad_qv,
        middle_rows[0],
        middle_rows[1],
        middle_rows[2],
        middle_rows[3],
        router_grad[:, :experts],
        router_grad[:, experts : 2 * experts],
        middle_rows[4 : 4 + experts].reshape(experts, dp, ctx, share).transpose(1, 2, 0, 3),
        own_columns(upb_grads[0].reshape(dp, unit)),
        own_columns(expert_upb.reshape(dp, experts * unit)),
    ]
    sizes = [grad.size // (dp * ctx) for grad in small_grads]
    small_sum = jnp.concatenate([g.reshape(dp, ctx, -1) for g in small_grads], -1)
    small_pieces = trade(by_peer(small_sum.transpose(1, 0, 2)))

    (last_sum,) = sum_last.sent
    qkv_part, out_sums = last_sum[:, : 3 * own_width], last_sum[:, 3 * own_width :]
    out_sums = out_sums.reshape(ctx, share, own_width).transpose(1, 0, 2).reshape(share, width)
    small_sum = sum(small_pieces).reshape(dp, 1, -1)[places]
    small_sum = small_sum[:depth] + swap_core(small_sum[depth:])
    pairs = [[(i, (i + dp - 2 * t) % dp) for i in range(dp)] for t in range(depth)]
    small_sum = sum(
        [small_sum[0]] + [lax.ppermute(small_sum[t], "dp", pairs[t]) for t in range(1, depth)]
    )[0]
    late_pieces = trade(cut_columns([qkv_part]))
    result = make_result(base, unsort, result_pieces)
    up_grads = [
        from_columns(early_pieces, 0, own_hidden, dp),
        from_columns(early_pieces, own_hidden, own_hidden, dp),
        from_columns(early_pieces, 2 * own_hidden, own_hidden, dp),
    ]
    qkv_grad = from_columns(late_pieces, 0, 3 * own_width, 3)
    down_sums = [one[1] for one in sums]
    outs, at = [], 0
    for size in sizes:
        outs.append(small_sum[at : at + size])
        at += size
    return (
        result[None],
        grad_inputs[None],
        outs[0],
        outs[1],
        qkv_grad,
        outs[2],
        out_sums,
        outs[3],
        outs[4],
        outs[5],
        up_grads[0],
        outs[10],
        down_sums[0],
        outs[6],
        outs[7].reshape(router_weight.shape),
        outs[8].reshape(mix_weight.shape),
        jnp.stack(up_grads[1:]),
        outs[11].reshape(expert_up_bias.shape),
        jnp.stack(down_sums[1:]),
        outs[9].reshape(expert_down_bias.shape),
    )


def solution(mesh):
    both = ("dp", "ctx")
    data = P("dp", "ctx", None)
    vector = P(both)
    matrix = P(both, None)
    expert_matrix = P(None, both, None)
    expert_vector = P(None, both)
    weights = (
        vector,
        vector,
        matrix,
        vector,
        matrix,
        vector,
        vector,
        vector,
        matrix,
        vector,
        matrix,
        vector,
        matrix,
        matrix,
        expert_matrix,
        expert_vector,
        expert_matrix,
        expert_vector,
    )
    return jax.shard_map(
        functools.partial(layer, mesh.shape["dp"], mesh.shape["ctx"]),
        mesh=mesh,
        in_specs=(data, data, data) + weights,
        out_specs=(data, data) + weights,
        check_vma=False,
    )
```

```python
import functools

import jax
import jax.numpy as jnp
from jax import lax
from jax.experimental import pallas as pl
from jax.experimental.pallas import tpu as pltpu
from jax.sharding import PartitionSpec as P

HEAD_DIM = 64
EPSILON = 1e-05
ROOT = 0.7978845608028654
CUBE = 0.044715
LANES = 128
f32 = jnp.float32
bf16 = jnp.bfloat16

ROUTER, MIX, GAIN_ONE, SHIFT_ONE, QV, OUT_BIAS, GAIN_TWO, SHIFT_TWO = 0, 2, 12, 13, 14, 16, 17, 18
DOWN_BIAS, EXPERT_DOWN, COUNT, UP_BIAS = 19, 20, 22, 23
SMALL_ROWS = 32

anywhere = pl.BlockSpec(memory_space=pl.ANY)
inside = pl.BlockSpec(memory_space=pltpu.VMEM)
scalar = pl.BlockSpec(memory_space=pltpu.SMEM)


def product(left_op, right_op):
    return jnp.dot(left_op, right_op, preferred_element_type=f32)


def left_product(left_op, right_op):
    return lax.dot_general(left_op, right_op, (((0,), (0,)), ((), ())), preferred_element_type=f32)


def right_product(left_op, right_op):
    return lax.dot_general(left_op, right_op, (((1,), (1,)), ((), ())), preferred_element_type=f32)


def layer_stats(values):
    row_mean = jnp.mean(values, -1, keepdims=True)
    centred = values - row_mean
    inverse = lax.rsqrt(jnp.mean(centred * centred, -1, keepdims=True) + EPSILON)
    return (centred * inverse, inverse)


def norm_back(grad_norm, normed, inverse, gain):
    scaled = grad_norm * gain
    return inverse * (
        scaled
        - jnp.mean(scaled, -1, keepdims=True)
        - normed * jnp.mean(scaled * normed, -1, keepdims=True)
    )


def sigmoid_pair(low, high):
    return 1.0 / (1.0 + jnp.exp(high - low))


def three_parts(values):
    high = values.astype(bf16)
    rest = values - high.astype(f32)
    middle = rest.astype(bf16)
    return high, middle, (rest - middle.astype(f32)).astype(bf16)


def aligned(index, size):
    return pl.ds(pl.multiple_of(index * size, size), size)


def run(kernel, name, micros, inputs, specs, outs, out_specs, scratch, grid=()):
    return pl.pallas_call(
        kernel,
        grid=grid,
        in_specs=specs,
        out_specs=out_specs,
        out_shape=[jax.ShapeDtypeStruct(shape, kind) for shape, kind in outs],
        scratch_shapes=scratch,
        compiler_params=pltpu.CompilerParams(
            dimension_semantics=("arbitrary",) * len(grid), vmem_limit_bytes=56 * 1024 * 1024
        ),
        cost_estimate=pl.CostEstimate(
            flops=int(micros * 10**9), bytes_accessed=1024, transcendentals=0
        ),
        name=name,
    )(*inputs)


def gate_kernel(*refs):
    in_ref, out_ref = refs[0], refs[-1]
    for i in range(in_ref.shape[0]):
        out_ref[i] = in_ref[i]


def gate(scalars, *others):
    return pl.pallas_call(
        gate_kernel,
        in_specs=[scalar] + [anywhere] * len(others),
        out_specs=scalar,
        out_shape=jax.ShapeDtypeStruct(scalars.shape, scalars.dtype),
        cost_estimate=pl.CostEstimate(flops=3 * 10**10, bytes_accessed=1024, transcendentals=0),
        name="gate",
    )(scalars, *others)


def start_all(copies):
    for copy in copies:
        copy.start()
    return copies


def wait_all(copies):
    for copy in copies:
        copy.wait()


def unpack_kernel(plan, places, *refs):
    dp, ctx, share, own, experts = plan
    parts, (by_row, by_column, out_ref), (held, sems) = refs[:dp], refs[dp : dp + 3], refs[dp + 3 :]
    size = parts[0].shape[0]
    wait_all(
        start_all(
            [
                pltpu.make_async_copy(part, held.at[aligned(places[i], size)], sems.at[i])
                for i, part in enumerate(parts)
            ]
        )
    )
    small = held[:, 4 * own :]
    by_row[...] = small
    turned = jnp.transpose(small.astype(f32))
    by_column[...] = turned[:SMALL_ROWS]
    for block in range(dp):
        for piece in range(ctx):
            at = block * size + piece * share
            out_ref[block * share : (block + 1) * share, piece * own : (piece + 1) * own] = held[
                at : at + share, 3 * own : 4 * own
            ]


def unpack(places, parts, plan):
    dp, ctx, share, own, experts = plan
    size = parts[0].shape[0]
    width = dp * size
    return run(
        functools.partial(unpack_kernel, plan),
        "unpack",
        3,
        [places] + parts,
        [scalar] + [anywhere] * dp,
        [((width, LANES), bf16), ((SMALL_ROWS, width), f32), ((dp * share, ctx * own), bf16)],
        [inside] * 3,
        [pltpu.VMEM((width, 4 * own + LANES), bf16), pltpu.SemaphoreType.DMA((dp,))],
    )


def qkv_kernel(plan, scalars, small_ref, *refs):
    dp, ctx, rows, own, share = plan
    parts, tokens = refs[:dp], refs[dp : dp + ctx]
    qkv_ref, norm_ref, weight_ref, sems = refs[dp + ctx :]
    size = parts[0].shape[0]
    moves = [
        pltpu.make_async_copy(token, norm_ref.at[aligned(scalars[dp + i], rows)], sems.at[i])
        for i, token in enumerate(tokens)
    ] + [
        pltpu.make_async_copy(part, weight_ref.at[aligned(scalars[i], size)], sems.at[ctx + i])
        for i, part in enumerate(parts)
    ]
    start_all(moves)
    width = small_ref.shape[1]
    column = lax.broadcasted_iota(jnp.int32, (width, own), 1) + scalars[dp] * own
    source = lax.broadcasted_iota(jnp.int32, (width, own), 0)
    rank, inner = column // (2 * share), column % (2 * share)
    pair = small_ref[QV : QV + 2, :].astype(bf16)
    biases = []
    for part in range(2):
        picks = [
            (source == (rank + part * (width // (2 * share))) * share + inner - half * share)
            & (inner // share == half)
            for half in range(2)
        ]
        biases.append(
            sum(product(pair[half : half + 1], picks[half].astype(bf16)) for half in range(2))
        )
    bias = jnp.concatenate([biases[0], jnp.zeros_like(biases[0]), biases[1]], 1)
    gain, shift = small_ref[GAIN_ONE : GAIN_ONE + 1, :], small_ref[SHIFT_ONE : SHIFT_ONE + 1, :]
    wait_all(moves)
    tile = min(256, ctx * rows)
    for at in range(0, ctx * rows, tile):
        span = slice(at, at + tile)
        normed, _ = layer_stats(norm_ref[span, :].astype(f32))
        low = (normed * gain + shift).astype(bf16)
        norm_ref[span, :] = low
        qkv_ref[span, :] = (product(low, weight_ref[:, : 3 * own]) + bias).astype(bf16)


def make_qkv(scalars, small, parts, tokens, plan):
    dp, ctx, rows, own, share = plan
    width = tokens[0].shape[1]
    return run(
        functools.partial(qkv_kernel, plan),
        "norm_qkv",
        8,
        [scalars, small] + parts + tokens,
        [scalar, inside] + [anywhere] * (dp + ctx),
        [
            ((ctx * rows, 3 * own), bf16),
            ((ctx * rows, width), bf16),
            ((width, parts[0].shape[1]), bf16),
        ],
        [inside] * 3,
        [pltpu.SemaphoreType.DMA((dp + ctx,))],
    )


def score_parts(q_part, k_ref, column, step, block):
    scale = HEAD_DIM ** (-0.5)
    parts = []
    if step:
        parts.append(right_product(q_part, k_ref[0 : step * block, column]) * scale)
    diagonal = right_product(q_part, k_ref[step * block : (step + 1) * block, column]) * scale
    rows = lax.broadcasted_iota(jnp.int32, (block, block), 0)
    keys = lax.broadcasted_iota(jnp.int32, (block, block), 1)
    parts.append(jnp.where(keys <= rows, diagonal, -1e30))
    return parts


def softmax_of(parts):
    row_max = functools.reduce(jnp.maximum, [jnp.max(part, -1, keepdims=True) for part in parts])
    terms = [jnp.exp(part - row_max) for part in parts]
    total = functools.reduce(jnp.add, [jnp.sum(term, -1, keepdims=True) for term in terms])
    inverse = 1.0 / total
    return [term * inverse for term in terms]


def key_spans(step, block):
    spans = [slice(0, step * block)] if step else []
    return spans + [slice(step * block, (step + 1) * block)]


def attention_forward_kernel(heads, block, q_ref, k_ref, v_ref, out_ref):
    for head in range(heads):
        column = slice(head * HEAD_DIM, (head + 1) * HEAD_DIM)
        for step in range(q_ref.shape[0] // block):
            rows = slice(step * block, (step + 1) * block)
            probs = softmax_of(score_parts(q_ref[rows, column], k_ref, column, step, block))
            mixed = functools.reduce(
                jnp.add,
                [
                    product(prob.astype(bf16), v_ref[span, column])
                    for prob, span in zip(probs, key_spans(step, block))
                ],
            )
            out_ref[rows, column] = mixed.astype(bf16)


def attention_backward_kernel(
    heads, block, rows, scalars, q_ref, k_ref, v_ref, *refs
):
    scale = HEAD_DIM ** (-0.5)
    pieces, (dq_ref, dk_ref, dv_ref, held, k_acc, v_acc, sems) = refs[:-7], refs[-7:]
    step_now, lanes = pl.program_id(0), dq_ref.shape[1]

    @pl.when(step_now == 0)
    def _():
        wait_all(
            start_all(
                [
                    pltpu.make_async_copy(piece, held.at[aligned(scalars[i], rows)], sems.at[i])
                    for i, piece in enumerate(pieces)
                ]
            )
        )

    grads = held[...] if held.shape[1] == lanes else held[:, aligned(step_now, lanes)]
    for head in range(heads):
        column = slice(head * HEAD_DIM, (head + 1) * HEAD_DIM)
        for step in reversed(range(q_ref.shape[0] // block)):
            span_rows = slice(step * block, (step + 1) * block)
            spans = key_spans(step, block)
            q_part, o_part = q_ref[span_rows, column], grads[span_rows, column]
            probs = softmax_of(score_parts(q_part, k_ref, column, step, block))
            prob_grads = [right_product(o_part, v_ref[span, column]) for span in spans]
            delta = functools.reduce(
                jnp.add,
                [jnp.sum(p * g, -1, keepdims=True) for p, g in zip(probs, prob_grads)],
            )
            score_grads = [(p * (g - delta)).astype(bf16) for p, g in zip(probs, prob_grads)]
            q_grad = functools.reduce(
                jnp.add,
                [product(s, k_ref[span, column]) for s, span in zip(score_grads, spans)],
            )
            dq_ref[span_rows, column] = (q_grad * scale).astype(bf16)
            first = step == q_ref.shape[0] // block - 1
            for span, score_grad, prob in zip(spans, score_grads, probs):
                key_grad = left_product(score_grad, q_part)
                value_grad = left_product(prob.astype(bf16), o_part)
                k_acc[span, column] = key_grad if first else k_acc[span, column] + key_grad
                v_acc[span, column] = value_grad if first else v_acc[span, column] + value_grad
    dk_ref[...] = (k_acc[...] * scale).astype(bf16)
    dv_ref[...] = v_acc[...].astype(bf16)


def attention_plan(qkv, width):
    length = qkv.shape[0]
    heads = min(2, width // HEAD_DIM)
    block = min(256, length)
    lanes = heads * HEAD_DIM
    steps = width // lanes
    whole = lanes % LANES == 0
    joined = [qkv] * 3 if whole else [qkv[:, i * width : (i + 1) * width] for i in range(3)]

    def spec(part):
        first = part * steps if whole else 0
        return pl.BlockSpec((length, lanes), lambda step: (0, first + step))

    return length, heads, block, lanes, steps, spec, joined


def attention_forward(qkv, width):
    length, heads, block, lanes, steps, spec, joined = attention_plan(qkv, width)
    return run(
        functools.partial(attention_forward_kernel, heads, block),
        "attention_forward",
        10,
        joined,
        [spec(0), spec(1), spec(2)],
        [((length, width), bf16)],
        [spec(0)],
        [],
        (steps,),
    )[0]


def attention_backward(scalars, qkv, pieces, width):
    length, heads, block, lanes, steps, spec, joined = attention_plan(qkv, width)
    return run(
        functools.partial(attention_backward_kernel, heads, block, pieces[0].shape[0]),
        "attention_backward",
        18,
        [scalars] + joined + pieces,
        [scalar, spec(0), spec(1), spec(2)] + [anywhere] * len(pieces),
        [((length, width), bf16)] * 3,
        [spec(0)] * 3,
        [
            pltpu.VMEM((length, width), bf16),
            pltpu.VMEM((length, lanes), f32),
            pltpu.VMEM((length, lanes), f32),
            pltpu.SemaphoreType.DMA((len(pieces),)),
        ],
        (steps,),
    )


def hidden_kernel(ctx, scalars, small_ref, out_ref, tokens_ref, sort_ref, *refs):
    pieces, (hidden_ref, norm_ref, sorted_ref) = refs[:ctx], refs[ctx:]
    own = pieces[0].shape[1]
    hidden = tokens_ref[...].astype(f32) + (
        sum(
            product(piece[...], out_ref[aligned(scalars[i], own), :])
            for i, piece in enumerate(pieces)
        )
        + small_ref[OUT_BIAS : OUT_BIAS + 1, :]
    )
    hidden_ref[...] = hidden
    normed, _ = layer_stats(hidden)
    low = (
        normed * small_ref[GAIN_TWO : GAIN_TWO + 1, :] + small_ref[SHIFT_TWO : SHIFT_TWO + 1, :]
    ).astype(bf16)
    norm_ref[...] = low
    sorted_ref[...] = product(sort_ref[...], low).astype(bf16)


def make_hidden(scalars, small, full_out, tokens, sort, pieces):
    shape = tokens.shape
    return run(
        functools.partial(hidden_kernel, len(pieces)),
        "hidden",
        4,
        [scalars, small, full_out, tokens, sort] + pieces,
        [scalar] + [inside] * (4 + len(pieces)),
        [(shape, f32), (shape, bf16), (shape, bf16)],
        [inside] * 3,
        [],
    )


def mlp_kernel(plan, scalars, small_ref, by_column, *refs):
    dp, ctx, rows, start, count, expert, merged, last = plan
    base = 2 if expert == 1 else 0
    depth = dp // 2
    refs = list(refs)

    def take(number):
        taken = refs[:number]
        del refs[:number]
        return taken

    x_parts, g_parts = take(ctx), take(ctx)
    parts = take(dp if merged else 2 * dp)
    sums = take(6) if last else []
    if last:
        y_refs, gx_refs = take(ctx), take(ctx)
    else:
        y_ref, gx_ref, dots_out = take(3)
    (gb_ref,) = take(1)
    mine, other = take(1 if merged else 2), take(1 if merged else 2)
    up, down, x_all, x_turned, g_all, act_all, go_all, gu_all, up_grad, down_grad = take(10)
    pre_all, back_all = take(2)
    held = take(6) if last else take(2)
    in_sems, x_sems, out_sems, held_sems = take(4)
    width, hidden = up.shape
    up_rows, down_rows = width // dp, hidden // dp
    tile = min(256, hidden)
    tiles = [slice(at, at + tile) for at in range(0, hidden, tile)]
    total = ctx * count

    def loads(target, size, which):
        return [
            pltpu.make_async_copy(
                parts[i].at[base + which] if merged else parts[which * dp + i],
                target.at[aligned(scalars[i], size)],
                in_sems.at[which * dp + i],
            )
            for i in range(dp)
        ]

    def rows_of(block):
        return slice(block * count, (block + 1) * count)

    tokens = [
        pltpu.make_async_copy(
            part.at[start : start + count], x_all.at[rows_of(i)], x_sems.at[i]
        )
        for i, part in enumerate(x_parts)
    ]
    grads = [
        pltpu.make_async_copy(
            part.at[start : start + count], g_all.at[rows_of(i)], x_sems.at[ctx + i]
        )
        for i, part in enumerate(g_parts)
    ]
    ups, downs = loads(up, up_rows, 0), loads(down, down_rows, 1)
    start_all(tokens + ups + grads + downs)
    gathered = [
        pltpu.make_async_copy(ref, held[i], held_sems.at[i]) for i, ref in enumerate(sums)
    ]
    start_all(gathered)
    wait_all(tokens)
    logits = product(x_all[...], small_ref[...])
    route_zero, route_one = logits[:, ROUTER : ROUTER + 1], logits[:, ROUTER + 1 : ROUTER + 2]
    mix_zero, mix_one = logits[:, MIX : MIX + 1], logits[:, MIX + 1 : MIX + 2]
    if expert is None:
        mask = None
        coef = sigmoid_pair(mix_zero, mix_one)
    else:
        place = lax.broadcasted_iota(jnp.int32, (count, 1), 0) + start
        firsts = [place < scalars[dp + block] for block in range(ctx)]
        masks = [(first if expert == 0 else ~first).astype(f32) for first in firsts]
        mask = jnp.concatenate(masks, 0)
        gate = (
            sigmoid_pair(route_zero, route_one)
            if expert == 0
            else sigmoid_pair(route_one, route_zero)
        )
        coef = sigmoid_pair(mix_one, mix_zero) * gate * mask
    x_turned[...] = jnp.transpose(x_all[...])
    wait_all(grads)
    go_all[...] = (g_all[...].astype(f32) * coef).astype(bf16)
    wait_all(ups)

    piece = 64 if total % 64 == 0 else 16

    def activate(cut):
        bias = by_column[:, cut]
        column_sum = jnp.zeros((8, tile), f32)
        for at in range(0, total, piece):
            span = slice(at, at + piece)
            pre = pre_all[span, :] + bias
            square = pre * pre
            bend = jnp.tanh((ROOT * pre) * (1.0 + CUBE * square))
            half = 0.5 + 0.5 * bend
            act_all[span, cut] = (pre * half).astype(bf16)
            slope = half + ((0.5 * ROOT) * pre) * (1.0 - bend * bend) * (
                1.0 + (3.0 * CUBE) * square
            )
            grad_up = (back_all[span, :] * slope).astype(bf16)
            gu_all[span, cut] = grad_up
            column_sum = column_sum + jnp.sum(
                grad_up.astype(f32).reshape(piece // 8, 8, tile), 0
            )
        gb_ref[:, cut] = jnp.sum(column_sum, 0, keepdims=True)

    for number, cut in enumerate(tiles):
        pre_all[...] = product(x_all[...], up[:, cut])
        if number == 0:
            wait_all(downs)
        back_all[...] = right_product(go_all[...], down[cut, :])
        activate(cut)
        down_grad[cut, :] = left_product(act_all[:, cut], go_all[...]).astype(bf16)
        up_grad[:, cut] = product(x_turned[...], gu_all[:, cut]).astype(bf16)

    def stores(grad, size, which):
        targets = [
            (mine[0].at[i, which] if merged else mine[which].at[i])
            if i < depth
            else (other[0].at[i - depth, which] if merged else other[which].at[i - depth])
            for i in range(dp)
        ]
        return [
            pltpu.make_async_copy(
                grad.at[aligned(scalars[i], size)], target, out_sems.at[which * dp + i]
            )
            for i, target in enumerate(targets)
        ]

    saved = start_all(stores(up_grad, up_rows, 0) + stores(down_grad, down_rows, 1))
    wait_all(gathered)
    sums_sent = []
    for block in range(ctx):
        span = rows_of(block)
        out = product(act_all[span, :], down[...])
        grad_x = right_product(gu_all[span, :], up[...])
        dot = jnp.sum(g_all[span, :].astype(f32) * out, -1, keepdims=True)
        out = out * coef[span]
        if not last:
            held[0][span, :], held[1][span, :] = out, grad_x
            for number, target in enumerate((y_ref, gx_ref)):
                copy = pltpu.make_async_copy(
                    held[number].at[span], target.at[span], held_sems.at[2 * block + number]
                )
                copy.start()
                sums_sent.append(copy)
            dots_out[span, :] = dot if mask is None else dot * mask[span]
            continue
        y_dense, gx_dense, dots_dense, y_first, gx_first, dots_first = held
        whole = slice(block * rows, (block + 1) * rows)
        sets = ((y_dense, y_first, out, y_refs), (gx_dense, gx_first, grad_x, gx_refs))
        for dense, first, own, target in sets:
            early = dense[whole, :][:start] + first[span, :][:start]
            middle = dense[whole, :][start:count] + (first[span, :][start:] + own[: count - start])
            late = dense[whole, :][count:] + own[count - start :]
            target[block][0:start, 0:width] = early.astype(bf16)
            target[block][start:count, 0:width] = middle.astype(bf16)
            target[block][count:rows, 0:width] = late.astype(bf16)
        own_dot = dot * mask[span]
        first_dot = dots_first[span, :]
        moe = jnp.concatenate(
            [
                first_dot[:start],
                first_dot[start:] + own_dot[: count - start],
                own_dot[count - start :],
            ],
            0,
        )
        lane = lax.broadcasted_iota(jnp.int32, (rows, LANES), 1)
        both = jnp.where(lane % 2 == 0, dots_dense[whole, :], moe)
        high, middle, low = three_parts(both)
        extra = jnp.where(lane < 2, high.astype(f32), jnp.where(lane < 4, middle.astype(f32), low.astype(f32)))
        gx_refs[block][:, width:] = jnp.where(lane < 6, extra, 0.0).astype(bf16)
    wait_all(saved + sums_sent)


def mlp(scalars, small, bias, x, g, parts, expert, merged, sums):
    ctx = len(x)
    rows, width = x[0].shape
    dp = len(parts) if merged else len(parts) // 2
    depth = dp // 2
    hidden = bias.shape[1]
    count = rows if expert is None else rows * 5 // 8
    start = 0 if expert in (None, 0) else rows - count
    total = ctx * count
    last = expert == 1
    if merged:
        halves = [((depth, 2) + parts[0].shape[1:], bf16)]
    else:
        halves = [((depth,) + parts[0].shape, bf16), ((depth,) + parts[dp].shape, bf16)]
    if last:
        outs = [((rows, width), bf16)] * ctx + [((rows, width + LANES), bf16)] * ctx
    else:
        outs = [((total, width), f32), ((total, width), f32), ((total, 1), f32)]
    outs = outs + [((1, hidden), f32)] + halves + halves
    small_outs = len(outs) - 2 * len(halves)
    held = [pltpu.VMEM(ref.shape, f32) for ref in sums] or [pltpu.VMEM((total, width), f32)] * 2
    tile = min(256, hidden)
    return run(
        functools.partial(mlp_kernel, (dp, ctx, rows, start, count, expert, merged, last)),
        "mlp",
        20 if total % LANES == 0 and expert is None else 18,
        [scalars, small, bias] + x + g + parts + sums,
        [scalar, inside, inside] + [anywhere] * (2 * ctx + len(parts) + len(sums)),
        outs,
        ([] if last else [anywhere] * 2)
        + [inside] * (small_outs if last else small_outs - 2)
        + [anywhere] * (2 * len(halves)),
        [
            pltpu.VMEM((width, hidden), bf16),
            pltpu.VMEM((hidden, width), bf16),
            pltpu.VMEM((total, width), bf16),
            pltpu.VMEM((width, total), bf16),
            pltpu.VMEM((total, width), bf16),
            pltpu.VMEM((total, hidden), bf16),
            pltpu.VMEM((total, width), bf16),
            pltpu.VMEM((total, hidden), bf16),
            pltpu.VMEM((width, hidden), bf16),
            pltpu.VMEM((hidden, width), bf16),
            pltpu.VMEM((total, tile), f32),
            pltpu.VMEM((total, tile), f32),
        ]
        + held
        + [
            pltpu.SemaphoreType.DMA((2 * dp,)),
            pltpu.SemaphoreType.DMA((2 * ctx,)),
            pltpu.SemaphoreType.DMA((2 * dp,)),
            pltpu.SemaphoreType.DMA((max(2 * ctx, len(sums)),)),
        ],
    )


def middle_kernel(
    ctx, scalars, by_row, by_column, out_ref, hidden_ref, norm_ref, g_ref, first_ref, unsort_ref, *refs
):
    gx, pieces = refs[:ctx], refs[ctx : 2 * ctx]
    outs = refs[2 * ctx :]
    base_ref, grad_hidden_ref, rows_ref = outs[:3]
    out_grads, grad_pieces = outs[3 : 3 + ctx], outs[3 + ctx : 3 + 2 * ctx]
    out_all, sems = outs[3 + 2 * ctx :]
    rows, width = hidden_ref.shape
    own = pieces[0].shape[1]
    unsort = unsort_ref[...]
    gathered = sum(product(unsort, piece[...]) for piece in gx)
    grad_norm = gathered[:, :width]
    extra = gathered[:, width:]
    dense_dot = extra[:, 0:1] + (extra[:, 2:3] + extra[:, 4:5])
    moe_dot = extra[:, 1:2] + (extra[:, 3:4] + extra[:, 5:6])
    grad_out = g_ref[...].astype(f32)
    first = first_ref[...]
    down_bias = by_column[DOWN_BIAS : DOWN_BIAS + 1, :]
    moe_bias = jnp.where(
        first > 0.5,
        by_column[EXPERT_DOWN : EXPERT_DOWN + 1, :],
        by_column[EXPERT_DOWN + 1 : EXPERT_DOWN + 2, :],
    )
    dense_dot = dense_dot + jnp.sum(grad_out * down_bias, -1, keepdims=True)
    moe_dot = moe_dot + jnp.sum(grad_out * moe_bias, -1, keepdims=True)
    norm = norm_ref[...]
    logits = product(norm, by_row[...])
    route = [
        sigmoid_pair(logits[:, a : a + 1], logits[:, b : b + 1])
        for a, b in ((ROUTER, ROUTER + 1), (ROUTER + 1, ROUTER))
    ]
    mix = [
        sigmoid_pair(logits[:, a : a + 1], logits[:, b : b + 1])
        for a, b in ((MIX, MIX + 1), (MIX + 1, MIX))
    ]
    hot = [first, 1.0 - first]
    gate = route[0] * hot[0] + route[1] * hot[1]
    branch = mix[1] * gate
    hidden = hidden_ref[...]
    base_ref[...] = hidden + (mix[0] * down_bias + branch * moe_bias)
    grad_mix = [dense_dot, moe_dot * gate]
    mean_mix = mix[0] * grad_mix[0] + mix[1] * grad_mix[1]
    grad_gate = moe_dot * mix[1]
    grad_route = [hot[0] * grad_gate, hot[1] * grad_gate]
    mean_route = route[0] * grad_route[0] + route[1] * grad_route[1]
    lane = lax.broadcasted_iota(jnp.int32, (rows, LANES), 1)
    columns = [route[i] * (grad_route[i] - mean_route) for i in range(2)]
    columns += [mix[i] * (grad_mix[i] - mean_mix) for i in range(2)]
    logit_grads = jnp.zeros((rows, LANES), f32)
    for i, column in enumerate(columns):
        logit_grads = jnp.where((lane % 4 == i) & (lane < 12), column, logit_grads)
    high, middle, rest = [part.astype(f32) for part in three_parts(logit_grads)]
    split = jnp.where(lane < 4, high, jnp.where(lane < 8, middle, rest)).astype(bf16)
    grad_norm = grad_norm + right_product(split, by_row[...])
    small_grads = left_product(split, norm)
    small_grads = small_grads[0:4] + (small_grads[4:8] + small_grads[8:12])
    grad_dense = (grad_out * mix[0]).astype(bf16).astype(f32)
    grad_moe = (grad_out * branch).astype(bf16).astype(f32)
    normed, inverse = layer_stats(hidden)
    gain = by_column[GAIN_TWO : GAIN_TWO + 1, :]
    grad_hidden = grad_out + norm_back(grad_norm, normed, inverse, gain)
    grad_hidden_ref[...] = grad_hidden
    low = grad_hidden.astype(bf16)

    def total(values):
        return jnp.sum(values, 0, keepdims=True)

    sums = [
        total(low.astype(f32)),
        total(grad_norm * normed),
        total(grad_norm),
        total(grad_dense),
        total(grad_moe * hot[0]),
        total(grad_moe * hot[1]),
    ]
    rows_ref[...] = jnp.concatenate(sums + [small_grads, jnp.zeros((6, width), f32)], 0)
    for i, (piece, target) in enumerate(zip(pieces, grad_pieces)):
        span = aligned(scalars[i], own)
        target[...] = right_product(low, out_ref[span, :]).astype(bf16)
        part = left_product(piece[...], low).astype(bf16)
        share = out_all.shape[3]
        many = own // (ctx * share)
        for c in range(ctx):
            columns = part[:, c * own : (c + 1) * own].reshape(many, ctx, share, own)
            out_all[aligned(scalars[i], many), :, c] = columns
    wait_all(
        start_all(
            [
                pltpu.make_async_copy(out_all.at[:, scalars[i]], target, sems.at[i])
                for i, target in enumerate(out_grads)
            ]
        )
    )


def make_middle(
    scalars, by_row, by_column, full_out, hidden, norm, g, first, unsort, gx, pieces, dp
):
    ctx = len(gx)
    rows, width = hidden.shape
    own = pieces[0].shape[1]
    return run(
        functools.partial(middle_kernel, ctx),
        "middle",
        11,
        [scalars, by_row, by_column, full_out, hidden, norm, g, first, unsort] + gx + pieces,
        [scalar] + [inside] * (8 + 2 * ctx),
        [
            ((rows, width), f32),
            ((rows, width), f32),
            ((16, width), f32),
        ]
        + [((dp, ctx, width // (dp * ctx), own), bf16)] * ctx
        + [((rows, own), bf16)] * ctx,
        [inside] * 3 + [anywhere] * ctx + [inside] * ctx,
        [
            pltpu.VMEM((dp, ctx, ctx, width // (dp * ctx), own), bf16),
            pltpu.SemaphoreType.DMA((ctx,)),
        ],
    )


def qkv_back_kernel(plan, scalars, norm_ref, dq_ref, dk_ref, dv_ref, weight_ref, *refs):
    dp, ctx, rows, own = plan
    depth = dp // 2
    out_pieces, gn_refs = refs[:ctx], refs[ctx : 2 * ctx]
    mine, other, bias_ref, grad, weight_grad, gn, sems, gn_sems = refs[2 * ctx :]
    width = norm_ref.shape[1]
    size = width // dp
    for part, ref in enumerate((dq_ref, dk_ref, dv_ref)):
        grad[:, part * own : (part + 1) * own] = ref[...]
    tile = min(256, ctx * rows)
    weight = weight_ref[:, : 3 * own]
    for at in range(0, ctx * rows, tile):
        gn[at : at + tile, :] = right_product(grad[at : at + tile, :], weight).astype(bf16)
    sent = start_all(
        [
            pltpu.make_async_copy(gn.at[aligned(scalars[dp + i], rows)], ref, gn_sems.at[i])
            for i, ref in enumerate(gn_refs)
        ]
    )
    step = min(256, width)
    for at in range(0, width, step):
        weight_grad[at : at + step, : 3 * own] = left_product(
            norm_ref[:, at : at + step], grad[...]
        ).astype(bf16)
    weight_grad[:, 3 * own :] = sum(piece[...].astype(f32) for piece in out_pieces).astype(bf16)
    saved = start_all(
        [
            pltpu.make_async_copy(
                weight_grad.at[aligned(scalars[i], size)],
                mine.at[i] if i < depth else other.at[i - depth],
                sems.at[i],
            )
            for i in range(dp)
        ]
    )
    bias = jnp.sum(grad[...].astype(f32), 0, keepdims=True)
    here = lax.broadcasted_iota(jnp.int32, (1, width), 1) // own == scalars[dp]
    for row, at in enumerate((0, 2 * own)):
        spread = jnp.concatenate([bias[:, at : at + own]] * ctx, 1)
        bias_ref[row : row + 1, :] = jnp.where(here, spread, 0.0)
    wait_all(sent + saved)


def qkv_back(scalars, norm, grads, weight, out_pieces, plan):
    dp, ctx, rows, own = plan
    length, width = norm.shape
    half = ((dp // 2, width // dp, 4 * own), bf16)
    return run(
        functools.partial(qkv_back_kernel, plan),
        "qkv_back",
        8,
        [scalars, norm] + list(grads) + [weight] + list(out_pieces),
        [scalar] + [inside] * (5 + ctx),
        [((rows, width), bf16)] * ctx + [half, half, ((2, width), f32)],
        [anywhere] * (ctx + 2) + [inside],
        [
            pltpu.VMEM((length, 3 * own), bf16),
            pltpu.VMEM((width, 4 * own), bf16),
            pltpu.VMEM((length, width), bf16),
            pltpu.SemaphoreType.DMA((dp,)),
            pltpu.SemaphoreType.DMA((ctx,)),
        ],
    )


def final_kernel(ctx, order, by_column, tokens_ref, grad_hidden_ref, *refs):
    pieces, (grad_ref, rows_ref) = refs[:ctx], refs[ctx:]
    grad_norm = sum(piece[...].astype(f32) for piece in pieces)
    normed, inverse = layer_stats(tokens_ref[...].astype(f32))
    gain = by_column[GAIN_ONE : GAIN_ONE + 1, :]
    grad_ref[...] = grad_hidden_ref[...] + norm_back(grad_norm, normed, inverse, gain)
    rows_ref[0:1, :] = jnp.sum(grad_norm * normed, 0, keepdims=True)
    rows_ref[1:2, :] = jnp.sum(grad_norm, 0, keepdims=True)


def make_final(order, by_column, tokens, grad_hidden, pieces):
    return run(
        functools.partial(final_kernel, len(pieces)),
        "final",
        4,
        [order, by_column, tokens, grad_hidden] + pieces,
        [scalar] + [inside] * (3 + len(pieces)),
        [(tokens.shape, f32), ((2, tokens.shape[1]), f32)],
        [inside] * 2,
        [],
    )


def result_kernel(ctx, base_ref, unsort_ref, *refs):
    pieces, (out_ref,) = refs[:ctx], refs[ctx:]
    unsort = unsort_ref[...]
    out_ref[...] = base_ref[...] + sum(product(unsort, piece[...]) for piece in pieces)


def make_result(base, unsort, pieces):
    return run(
        functools.partial(result_kernel, len(pieces)),
        "result",
        3.5,
        [base, unsort] + pieces,
        [inside] * (2 + len(pieces)),
        [(base.shape, f32)],
        [inside],
        [],
    )[0]


def layer(
    dp,
    ctx,
    tokens,
    cotangent,
    routes,
    ln1_gain,
    ln1_bias,
    qkv_weight,
    qv_bias,
    out_weight,
    out_bias,
    ln2_gain,
    ln2_bias,
    up_weight,
    up_bias,
    down_weight,
    down_bias,
    router_weight,
    mix_weight,
    expert_up,
    expert_up_bias,
    expert_down,
    expert_down_bias,
):
    rows, width = tokens.shape[0] * tokens.shape[1], tokens.shape[2]
    experts, share, hidden = expert_up.shape
    own_hidden = hidden // ctx
    own_width = width // ctx
    unit = hidden // (dp * ctx)
    me = lax.axis_index("ctx")
    place_dp = lax.axis_index("dp")
    core = place_dp % 2
    depth = dp // 2
    shifts = range(1, ctx)
    ring_pairs = [(i, (i + 2) % dp) for i in range(dp)]
    core_pairs = [(i, i ^ 1) for i in range(dp)]
    places = jnp.stack(
        [
            ((place_dp // 2 + depth - t) % depth) * 2 + c
            for c in (core, 1 - core)
            for t in range(depth)
        ]
    ).astype(jnp.int32)
    peers = jnp.stack([me ^ s for s in range(ctx)]).astype(jnp.int32)

    def swap(array, shift):
        return lax.ppermute(array, "ctx", [(i, i ^ shift) for i in range(ctx)])

    def gather_ctx(array):
        return [array] + [swap(array, s) for s in shifts]

    def trade(pieces):
        return [pieces[0]] + [swap(pieces[s], s) for s in shifts]

    def by_peer(pieces):
        return [lax.dynamic_index_in_dim(pieces, me ^ s, 0, keepdims=False) for s in range(ctx)]

    def natural(pieces):
        whole = jnp.zeros((ctx,) + pieces[0].shape, pieces[0].dtype)
        for s, piece in enumerate(pieces):
            whole = lax.dynamic_update_slice_in_dim(whole, piece[None], me ^ s, 0)
        return whole

    def ring(array):
        return lax.ppermute(array, "dp", ring_pairs)

    def swap_core(array):
        return lax.ppermute(array, "dp", core_pairs)

    def sync(*trees):
        return lax.optimization_barrier(trees)

    class Rings:
        def __init__(self, arrays):
            self.parts = [list(arrays)]

        def move(self):
            self.parts.append([ring(array) for array in self.parts[-1]])

        def rest(self):
            while len(self.parts) < depth:
                self.move()

        def pieces(self, others, which):
            return [part[which] for part in self.parts] + [part[which] for part in others]

    def swap_cores(part):
        return [swap_core(array) for array in part]

    class Scatter:
        def __init__(self, *halves):
            half = len(halves) // 2
            self.mine, self.step = list(halves[:half]), 0
            self.got = [swap_core(other) for other in halves[half:]]
            self.arrived = self.sent = None

        def receive(self, others):
            if self.sent is None:
                self.got, others = sync(self.got, others)
            else:
                self.arrived, others = sync([ring(part) for part in self.sent], others)
            return others

        def add(self):
            self.step += 1
            at = self.step % depth
            parts = [m[at].astype(f32) + g[at].astype(f32) for m, g in zip(self.mine, self.got)]
            if self.arrived is not None:
                parts = [p + c.astype(f32) for p, c in zip(parts, self.arrived)]
            self.sent = [part.astype(bf16) if at else part for part in parts]

        def move(self, others):
            others = self.receive(others)
            self.add()
            return others

        def close(self):
            self.add()
            while self.step < depth:
                self.arrived = [ring(part) for part in self.sent]
                self.add()

    def pin(value, *sums):
        value, sent = sync(value, [one.sent for one in sums])
        for one, parts in zip(sums, sent):
            one.sent = parts
        return value

    def pair(sums):
        return sums if len(sums) == 2 else [sums[0][0], sums[0][1]]

    tokens = tokens.reshape(rows, width)
    cotangent = cotangent.reshape(rows, width)
    first_hot = routes.reshape(rows) == 0
    first_float = first_hot.astype(f32)
    first_count = jnp.sum(first_float)

    def column(vector):
        return vector.reshape(-1, share).T

    def bias_column(vector):
        return jnp.pad(vector.reshape(unit, 1), ((0, ctx * share - unit), (0, 0)))

    small = jnp.concatenate(
        [
            jnp.concatenate([router_weight, mix_weight] * 3, 1),
            column(ln1_gain),
            column(ln1_bias),
            column(qv_bias),
            column(out_bias),
            column(ln2_gain),
            column(ln2_bias),
            column(down_bias),
            expert_down_bias.T,
            jnp.broadcast_to(first_count.astype(bf16), (share, 1)),
        ],
        1,
    )
    small = jnp.pad(small, ((0, 0), (0, LANES - small.shape[1])))
    qkv_cut = qkv_weight.reshape(share, 3, ctx, own_width).transpose(2, 0, 1, 3)
    first_cut = jnp.concatenate(
        [
            qkv_cut.reshape(ctx, share, 3 * own_width),
            jnp.broadcast_to(small[None], (ctx, share, LANES)),
        ],
        -1,
    )
    ups = jnp.concatenate([up_weight[None], expert_up], 0)
    ups_cut = ups.reshape(experts + 1, share, dp, ctx, unit).transpose(3, 0, 1, 2, 4)
    ups_sent = by_peer(ups_cut.reshape(ctx, experts + 1, share, own_hidden))
    first_rows, ups_sent = sync(trade(by_peer(first_cut)), ups_sent)
    first_rows = natural(first_rows).reshape(ctx * share, 3 * own_width + LANES)
    qkv_rows = first_rows[:, : 3 * own_width]
    small_rows = first_rows[:, 3 * own_width :]
    counts = small_rows[::share, COUNT]
    bias_lanes = jnp.concatenate(
        [bias_column(up_bias)] + [bias_column(expert_up_bias[e]) for e in range(experts)], 1
    )
    lane = jnp.arange(LANES)[None, :]
    bias_lanes = jnp.pad(bias_lanes, ((0, 0), (UP_BIAS, LANES - UP_BIAS - bias_lanes.shape[1])))
    small_rows = jnp.where((lane >= UP_BIAS) & (lane < UP_BIAS + experts + 1), bias_lanes, small_rows)
    out_rows = out_weight.reshape(share, ctx, own_width).transpose(1, 0, 2)
    out_rows = out_rows.reshape(ctx * share, own_width)
    first = Rings([jnp.concatenate([qkv_rows, out_rows, small_rows], 1)])

    first.move()
    first_others = [swap_cores(first.parts[0])]
    token_parts = gather_ctx(tokens)
    first.parts[1], first_others[0] = sync(first.parts[1], first_others[0])
    first.move()
    first_others.append(swap_cores(first.parts[1]))
    token_parts, first.parts[2], first_others[1], ups_sent = sync(
        token_parts, first.parts[2], first_others[1], ups_sent
    )
    first.rest()
    first_others += [swap_cores(part) for part in first.parts[2:-1]]
    ups_rows, first.parts[-1], first_others = sync(trade(ups_sent), first.parts[-1], first_others)
    ups_rows = natural(ups_rows).transpose(1, 0, 2, 3)
    ups_rows = ups_rows.reshape(experts + 1, ctx * share, own_hidden)
    downs = [down_weight] + [expert_down[e] for e in range(experts)]
    merged = downs[0].shape == ups_rows.shape[1:]
    if merged:
        dense_weights = [jnp.stack([ups_rows[0], downs[0]])]
        expert_weights = [jnp.stack([ups_rows[1], downs[1], ups_rows[2], downs[2]])]
    else:
        dense_weights = [ups_rows[0], downs[0]]
        expert_weights = [ups_rows[1], downs[1], ups_rows[2], downs[2]]
    dense_ring = Rings(dense_weights)
    dense_ring.move()
    first_others.append(swap_cores(first.parts[-1]))
    first_parts = first.pieces(first_others, 0)
    plan = (dp, ctx, share, own_width, experts)
    by_row, by_column, out_own = unpack(places, first_parts, plan)
    expert_weights, by_row = sync(expert_weights, by_row)
    expert_ring = Rings(expert_weights)
    expert_ring.move()
    out_pieces = gather_ctx(out_own)

    order = jnp.arange(rows).astype(f32)
    counted = jnp.cumsum(first_float)
    place = jnp.where(first_hot, counted - 1.0, first_count + order - counted)
    unsort = (place[:, None] == order[None, :]).astype(bf16)
    sort = (place[None, :] == order[:, None]).astype(bf16)
    sorted_grad = product(sort, cotangent).astype(bf16)

    scalars = jnp.concatenate([places, peers])
    qkv, attn_in, own_qkv = make_qkv(
        scalars, by_column, first_parts, token_parts, (dp, ctx, rows, own_width, share)
    )
    qkv, dense_ring.parts[1] = sync(qkv, dense_ring.parts[1])
    dense_ring.move()
    attended_heads = attention_forward(qkv, own_width)
    attended_heads, out_pieces = sync(attended_heads, out_pieces)
    attended = trade(by_peer(attended_heads.reshape(ctx, rows, own_width)))
    full_out = natural(out_pieces).reshape(ctx, dp, share, width).transpose(1, 0, 2, 3)
    full_out = full_out.reshape(width, width)
    hidden_state, ffn_in, sorted_in = make_hidden(
        peers, by_column, full_out, tokens, sort, attended
    )
    sorted_in, expert_ring.parts[1] = sync(sorted_in, expert_ring.parts[1])
    expert_ring.move()
    ffn_parts = gather_ctx(sorted_in)
    late_columns, late_counts, _ = sync(by_column, counts, sorted_in)
    row_counts = jnp.stack([late_counts[me ^ s] for s in range(ctx)]).astype(jnp.int32)
    mlp_scalars = jnp.concatenate([places, row_counts])
    up_biases = late_columns[UP_BIAS : UP_BIAS + experts + 1]
    up_biases = up_biases.reshape(experts + 1, dp, -1)[:, :, :unit].reshape(experts + 1, own_hidden)

    mlp_scalars = gate(mlp_scalars, *dense_ring.parts[2])
    ffn_parts, dense_ring.parts[2], sorted_grad, up_biases, mlp_scalars = sync(
        ffn_parts, dense_ring.parts[2], sorted_grad, up_biases, mlp_scalars
    )
    dense_ring.rest()
    grad_parts = [sorted_grad] + [swap(sorted_grad, s) for s in shifts[:2]]
    expert_ring.parts[2], late_grad = sync(expert_ring.parts[2], sorted_grad)
    expert_ring.rest()
    grad_parts += [swap(late_grad, s) for s in shifts[2:]]
    grad_parts, dense_ring.parts = sync(grad_parts, dense_ring.parts)
    dense_others = [swap_cores(part) for part in dense_ring.parts]
    dense_others, early = sync(dense_others, expert_ring.parts[:-1])
    expert_others = [swap_cores(part) for part in early]

    def run_mlp(which, held, parts, sums):
        return mlp(
            held,
            by_row,
            up_biases[which][None],
            ffn_parts,
            grad_parts,
            parts,
            which - 1 if which else None,
            merged,
            list(sums),
        )

    def weights_of(rings, others, first_array):
        if merged:
            return rings.pieces(others, 0)
        return rings.pieces(others, first_array) + rings.pieces(others, first_array + 1)

    dense = run_mlp(0, mlp_scalars, weights_of(dense_ring, dense_others, 0), [])
    sum_dense = Scatter(*dense[4:])
    expert_last, expert_others, gb_dense = sync(expert_ring.parts[-1], expert_others, dense[3])
    expert_ring.parts[-1] = expert_last
    expert_others = expert_others + [swap_cores(expert_last)]
    gb_dense = sum_dense.move(gb_dense)
    first_mlp = run_mlp(
        1,
        pin(gate(mlp_scalars), sum_dense),
        weights_of(expert_ring, expert_others, 0),
        [],
    )
    sum_first = Scatter(*first_mlp[4:])
    gb_first = sum_dense.move(first_mlp[3])
    second_mlp = run_mlp(
        2,
        pin(mlp_scalars, sum_dense),
        weights_of(expert_ring, expert_others, 2),
        dense[:3] + first_mlp[:3],
    )
    gb_second = sum_first.move(sum_dense.move(second_mlp[2 * ctx]))
    grad_sent = list(second_mlp[ctx : 2 * ctx])
    grad_pieces = trade(grad_sent[:3] + pin(grad_sent[3:], sum_dense, sum_first))
    grad_pieces, halves, result_sent = sync(
        grad_pieces, second_mlp[2 * ctx + 1 :], second_mlp[:ctx]
    )
    grad_pieces = sum_first.move(sum_dense.receive(grad_pieces))
    sum_second = Scatter(*halves)
    result_pieces = [result_sent[0]] + [swap(result_sent[s], s) for s in shifts[:2]]

    middle_peers, sum_dense.arrived = sync(peers, sum_dense.arrived)
    base, grad_hidden, middle_rows, *rest = make_middle(
        pin(middle_peers, sum_first),
        by_row,
        by_column,
        full_out,
        hidden_state,
        ffn_in,
        cotangent,
        first_float[:, None],
        unsort,
        grad_pieces,
        attended,
        dp,
    )
    out_sent, att_sent = rest[:ctx], rest[ctx:]
    result_pieces, att_sent = sync(result_pieces, att_sent)
    att_grads, out_sent = sync(trade(att_sent), out_sent)
    out_sent = [piece.reshape(width, own_width) for piece in out_sent]
    out_pieces = trade(out_sent)
    middle_rows = sum_second.move(sum_first.move(middle_rows))

    grad_heads = attention_backward(pin(peers, sum_first, sum_second), qkv, att_grads, own_width)
    grad_heads = sum_second.move(sum_first.receive(grad_heads))
    back_scalars, sum_first.arrived = sync(pin(scalars, sum_second), sum_first.arrived)
    *norm_grads, last_mine, last_other, grad_b_qkv = qkv_back(
        back_scalars,
        attn_in,
        grad_heads,
        own_qkv,
        out_pieces,
        (dp, ctx, rows, own_width),
    )
    sum_last = Scatter(last_mine, last_other)
    norm_pieces = [norm_grads[0]] + [swap(norm_grads[s], s) for s in shifts[:2]]
    late_pieces = [swap(norm_grads[s], s) for s in shifts[2:]]
    grad_b_qkv = sum_last.move(grad_b_qkv)
    norm_pieces[1] = sum_last.move(sum_second.move(norm_pieces[1]))
    small_sources = (grad_b_qkv, middle_rows, gb_dense, gb_first, gb_second)
    norm_pieces, small_sources, sum_dense.arrived, sum_first.arrived = pin(
        (norm_pieces, small_sources, sum_dense.arrived, sum_first.arrived), sum_last, sum_second
    )
    grad_b_qkv, middle_rows, gb_dense, gb_first, gb_second = small_sources
    norm_pieces += late_pieces
    sum_dense.close()
    sum_first.close()

    def cut_columns(parts):
        joined = jnp.concatenate([part.astype(bf16) for part in parts], 1)
        return by_peer(joined.reshape(ctx, share, joined.shape[1]))

    def from_columns(pieces, at, size, groups):
        whole = natural([piece[:, at : at + size] for piece in pieces])
        whole = whole.reshape(ctx, share, groups, size // groups).transpose(1, 2, 0, 3)
        return whole.reshape(share, ctx * size).astype(f32)

    norm_pieces, result_sent = sync(norm_pieces, result_sent)
    result_pieces = result_pieces + [swap(result_sent[s], s) for s in shifts[2:]]
    grad_inputs, final_rows = make_final(peers, by_column, tokens, grad_hidden, norm_pieces)
    final_rows = pin(sum_last.move(final_rows), sum_last)

    small_rows = jnp.concatenate(
        [middle_rows[:10], final_rows, grad_b_qkv, jnp.zeros((2, width), f32)], 0
    )
    small_rows, result_pieces = sync(small_rows, result_pieces)
    small_pieces = gather_ctx(small_rows)

    small_pieces = sum_last.receive(sum_second.receive(small_pieces))
    sum_last.close()
    (last_sum,) = sum_last.sent
    qkv_part, out_sums = last_sum[:, : 3 * own_width], last_sum[:, 3 * own_width :]
    out_sums = out_sums.reshape(ctx, share, own_width).transpose(1, 0, 2).reshape(share, width)
    late_pieces = trade(cut_columns([qkv_part]))
    up_rows = jnp.concatenate([gb_dense, gb_first, gb_second, jnp.zeros((5, own_hidden), f32)], 0)
    up_rows = jnp.pad(up_rows, ((0, 0), (0, width - own_hidden)))
    small_sum = jnp.concatenate([sum(small_pieces), up_rows], 0)
    small_sum, late_pieces = sync(small_sum + swap_core(small_sum), late_pieces)
    pairs = [[(i, (i + 2 * t) % dp) for i in range(dp)] for t in range(depth)]
    small_sum = sum(
        [small_sum] + [lax.ppermute(small_sum, "dp", pairs[t]) for t in range(1, depth)]
    )
    sum_second.close()
    sums = [pair(one.sent) for one in (sum_dense, sum_first, sum_second)]
    early_sent, late_pieces = sync(cut_columns([one[0] for one in sums]), late_pieces)
    early_pieces = trade(early_sent)
    result = make_result(base, unsort, result_pieces)
    up_grads = [
        from_columns(early_pieces, which * own_hidden, own_hidden, dp)
        for which in range(experts + 1)
    ]
    qkv_grad = from_columns(late_pieces, 0, 3 * own_width, 3)
    down_sums = [one[1] for one in sums]
    owner = place_dp * ctx + me
    own = lax.dynamic_slice(small_sum, (0, owner * share), (12, share))
    own_qv = lax.dynamic_slice(small_sum[12:14].reshape(-1), (owner * 2 * share,), (2 * share,))
    own_up = lax.dynamic_slice(small_sum, (16, place_dp * unit), (3, unit))
    return (
        result[None],
        grad_inputs[None],
        own[10],
        own[11],
        qkv_grad,
        own_qv,
        out_sums,
        own[0],
        own[1],
        own[2],
        up_grads[0],
        own_up[0],
        down_sums[0],
        own[3],
        own[6:8].T,
        own[8:10].T,
        jnp.stack(up_grads[1:]),
        own_up[1:],
        jnp.stack(down_sums[1:]),
        own[4:6],
    )


def solution(mesh):
    both = ("dp", "ctx")
    data = P("dp", "ctx", None)
    vector = P(both)
    matrix = P(both, None)
    expert_matrix = P(None, both, None)
    expert_vector = P(None, both)
    weights = (
        vector,
        vector,
        matrix,
        vector,
        matrix,
        vector,
        vector,
        vector,
        matrix,
        vector,
        matrix,
        vector,
        matrix,
        matrix,
        expert_matrix,
        expert_vector,
        expert_matrix,
        expert_vector,
    )
    return jax.shard_map(
        functools.partial(layer, mesh.shape["dp"], mesh.shape["ctx"]),
        mesh=mesh,
        in_specs=(data, data, data) + weights,
        out_specs=(data, data) + weights,
        check_vma=False,
    )
```

```python
import functools

import jax
import jax.numpy as jnp
from jax import lax
from jax.experimental import pallas as pl
from jax.experimental.pallas import tpu as pltpu
from jax.sharding import PartitionSpec as P

HEAD_DIM = 64
EPSILON = 1e-05
ROOT = 0.7978845608028654
CUBE = 0.044715
LANES = 128
f32 = jnp.float32
bf16 = jnp.bfloat16

ROUTER, MIX, GAIN_ONE, SHIFT_ONE, QV, OUT_BIAS, GAIN_TWO, SHIFT_TWO = 0, 2, 12, 13, 14, 16, 17, 18
DOWN_BIAS, EXPERT_DOWN, COUNT, UP_BIAS = 19, 20, 22, 23
SMALL_ROWS = 32

anywhere = pl.BlockSpec(memory_space=pl.ANY)
inside = pl.BlockSpec(memory_space=pltpu.VMEM)
scalar = pl.BlockSpec(memory_space=pltpu.SMEM)


def product(left_op, right_op):
    return jnp.dot(left_op, right_op, preferred_element_type=f32)


def left_product(left_op, right_op):
    return lax.dot_general(left_op, right_op, (((0,), (0,)), ((), ())), preferred_element_type=f32)


def right_product(left_op, right_op):
    return lax.dot_general(left_op, right_op, (((1,), (1,)), ((), ())), preferred_element_type=f32)


def layer_stats(values):
    row_mean = jnp.mean(values, -1, keepdims=True)
    centred = values - row_mean
    inverse = lax.rsqrt(jnp.mean(centred * centred, -1, keepdims=True) + EPSILON)
    return (centred * inverse, inverse)


def norm_back(grad_norm, normed, inverse, gain):
    scaled = grad_norm * gain
    return inverse * (
        scaled
        - jnp.mean(scaled, -1, keepdims=True)
        - normed * jnp.mean(scaled * normed, -1, keepdims=True)
    )


def sigmoid_pair(low, high):
    return 1.0 / (1.0 + jnp.exp(high - low))


def three_parts(values):
    high = values.astype(bf16)
    rest = values - high.astype(f32)
    middle = rest.astype(bf16)
    return high, middle, (rest - middle.astype(f32)).astype(bf16)


def aligned(index, size):
    return pl.ds(pl.multiple_of(index * size, size), size)


def run(kernel, name, micros, inputs, specs, outs, out_specs, scratch, grid=()):
    return pl.pallas_call(
        kernel,
        grid=grid,
        in_specs=specs,
        out_specs=out_specs,
        out_shape=[jax.ShapeDtypeStruct(shape, kind) for shape, kind in outs],
        scratch_shapes=scratch,
        compiler_params=pltpu.CompilerParams(
            dimension_semantics=("arbitrary",) * len(grid), vmem_limit_bytes=56 * 1024 * 1024
        ),
        cost_estimate=pl.CostEstimate(
            flops=int(micros * 10**9), bytes_accessed=1024, transcendentals=0
        ),
        name=name,
    )(*inputs)


def gate_kernel(*refs):
    in_ref, out_ref = refs[0], refs[-1]
    for i in range(in_ref.shape[0]):
        out_ref[i] = in_ref[i]


def gate(scalars, *others):
    return pl.pallas_call(
        gate_kernel,
        in_specs=[scalar] + [anywhere] * len(others),
        out_specs=scalar,
        out_shape=jax.ShapeDtypeStruct(scalars.shape, scalars.dtype),
        cost_estimate=pl.CostEstimate(flops=3 * 10**10, bytes_accessed=1024, transcendentals=0),
        name="gate",
    )(scalars, *others)


def start_all(copies):
    for copy in copies:
        copy.start()
    return copies


def wait_all(copies):
    for copy in copies:
        copy.wait()


def unpack_kernel(plan, places, *refs):
    dp, ctx, share, own, experts = plan
    parts, (by_row, by_column, out_ref), (held, sems) = refs[:dp], refs[dp : dp + 3], refs[dp + 3 :]
    size = parts[0].shape[0]
    wait_all(
        start_all(
            [
                pltpu.make_async_copy(part, held.at[aligned(places[i], size)], sems.at[i])
                for i, part in enumerate(parts)
            ]
        )
    )
    small = held[:, 4 * own :]
    by_row[...] = small
    turned = jnp.transpose(small.astype(f32))
    by_column[...] = turned[:SMALL_ROWS]
    for block in range(dp):
        for piece in range(ctx):
            at = block * size + piece * share
            out_ref[block * share : (block + 1) * share, piece * own : (piece + 1) * own] = held[
                at : at + share, 3 * own : 4 * own
            ]


def unpack(places, parts, plan):
    dp, ctx, share, own, experts = plan
    size = parts[0].shape[0]
    width = dp * size
    return run(
        functools.partial(unpack_kernel, plan),
        "unpack",
        3,
        [places] + parts,
        [scalar] + [anywhere] * dp,
        [((width, LANES), bf16), ((SMALL_ROWS, width), f32), ((dp * share, ctx * own), bf16)],
        [inside] * 3,
        [pltpu.VMEM((width, 4 * own + LANES), bf16), pltpu.SemaphoreType.DMA((dp,))],
    )


def qkv_kernel(plan, scalars, small_ref, *refs):
    dp, ctx, rows, own, share = plan
    parts, tokens = refs[:dp], refs[dp : dp + ctx]
    qkv_ref, norm_ref, weight_ref, sems = refs[dp + ctx :]
    size = parts[0].shape[0]
    moves = [
        pltpu.make_async_copy(token, norm_ref.at[aligned(scalars[dp + i], rows)], sems.at[i])
        for i, token in enumerate(tokens)
    ] + [
        pltpu.make_async_copy(part, weight_ref.at[aligned(scalars[i], size)], sems.at[ctx + i])
        for i, part in enumerate(parts)
    ]
    start_all(moves)
    width = small_ref.shape[1]
    column = lax.broadcasted_iota(jnp.int32, (width, own), 1) + scalars[dp] * own
    source = lax.broadcasted_iota(jnp.int32, (width, own), 0)
    rank, inner = column // (2 * share), column % (2 * share)
    pair = small_ref[QV : QV + 2, :].astype(bf16)
    biases = []
    for part in range(2):
        picks = [
            (source == (rank + part * (width // (2 * share))) * share + inner - half * share)
            & (inner // share == half)
            for half in range(2)
        ]
        biases.append(
            sum(product(pair[half : half + 1], picks[half].astype(bf16)) for half in range(2))
        )
    bias = jnp.concatenate([biases[0], jnp.zeros_like(biases[0]), biases[1]], 1)
    gain, shift = small_ref[GAIN_ONE : GAIN_ONE + 1, :], small_ref[SHIFT_ONE : SHIFT_ONE + 1, :]
    wait_all(moves)
    tile = min(256, ctx * rows)
    for at in range(0, ctx * rows, tile):
        span = slice(at, at + tile)
        normed, _ = layer_stats(norm_ref[span, :].astype(f32))
        low = (normed * gain + shift).astype(bf16)
        norm_ref[span, :] = low
        qkv_ref[span, :] = (product(low, weight_ref[:, : 3 * own]) + bias).astype(bf16)


def make_qkv(scalars, small, parts, tokens, plan):
    dp, ctx, rows, own, share = plan
    width = tokens[0].shape[1]
    return run(
        functools.partial(qkv_kernel, plan),
        "norm_qkv",
        8,
        [scalars, small] + parts + tokens,
        [scalar, inside] + [anywhere] * (dp + ctx),
        [
            ((ctx * rows, 3 * own), bf16),
            ((ctx * rows, width), bf16),
            ((width, parts[0].shape[1]), bf16),
        ],
        [inside] * 3,
        [pltpu.SemaphoreType.DMA((dp + ctx,))],
    )


def score_parts(q_part, k_ref, column, step, block):
    scale = HEAD_DIM ** (-0.5)
    parts = []
    if step:
        parts.append(right_product(q_part, k_ref[0 : step * block, column]) * scale)
    diagonal = right_product(q_part, k_ref[step * block : (step + 1) * block, column]) * scale
    rows = lax.broadcasted_iota(jnp.int32, (block, block), 0)
    keys = lax.broadcasted_iota(jnp.int32, (block, block), 1)
    parts.append(jnp.where(keys <= rows, diagonal, -1e30))
    return parts


def softmax_of(parts):
    row_max = functools.reduce(jnp.maximum, [jnp.max(part, -1, keepdims=True) for part in parts])
    terms = [jnp.exp(part - row_max) for part in parts]
    total = functools.reduce(jnp.add, [jnp.sum(term, -1, keepdims=True) for term in terms])
    inverse = 1.0 / total
    return [term * inverse for term in terms]


def key_spans(step, block):
    spans = [slice(0, step * block)] if step else []
    return spans + [slice(step * block, (step + 1) * block)]


def attention_forward_kernel(heads, block, rows_each, scalars, q_ref, k_ref, v_ref, *refs):
    out_refs, (held, out_ref, sems) = refs[:-3], refs[-3:]
    for head in range(heads):
        column = slice(head * HEAD_DIM, (head + 1) * HEAD_DIM)
        for step in range(q_ref.shape[0] // block):
            rows = slice(step * block, (step + 1) * block)
            probs = softmax_of(score_parts(q_ref[rows, column], k_ref, column, step, block))
            mixed = functools.reduce(
                jnp.add,
                [
                    product(prob.astype(bf16), v_ref[span, column])
                    for prob, span in zip(probs, key_spans(step, block))
                ],
            )
            out_ref[rows, column] = mixed.astype(bf16)
    step_now, lanes = pl.program_id(0), out_ref.shape[1]
    if held.shape[1] == lanes:
        held[...] = out_ref[...]
    else:
        held[:, aligned(step_now, lanes)] = out_ref[...]

    @pl.when(step_now == pl.num_programs(0) - 1)
    def _():
        wait_all(
            start_all(
                [
                    pltpu.make_async_copy(held.at[aligned(scalars[i], rows_each)], ref, sems.at[i])
                    for i, ref in enumerate(out_refs)
                ]
            )
        )


def attention_backward_kernel(
    heads, block, rows, scalars, q_ref, k_ref, v_ref, *refs
):
    scale = HEAD_DIM ** (-0.5)
    pieces, (dq_ref, dk_ref, dv_ref, held, k_acc, v_acc, sems) = refs[:-7], refs[-7:]
    step_now, lanes = pl.program_id(0), dq_ref.shape[1]

    @pl.when(step_now == 0)
    def _():
        wait_all(
            start_all(
                [
                    pltpu.make_async_copy(piece, held.at[aligned(scalars[i], rows)], sems.at[i])
                    for i, piece in enumerate(pieces)
                ]
            )
        )

    grads = held[...] if held.shape[1] == lanes else held[:, aligned(step_now, lanes)]
    for head in range(heads):
        column = slice(head * HEAD_DIM, (head + 1) * HEAD_DIM)
        for step in reversed(range(q_ref.shape[0] // block)):
            span_rows = slice(step * block, (step + 1) * block)
            spans = key_spans(step, block)
            q_part, o_part = q_ref[span_rows, column], grads[span_rows, column]
            probs = softmax_of(score_parts(q_part, k_ref, column, step, block))
            prob_grads = [right_product(o_part, v_ref[span, column]) for span in spans]
            delta = functools.reduce(
                jnp.add,
                [jnp.sum(p * g, -1, keepdims=True) for p, g in zip(probs, prob_grads)],
            )
            score_grads = [(p * (g - delta)).astype(bf16) for p, g in zip(probs, prob_grads)]
            q_grad = functools.reduce(
                jnp.add,
                [product(s, k_ref[span, column]) for s, span in zip(score_grads, spans)],
            )
            dq_ref[span_rows, column] = (q_grad * scale).astype(bf16)
            first = step == q_ref.shape[0] // block - 1
            for span, score_grad, prob in zip(spans, score_grads, probs):
                key_grad = left_product(score_grad, q_part)
                value_grad = left_product(prob.astype(bf16), o_part)
                k_acc[span, column] = key_grad if first else k_acc[span, column] + key_grad
                v_acc[span, column] = value_grad if first else v_acc[span, column] + value_grad
    dk_ref[...] = (k_acc[...] * scale).astype(bf16)
    dv_ref[...] = v_acc[...].astype(bf16)


def attention_plan(qkv, width):
    length = qkv.shape[0]
    heads = min(2, width // HEAD_DIM)
    block = min(256, length)
    lanes = heads * HEAD_DIM
    steps = width // lanes
    whole = lanes % LANES == 0
    joined = [qkv] * 3 if whole else [qkv[:, i * width : (i + 1) * width] for i in range(3)]

    def spec(part):
        first = part * steps if whole else 0
        return pl.BlockSpec((length, lanes), lambda step: (0, first + step))

    return length, heads, block, lanes, steps, spec, joined


def attention_forward(scalars, qkv, width, rows):
    length, heads, block, lanes, steps, spec, joined = attention_plan(qkv, width)
    pieces = length // rows
    return run(
        functools.partial(attention_forward_kernel, heads, block, rows),
        "attention_forward",
        10,
        [scalars] + joined,
        [scalar, spec(0), spec(1), spec(2)],
        [((rows, width), bf16)] * pieces,
        [anywhere] * pieces,
        [
            pltpu.VMEM((length, width), bf16),
            pltpu.VMEM((length, lanes), bf16),
            pltpu.SemaphoreType.DMA((pieces,)),
        ],
        (steps,),
    )


def attention_backward(scalars, qkv, pieces, width):
    length, heads, block, lanes, steps, spec, joined = attention_plan(qkv, width)
    return run(
        functools.partial(attention_backward_kernel, heads, block, pieces[0].shape[0]),
        "attention_backward",
        18,
        [scalars] + joined + pieces,
        [scalar, spec(0), spec(1), spec(2)] + [anywhere] * len(pieces),
        [((length, width), bf16)] * 3,
        [spec(0)] * 3,
        [
            pltpu.VMEM((length, width), bf16),
            pltpu.VMEM((length, lanes), f32),
            pltpu.VMEM((length, lanes), f32),
            pltpu.SemaphoreType.DMA((len(pieces),)),
        ],
        (steps,),
    )


def hidden_kernel(ctx, scalars, small_ref, out_ref, tokens_ref, sort_ref, *refs):
    pieces, (hidden_ref, norm_ref, sorted_ref) = refs[:ctx], refs[ctx:]
    own = pieces[0].shape[1]
    hidden = tokens_ref[...].astype(f32) + (
        sum(
            product(piece[...], out_ref[aligned(scalars[i], own), :])
            for i, piece in enumerate(pieces)
        )
        + small_ref[OUT_BIAS : OUT_BIAS + 1, :]
    )
    hidden_ref[...] = hidden
    normed, _ = layer_stats(hidden)
    low = (
        normed * small_ref[GAIN_TWO : GAIN_TWO + 1, :] + small_ref[SHIFT_TWO : SHIFT_TWO + 1, :]
    ).astype(bf16)
    norm_ref[...] = low
    sorted_ref[...] = product(sort_ref[...], low).astype(bf16)


def make_hidden(scalars, small, full_out, tokens, sort, pieces):
    shape = tokens.shape
    return run(
        functools.partial(hidden_kernel, len(pieces)),
        "hidden",
        4,
        [scalars, small, full_out, tokens, sort] + pieces,
        [scalar] + [inside] * (4 + len(pieces)),
        [(shape, f32), (shape, bf16), (shape, bf16)],
        [inside] * 3,
        [],
    )


def mlp_kernel(plan, scalars, small_ref, by_column, *refs):
    dp, ctx, rows, start, count, expert, merged, last = plan
    base = 2 if expert == 1 else 0
    depth = dp // 2
    refs = list(refs)

    def take(number):
        taken = refs[:number]
        del refs[:number]
        return taken

    x_parts, g_parts = take(ctx), take(ctx)
    parts = take(dp if merged else 2 * dp)
    sums = take(6) if last else []
    if last:
        y_refs, gx_refs = take(ctx), take(ctx)
    else:
        y_ref, gx_ref, dots_out = take(3)
    (gb_ref,) = take(1)
    mine, other = take(1 if merged else 2), take(1 if merged else 2)
    up, down, x_all, x_turned, g_all, act_all, go_all, gu_all, up_grad, down_grad = take(10)
    pre_all, back_all = take(2)
    held = take(6) if last else take(2)
    in_sems, x_sems, out_sems, held_sems = take(4)
    width, hidden = up.shape
    up_rows, down_rows = width // dp, hidden // dp
    tile = min(256, hidden)
    tiles = [slice(at, at + tile) for at in range(0, hidden, tile)]
    total = ctx * count

    def loads(target, size, which):
        return [
            pltpu.make_async_copy(
                parts[i].at[base + which] if merged else parts[which * dp + i],
                target.at[aligned(scalars[i], size)],
                in_sems.at[which * dp + i],
            )
            for i in range(dp)
        ]

    def rows_of(block):
        return slice(block * count, (block + 1) * count)

    tokens = [
        pltpu.make_async_copy(
            part.at[start : start + count], x_all.at[rows_of(i)], x_sems.at[i]
        )
        for i, part in enumerate(x_parts)
    ]
    grads = [
        pltpu.make_async_copy(
            part.at[start : start + count], g_all.at[rows_of(i)], x_sems.at[ctx + i]
        )
        for i, part in enumerate(g_parts)
    ]
    ups, downs = loads(up, up_rows, 0), loads(down, down_rows, 1)
    start_all(tokens + ups + grads + downs)
    gathered = [
        pltpu.make_async_copy(ref, held[i], held_sems.at[i]) for i, ref in enumerate(sums)
    ]
    start_all(gathered)
    wait_all(tokens)
    logits = product(x_all[...], small_ref[...])
    route_zero, route_one = logits[:, ROUTER : ROUTER + 1], logits[:, ROUTER + 1 : ROUTER + 2]
    mix_zero, mix_one = logits[:, MIX : MIX + 1], logits[:, MIX + 1 : MIX + 2]
    if expert is None:
        mask = None
        coef = sigmoid_pair(mix_zero, mix_one)
    else:
        place = lax.broadcasted_iota(jnp.int32, (count, 1), 0) + start
        firsts = [place < scalars[dp + block] for block in range(ctx)]
        masks = [(first if expert == 0 else ~first).astype(f32) for first in firsts]
        mask = jnp.concatenate(masks, 0)
        gate = (
            sigmoid_pair(route_zero, route_one)
            if expert == 0
            else sigmoid_pair(route_one, route_zero)
        )
        coef = sigmoid_pair(mix_one, mix_zero) * gate * mask
    x_turned[...] = jnp.transpose(x_all[...])
    wait_all(grads)
    go_all[...] = (g_all[...].astype(f32) * coef).astype(bf16)
    wait_all(ups)

    piece = 64 if total % 64 == 0 else 16

    def activate(cut):
        bias = by_column[:, cut]
        column_sum = jnp.zeros((8, tile), f32)
        for at in range(0, total, piece):
            span = slice(at, at + piece)
            pre = pre_all[span, :] + bias
            square = pre * pre
            bend = jnp.tanh((ROOT * pre) * (1.0 + CUBE * square))
            half = 0.5 + 0.5 * bend
            act_all[span, cut] = (pre * half).astype(bf16)
            slope = half + ((0.5 * ROOT) * pre) * (1.0 - bend * bend) * (
                1.0 + (3.0 * CUBE) * square
            )
            grad_up = (back_all[span, :] * slope).astype(bf16)
            gu_all[span, cut] = grad_up
            column_sum = column_sum + jnp.sum(
                grad_up.astype(f32).reshape(piece // 8, 8, tile), 0
            )
        gb_ref[:, cut] = jnp.sum(column_sum, 0, keepdims=True)

    for number, cut in enumerate(tiles):
        pre_all[...] = product(x_all[...], up[:, cut])
        if number == 0:
            wait_all(downs)
        back_all[...] = right_product(go_all[...], down[cut, :])
        activate(cut)
        down_grad[cut, :] = left_product(act_all[:, cut], go_all[...]).astype(bf16)
        up_grad[:, cut] = product(x_turned[...], gu_all[:, cut]).astype(bf16)

    def stores(grad, size, which):
        targets = [
            (mine[0].at[i, which] if merged else mine[which].at[i])
            if i < depth
            else (other[0].at[i - depth, which] if merged else other[which].at[i - depth])
            for i in range(dp)
        ]
        return [
            pltpu.make_async_copy(
                grad.at[aligned(scalars[i], size)], target, out_sems.at[which * dp + i]
            )
            for i, target in enumerate(targets)
        ]

    saved = start_all(stores(up_grad, up_rows, 0) + stores(down_grad, down_rows, 1))
    wait_all(gathered)
    sums_sent = []
    for block in range(ctx):
        span = rows_of(block)
        out = product(act_all[span, :], down[...])
        grad_x = right_product(gu_all[span, :], up[...])
        dot = jnp.sum(g_all[span, :].astype(f32) * out, -1, keepdims=True)
        out = out * coef[span]
        if not last:
            held[0][span, :], held[1][span, :] = out, grad_x
            for number, target in enumerate((y_ref, gx_ref)):
                copy = pltpu.make_async_copy(
                    held[number].at[span], target.at[span], held_sems.at[2 * block + number]
                )
                copy.start()
                sums_sent.append(copy)
            dots_out[span, :] = dot if mask is None else dot * mask[span]
            continue
        y_dense, gx_dense, dots_dense, y_first, gx_first, dots_first = held
        whole = slice(block * rows, (block + 1) * rows)
        sets = ((y_dense, y_first, out, y_refs), (gx_dense, gx_first, grad_x, gx_refs))
        for dense, first, own, target in sets:
            early = dense[whole, :][:start] + first[span, :][:start]
            middle = dense[whole, :][start:count] + (first[span, :][start:] + own[: count - start])
            late = dense[whole, :][count:] + own[count - start :]
            target[block][0:start, 0:width] = early.astype(bf16)
            target[block][start:count, 0:width] = middle.astype(bf16)
            target[block][count:rows, 0:width] = late.astype(bf16)
        own_dot = dot * mask[span]
        first_dot = dots_first[span, :]
        moe = jnp.concatenate(
            [
                first_dot[:start],
                first_dot[start:] + own_dot[: count - start],
                own_dot[count - start :],
            ],
            0,
        )
        lane = lax.broadcasted_iota(jnp.int32, (rows, LANES), 1)
        both = jnp.where(lane % 2 == 0, dots_dense[whole, :], moe)
        high, middle, low = three_parts(both)
        extra = jnp.where(lane < 2, high.astype(f32), jnp.where(lane < 4, middle.astype(f32), low.astype(f32)))
        gx_refs[block][:, width:] = jnp.where(lane < 6, extra, 0.0).astype(bf16)
    wait_all(saved + sums_sent)


def mlp(scalars, small, bias, x, g, parts, expert, merged, sums):
    ctx = len(x)
    rows, width = x[0].shape
    dp = len(parts) if merged else len(parts) // 2
    depth = dp // 2
    hidden = bias.shape[1]
    count = rows if expert is None else rows * 5 // 8
    start = 0 if expert in (None, 0) else rows - count
    total = ctx * count
    last = expert == 1
    if merged:
        halves = [((depth, 2) + parts[0].shape[1:], bf16)]
    else:
        halves = [((depth,) + parts[0].shape, bf16), ((depth,) + parts[dp].shape, bf16)]
    if last:
        outs = [((rows, width), bf16)] * ctx + [((rows, width + LANES), bf16)] * ctx
    else:
        outs = [((total, width), f32), ((total, width), f32), ((total, 1), f32)]
    outs = outs + [((1, hidden), f32)] + halves + halves
    small_outs = len(outs) - 2 * len(halves)
    held = [pltpu.VMEM(ref.shape, f32) for ref in sums] or [pltpu.VMEM((total, width), f32)] * 2
    tile = min(256, hidden)
    return run(
        functools.partial(mlp_kernel, (dp, ctx, rows, start, count, expert, merged, last)),
        "mlp",
        20 if total % LANES == 0 and expert is None else 18,
        [scalars, small, bias] + x + g + parts + sums,
        [scalar, inside, inside] + [anywhere] * (2 * ctx + len(parts) + len(sums)),
        outs,
        ([] if last else [anywhere] * 2)
        + [inside] * (small_outs if last else small_outs - 2)
        + [anywhere] * (2 * len(halves)),
        [
            pltpu.VMEM((width, hidden), bf16),
            pltpu.VMEM((hidden, width), bf16),
            pltpu.VMEM((total, width), bf16),
            pltpu.VMEM((width, total), bf16),
            pltpu.VMEM((total, width), bf16),
            pltpu.VMEM((total, hidden), bf16),
            pltpu.VMEM((total, width), bf16),
            pltpu.VMEM((total, hidden), bf16),
            pltpu.VMEM((width, hidden), bf16),
            pltpu.VMEM((hidden, width), bf16),
            pltpu.VMEM((total, tile), f32),
            pltpu.VMEM((total, tile), f32),
        ]
        + held
        + [
            pltpu.SemaphoreType.DMA((2 * dp,)),
            pltpu.SemaphoreType.DMA((2 * ctx,)),
            pltpu.SemaphoreType.DMA((2 * dp,)),
            pltpu.SemaphoreType.DMA((max(2 * ctx, len(sums)),)),
        ],
    )


def middle_kernel(
    ctx, scalars, by_row, by_column, out_ref, hidden_ref, norm_ref, g_ref, first_ref, unsort_ref, *refs
):
    gx, pieces = refs[:ctx], refs[ctx : 2 * ctx]
    outs = refs[2 * ctx :]
    base_ref, grad_hidden_ref, rows_ref = outs[:3]
    out_grads, grad_pieces = outs[3 : 3 + ctx], outs[3 + ctx : 3 + 2 * ctx]
    out_all, sems = outs[3 + 2 * ctx :]
    rows, width = hidden_ref.shape
    own = pieces[0].shape[1]
    unsort = unsort_ref[...]
    gathered = sum(product(unsort, piece[...]) for piece in gx)
    grad_norm = gathered[:, :width]
    extra = gathered[:, width:]
    dense_dot = extra[:, 0:1] + (extra[:, 2:3] + extra[:, 4:5])
    moe_dot = extra[:, 1:2] + (extra[:, 3:4] + extra[:, 5:6])
    grad_out = g_ref[...].astype(f32)
    first = first_ref[...]
    down_bias = by_column[DOWN_BIAS : DOWN_BIAS + 1, :]
    moe_bias = jnp.where(
        first > 0.5,
        by_column[EXPERT_DOWN : EXPERT_DOWN + 1, :],
        by_column[EXPERT_DOWN + 1 : EXPERT_DOWN + 2, :],
    )
    dense_dot = dense_dot + jnp.sum(grad_out * down_bias, -1, keepdims=True)
    moe_dot = moe_dot + jnp.sum(grad_out * moe_bias, -1, keepdims=True)
    norm = norm_ref[...]
    logits = product(norm, by_row[...])
    route = [
        sigmoid_pair(logits[:, a : a + 1], logits[:, b : b + 1])
        for a, b in ((ROUTER, ROUTER + 1), (ROUTER + 1, ROUTER))
    ]
    mix = [
        sigmoid_pair(logits[:, a : a + 1], logits[:, b : b + 1])
        for a, b in ((MIX, MIX + 1), (MIX + 1, MIX))
    ]
    hot = [first, 1.0 - first]
    gate = route[0] * hot[0] + route[1] * hot[1]
    branch = mix[1] * gate
    hidden = hidden_ref[...]
    base_ref[...] = hidden + (mix[0] * down_bias + branch * moe_bias)
    grad_mix = [dense_dot, moe_dot * gate]
    mean_mix = mix[0] * grad_mix[0] + mix[1] * grad_mix[1]
    grad_gate = moe_dot * mix[1]
    grad_route = [hot[0] * grad_gate, hot[1] * grad_gate]
    mean_route = route[0] * grad_route[0] + route[1] * grad_route[1]
    lane = lax.broadcasted_iota(jnp.int32, (rows, LANES), 1)
    columns = [route[i] * (grad_route[i] - mean_route) for i in range(2)]
    columns += [mix[i] * (grad_mix[i] - mean_mix) for i in range(2)]
    logit_grads = jnp.zeros((rows, LANES), f32)
    for i, column in enumerate(columns):
        logit_grads = jnp.where((lane % 4 == i) & (lane < 12), column, logit_grads)
    high, middle, rest = [part.astype(f32) for part in three_parts(logit_grads)]
    split = jnp.where(lane < 4, high, jnp.where(lane < 8, middle, rest)).astype(bf16)
    grad_norm = grad_norm + right_product(split, by_row[...])
    small_grads = left_product(split, norm)
    small_grads = small_grads[0:4] + (small_grads[4:8] + small_grads[8:12])
    grad_dense = (grad_out * mix[0]).astype(bf16).astype(f32)
    grad_moe = (grad_out * branch).astype(bf16).astype(f32)
    normed, inverse = layer_stats(hidden)
    gain = by_column[GAIN_TWO : GAIN_TWO + 1, :]
    grad_hidden = grad_out + norm_back(grad_norm, normed, inverse, gain)
    grad_hidden_ref[...] = grad_hidden
    low = grad_hidden.astype(bf16)

    def total(values):
        return jnp.sum(values, 0, keepdims=True)

    sums = [
        total(low.astype(f32)),
        total(grad_norm * normed),
        total(grad_norm),
        total(grad_dense),
        total(grad_moe * hot[0]),
        total(grad_moe * hot[1]),
    ]
    rows_ref[...] = jnp.concatenate(sums + [small_grads, jnp.zeros((6, width), f32)], 0)
    for i, (piece, target) in enumerate(zip(pieces, grad_pieces)):
        span = aligned(scalars[i], own)
        target[...] = right_product(low, out_ref[span, :]).astype(bf16)
        part = left_product(piece[...], low).astype(bf16)
        share = out_all.shape[3]
        many = own // (ctx * share)
        for c in range(ctx):
            columns = part[:, c * own : (c + 1) * own].reshape(many, ctx, share, own)
            out_all[aligned(scalars[i], many), :, c] = columns
    wait_all(
        start_all(
            [
                pltpu.make_async_copy(out_all.at[:, scalars[i]], target, sems.at[i])
                for i, target in enumerate(out_grads)
            ]
        )
    )


def make_middle(
    scalars, by_row, by_column, full_out, hidden, norm, g, first, unsort, gx, pieces, dp
):
    ctx = len(gx)
    rows, width = hidden.shape
    own = pieces[0].shape[1]
    return run(
        functools.partial(middle_kernel, ctx),
        "middle",
        11,
        [scalars, by_row, by_column, full_out, hidden, norm, g, first, unsort] + gx + pieces,
        [scalar] + [inside] * (8 + 2 * ctx),
        [
            ((rows, width), f32),
            ((rows, width), f32),
            ((16, width), f32),
        ]
        + [((dp, ctx, width // (dp * ctx), own), bf16)] * ctx
        + [((rows, own), bf16)] * ctx,
        [inside] * 3 + [anywhere] * ctx + [inside] * ctx,
        [
            pltpu.VMEM((dp, ctx, ctx, width // (dp * ctx), own), bf16),
            pltpu.SemaphoreType.DMA((ctx,)),
        ],
    )


def qkv_back_kernel(plan, scalars, norm_ref, dq_ref, dk_ref, dv_ref, weight_ref, *refs):
    dp, ctx, rows, own = plan
    depth = dp // 2
    out_pieces, gn_refs = refs[:ctx], refs[ctx : 2 * ctx]
    mine, other, bias_ref, grad, weight_grad, gn, sems, gn_sems = refs[2 * ctx :]
    width = norm_ref.shape[1]
    size = width // dp
    for part, ref in enumerate((dq_ref, dk_ref, dv_ref)):
        grad[:, part * own : (part + 1) * own] = ref[...]
    tile = min(256, ctx * rows)
    weight = weight_ref[:, : 3 * own]
    for at in range(0, ctx * rows, tile):
        gn[at : at + tile, :] = right_product(grad[at : at + tile, :], weight).astype(bf16)
    sent = start_all(
        [
            pltpu.make_async_copy(gn.at[aligned(scalars[dp + i], rows)], ref, gn_sems.at[i])
            for i, ref in enumerate(gn_refs)
        ]
    )
    step = min(256, width)
    for at in range(0, width, step):
        weight_grad[at : at + step, : 3 * own] = left_product(
            norm_ref[:, at : at + step], grad[...]
        ).astype(bf16)
    weight_grad[:, 3 * own :] = sum(piece[...].astype(f32) for piece in out_pieces).astype(bf16)
    saved = start_all(
        [
            pltpu.make_async_copy(
                weight_grad.at[aligned(scalars[i], size)],
                mine.at[i] if i < depth else other.at[i - depth],
                sems.at[i],
            )
            for i in range(dp)
        ]
    )
    bias = jnp.sum(grad[...].astype(f32), 0, keepdims=True)
    here = lax.broadcasted_iota(jnp.int32, (1, width), 1) // own == scalars[dp]
    for row, at in enumerate((0, 2 * own)):
        spread = jnp.concatenate([bias[:, at : at + own]] * ctx, 1)
        bias_ref[row : row + 1, :] = jnp.where(here, spread, 0.0)
    wait_all(sent + saved)


def qkv_back(scalars, norm, grads, weight, out_pieces, plan):
    dp, ctx, rows, own = plan
    length, width = norm.shape
    half = ((dp // 2, width // dp, 4 * own), bf16)
    return run(
        functools.partial(qkv_back_kernel, plan),
        "qkv_back",
        8,
        [scalars, norm] + list(grads) + [weight] + list(out_pieces),
        [scalar] + [inside] * (5 + ctx),
        [((rows, width), bf16)] * ctx + [half, half, ((2, width), f32)],
        [anywhere] * (ctx + 2) + [inside],
        [
            pltpu.VMEM((length, 3 * own), bf16),
            pltpu.VMEM((width, 4 * own), bf16),
            pltpu.VMEM((length, width), bf16),
            pltpu.SemaphoreType.DMA((dp,)),
            pltpu.SemaphoreType.DMA((ctx,)),
        ],
    )


def final_kernel(ctx, order, by_column, tokens_ref, grad_hidden_ref, *refs):
    pieces, (grad_ref, rows_ref) = refs[:ctx], refs[ctx:]
    grad_norm = sum(piece[...].astype(f32) for piece in pieces)
    normed, inverse = layer_stats(tokens_ref[...].astype(f32))
    gain = by_column[GAIN_ONE : GAIN_ONE + 1, :]
    grad_ref[...] = grad_hidden_ref[...] + norm_back(grad_norm, normed, inverse, gain)
    rows_ref[0:1, :] = jnp.sum(grad_norm * normed, 0, keepdims=True)
    rows_ref[1:2, :] = jnp.sum(grad_norm, 0, keepdims=True)


def make_final(order, by_column, tokens, grad_hidden, pieces):
    return run(
        functools.partial(final_kernel, len(pieces)),
        "final",
        4,
        [order, by_column, tokens, grad_hidden] + pieces,
        [scalar] + [inside] * (3 + len(pieces)),
        [(tokens.shape, f32), ((2, tokens.shape[1]), f32)],
        [inside] * 2,
        [],
    )


def result_kernel(ctx, base_ref, unsort_ref, *refs):
    pieces, (out_ref,) = refs[:ctx], refs[ctx:]
    unsort = unsort_ref[...]
    out_ref[...] = base_ref[...] + sum(product(unsort, piece[...]) for piece in pieces)


def make_result(base, unsort, pieces):
    return run(
        functools.partial(result_kernel, len(pieces)),
        "result",
        3.5,
        [base, unsort] + pieces,
        [inside] * (2 + len(pieces)),
        [(base.shape, f32)],
        [inside],
        [],
    )[0]


def layer(
    dp,
    ctx,
    tokens,
    cotangent,
    routes,
    ln1_gain,
    ln1_bias,
    qkv_weight,
    qv_bias,
    out_weight,
    out_bias,
    ln2_gain,
    ln2_bias,
    up_weight,
    up_bias,
    down_weight,
    down_bias,
    router_weight,
    mix_weight,
    expert_up,
    expert_up_bias,
    expert_down,
    expert_down_bias,
):
    rows, width = tokens.shape[0] * tokens.shape[1], tokens.shape[2]
    experts, share, hidden = expert_up.shape
    own_hidden = hidden // ctx
    own_width = width // ctx
    unit = hidden // (dp * ctx)
    me = lax.axis_index("ctx")
    place_dp = lax.axis_index("dp")
    core = place_dp % 2
    depth = dp // 2
    shifts = range(1, ctx)
    ring_pairs = [(i, (i + 2) % dp) for i in range(dp)]
    core_pairs = [(i, i ^ 1) for i in range(dp)]
    places = jnp.stack(
        [
            ((place_dp // 2 + depth - t) % depth) * 2 + c
            for c in (core, 1 - core)
            for t in range(depth)
        ]
    ).astype(jnp.int32)
    peers = jnp.stack([me ^ s for s in range(ctx)]).astype(jnp.int32)

    def swap(array, shift):
        return lax.ppermute(array, "ctx", [(i, i ^ shift) for i in range(ctx)])

    def gather_ctx(array):
        return [array] + [swap(array, s) for s in shifts]

    def trade(pieces):
        return [pieces[0]] + [swap(pieces[s], s) for s in shifts]

    def by_peer(pieces):
        return [lax.dynamic_index_in_dim(pieces, me ^ s, 0, keepdims=False) for s in range(ctx)]

    def natural(pieces):
        whole = jnp.zeros((ctx,) + pieces[0].shape, pieces[0].dtype)
        for s, piece in enumerate(pieces):
            whole = lax.dynamic_update_slice_in_dim(whole, piece[None], me ^ s, 0)
        return whole

    def ring(array):
        return lax.ppermute(array, "dp", ring_pairs)

    def swap_core(array):
        return lax.ppermute(array, "dp", core_pairs)

    def sync(*trees):
        return lax.optimization_barrier(trees)

    class Rings:
        def __init__(self, arrays):
            self.parts = [list(arrays)]

        def move(self):
            self.parts.append([ring(array) for array in self.parts[-1]])

        def rest(self):
            while len(self.parts) < depth:
                self.move()

        def pieces(self, others, which):
            return [part[which] for part in self.parts] + [part[which] for part in others]

    def swap_cores(part):
        return [swap_core(array) for array in part]

    class Scatter:
        def __init__(self, *halves):
            half = len(halves) // 2
            self.mine, self.step = list(halves[:half]), 0
            self.got = [swap_core(other) for other in halves[half:]]
            self.arrived = self.sent = None

        def receive(self, others):
            if self.sent is None:
                self.got, others = sync(self.got, others)
            else:
                self.arrived, others = sync([ring(part) for part in self.sent], others)
            return others

        def add(self):
            self.step += 1
            at = self.step % depth
            parts = [m[at].astype(f32) + g[at].astype(f32) for m, g in zip(self.mine, self.got)]
            if self.arrived is not None:
                parts = [p + c.astype(f32) for p, c in zip(parts, self.arrived)]
            self.sent = [part.astype(bf16) if at else part for part in parts]

        def move(self, others):
            others = self.receive(others)
            self.add()
            return others

        def close(self):
            self.add()
            while self.step < depth:
                self.arrived = [ring(part) for part in self.sent]
                self.add()

    def pin(value, *sums):
        value, sent = sync(value, [one.sent for one in sums])
        for one, parts in zip(sums, sent):
            one.sent = parts
        return value

    def pair(sums):
        return sums if len(sums) == 2 else [sums[0][0], sums[0][1]]

    tokens = tokens.reshape(rows, width)
    cotangent = cotangent.reshape(rows, width)
    first_hot = routes.reshape(rows) == 0
    first_float = first_hot.astype(f32)
    first_count = jnp.sum(first_float)

    def column(vector):
        return vector.reshape(-1, share).T

    def bias_column(vector):
        return jnp.pad(vector.reshape(unit, 1), ((0, ctx * share - unit), (0, 0)))

    small = jnp.concatenate(
        [
            jnp.concatenate([router_weight, mix_weight] * 3, 1),
            column(ln1_gain),
            column(ln1_bias),
            column(qv_bias),
            column(out_bias),
            column(ln2_gain),
            column(ln2_bias),
            column(down_bias),
            expert_down_bias.T,
            jnp.broadcast_to(first_count.astype(bf16), (share, 1)),
        ],
        1,
    )
    small = jnp.pad(small, ((0, 0), (0, LANES - small.shape[1])))
    qkv_cut = qkv_weight.reshape(share, 3, ctx, own_width).transpose(2, 0, 1, 3)
    first_cut = jnp.concatenate(
        [
            qkv_cut.reshape(ctx, share, 3 * own_width),
            jnp.broadcast_to(small[None], (ctx, share, LANES)),
        ],
        -1,
    )
    ups = jnp.concatenate([up_weight[None], expert_up], 0)
    ups_cut = ups.reshape(experts + 1, share, dp, ctx, unit).transpose(3, 0, 1, 2, 4)
    ups_sent = by_peer(ups_cut.reshape(ctx, experts + 1, share, own_hidden))
    first_rows, ups_sent = sync(trade(by_peer(first_cut)), ups_sent)
    first_rows = natural(first_rows).reshape(ctx * share, 3 * own_width + LANES)
    qkv_rows = first_rows[:, : 3 * own_width]
    small_rows = first_rows[:, 3 * own_width :]
    counts = small_rows[::share, COUNT]
    bias_lanes = jnp.concatenate(
        [bias_column(up_bias)] + [bias_column(expert_up_bias[e]) for e in range(experts)], 1
    )
    lane = jnp.arange(LANES)[None, :]
    bias_lanes = jnp.pad(bias_lanes, ((0, 0), (UP_BIAS, LANES - UP_BIAS - bias_lanes.shape[1])))
    small_rows = jnp.where((lane >= UP_BIAS) & (lane < UP_BIAS + experts + 1), bias_lanes, small_rows)
    out_rows = out_weight.reshape(share, ctx, own_width).transpose(1, 0, 2)
    out_rows = out_rows.reshape(ctx * share, own_width)
    first = Rings([jnp.concatenate([qkv_rows, out_rows, small_rows], 1)])

    first.move()
    first_others = [swap_cores(first.parts[0])]
    token_parts = gather_ctx(tokens)
    first.parts[1], first_others[0] = sync(first.parts[1], first_others[0])
    first.move()
    first_others.append(swap_cores(first.parts[1]))
    token_parts, first.parts[2], first_others[1], ups_sent = sync(
        token_parts, first.parts[2], first_others[1], ups_sent
    )
    first.rest()
    first_others += [swap_cores(part) for part in first.parts[2:-1]]
    ups_rows, first.parts[-1], first_others = sync(trade(ups_sent), first.parts[-1], first_others)
    ups_rows = natural(ups_rows).transpose(1, 0, 2, 3)
    ups_rows = ups_rows.reshape(experts + 1, ctx * share, own_hidden)
    downs = [down_weight] + [expert_down[e] for e in range(experts)]
    merged = downs[0].shape == ups_rows.shape[1:]
    if merged:
        dense_weights = [jnp.stack([ups_rows[0], downs[0]])]
        expert_weights = [jnp.stack([ups_rows[1], downs[1], ups_rows[2], downs[2]])]
    else:
        dense_weights = [ups_rows[0], downs[0]]
        expert_weights = [ups_rows[1], downs[1], ups_rows[2], downs[2]]
    dense_ring = Rings(dense_weights)
    dense_ring.move()
    first_others.append(swap_cores(first.parts[-1]))
    first_parts = first.pieces(first_others, 0)
    plan = (dp, ctx, share, own_width, experts)
    by_row, by_column, out_own = unpack(places, first_parts, plan)
    expert_weights, by_row = sync(expert_weights, by_row)
    expert_ring = Rings(expert_weights)
    expert_ring.move()
    out_pieces = gather_ctx(out_own)

    order = jnp.arange(rows).astype(f32)
    counted = jnp.cumsum(first_float)
    place = jnp.where(first_hot, counted - 1.0, first_count + order - counted)
    unsort = (place[:, None] == order[None, :]).astype(bf16)
    sort = (place[None, :] == order[:, None]).astype(bf16)
    sorted_grad = product(sort, cotangent).astype(bf16)

    scalars = jnp.concatenate([places, peers])
    qkv, attn_in, own_qkv = make_qkv(
        scalars, by_column, first_parts, token_parts, (dp, ctx, rows, own_width, share)
    )
    qkv, dense_ring.parts[1] = sync(qkv, dense_ring.parts[1])
    dense_ring.move()
    attended_heads = list(attention_forward(peers, qkv, own_width, rows))
    attended_heads, out_pieces = sync(attended_heads, out_pieces)
    attended = trade(attended_heads)
    full_out = natural(out_pieces).reshape(ctx, dp, share, width).transpose(1, 0, 2, 3)
    full_out = full_out.reshape(width, width)
    hidden_state, ffn_in, sorted_in = make_hidden(
        peers, by_column, full_out, tokens, sort, attended
    )
    sorted_in, expert_ring.parts[1] = sync(sorted_in, expert_ring.parts[1])
    expert_ring.move()
    ffn_parts = gather_ctx(sorted_in)
    late_columns, late_counts, _ = sync(by_column, counts, sorted_in)
    row_counts = jnp.stack([late_counts[me ^ s] for s in range(ctx)]).astype(jnp.int32)
    mlp_scalars = jnp.concatenate([places, row_counts])
    up_biases = late_columns[UP_BIAS : UP_BIAS + experts + 1]
    up_biases = up_biases.reshape(experts + 1, dp, -1)[:, :, :unit].reshape(experts + 1, own_hidden)

    mlp_scalars = gate(mlp_scalars, *dense_ring.parts[2])
    ffn_parts, dense_ring.parts[2], sorted_grad, up_biases, mlp_scalars = sync(
        ffn_parts, dense_ring.parts[2], sorted_grad, up_biases, mlp_scalars
    )
    dense_ring.rest()
    grad_parts = [sorted_grad] + [swap(sorted_grad, s) for s in shifts[:2]]
    expert_ring.parts[2], late_grad = sync(expert_ring.parts[2], sorted_grad)
    expert_ring.rest()
    grad_parts += [swap(late_grad, s) for s in shifts[2:]]
    grad_parts, dense_ring.parts = sync(grad_parts, dense_ring.parts)
    dense_others = [swap_cores(part) for part in dense_ring.parts]
    dense_others, early = sync(dense_others, expert_ring.parts[:-1])
    expert_others = [swap_cores(part) for part in early]

    def run_mlp(which, held, parts, sums):
        return mlp(
            held,
            by_row,
            up_biases[which][None],
            ffn_parts,
            grad_parts,
            parts,
            which - 1 if which else None,
            merged,
            list(sums),
        )

    def weights_of(rings, others, first_array):
        if merged:
            return rings.pieces(others, 0)
        return rings.pieces(others, first_array) + rings.pieces(others, first_array + 1)

    dense = run_mlp(0, mlp_scalars, weights_of(dense_ring, dense_others, 0), [])
    sum_dense = Scatter(*dense[4:])
    expert_last, expert_others, gb_dense = sync(expert_ring.parts[-1], expert_others, dense[3])
    expert_ring.parts[-1] = expert_last
    expert_others = expert_others + [swap_cores(expert_last)]
    gb_dense = sum_dense.move(gb_dense)
    first_mlp = run_mlp(
        1,
        pin(gate(mlp_scalars), sum_dense),
        weights_of(expert_ring, expert_others, 0),
        [],
    )
    sum_first = Scatter(*first_mlp[4:])
    gb_first = sum_dense.move(first_mlp[3])
    second_mlp = run_mlp(
        2,
        pin(mlp_scalars, sum_dense),
        weights_of(expert_ring, expert_others, 2),
        dense[:3] + first_mlp[:3],
    )
    gb_second = sum_first.move(sum_dense.move(second_mlp[2 * ctx]))
    grad_sent = list(second_mlp[ctx : 2 * ctx])
    grad_pieces = trade(grad_sent[:3] + pin(grad_sent[3:], sum_dense, sum_first))
    grad_pieces, halves, result_sent = sync(
        grad_pieces, second_mlp[2 * ctx + 1 :], second_mlp[:ctx]
    )
    grad_pieces = sum_first.move(sum_dense.receive(grad_pieces))
    sum_second = Scatter(*halves)
    result_pieces = [result_sent[0]] + [swap(result_sent[s], s) for s in shifts[:2]]

    middle_peers, sum_dense.arrived = sync(peers, sum_dense.arrived)
    base, grad_hidden, middle_rows, *rest = make_middle(
        pin(middle_peers, sum_first),
        by_row,
        by_column,
        full_out,
        hidden_state,
        ffn_in,
        cotangent,
        first_float[:, None],
        unsort,
        grad_pieces,
        attended,
        dp,
    )
    out_sent, att_sent = rest[:ctx], rest[ctx:]
    result_pieces, att_sent = sync(result_pieces, att_sent)
    att_grads, out_sent = sync(trade(att_sent), out_sent)
    out_sent = [piece.reshape(width, own_width) for piece in out_sent]
    out_pieces = trade(out_sent)
    middle_rows = sum_second.move(sum_first.move(middle_rows))

    grad_heads = attention_backward(pin(peers, sum_first, sum_second), qkv, att_grads, own_width)
    grad_heads = sum_second.move(sum_first.receive(grad_heads))
    back_scalars, sum_first.arrived = sync(pin(scalars, sum_second), sum_first.arrived)
    *norm_grads, last_mine, last_other, grad_b_qkv = qkv_back(
        back_scalars,
        attn_in,
        grad_heads,
        own_qkv,
        out_pieces,
        (dp, ctx, rows, own_width),
    )
    sum_last = Scatter(last_mine, last_other)
    norm_pieces = [norm_grads[0]] + [swap(norm_grads[s], s) for s in shifts[:2]]
    late_pieces = [swap(norm_grads[s], s) for s in shifts[2:]]
    grad_b_qkv = sum_last.move(grad_b_qkv)
    norm_pieces[1] = sum_last.move(sum_second.move(norm_pieces[1]))
    small_sources = (grad_b_qkv, middle_rows, gb_dense, gb_first, gb_second)
    norm_pieces, small_sources, sum_dense.arrived, sum_first.arrived = pin(
        (norm_pieces, small_sources, sum_dense.arrived, sum_first.arrived), sum_last, sum_second
    )
    grad_b_qkv, middle_rows, gb_dense, gb_first, gb_second = small_sources
    norm_pieces += late_pieces

    def cut_columns(parts):
        joined = jnp.concatenate([part.astype(bf16) for part in parts], 1)
        return by_peer(joined.reshape(ctx, share, joined.shape[1]))

    def from_columns(pieces, at, size, groups):
        whole = natural([piece[:, at : at + size] for piece in pieces])
        whole = whole.reshape(ctx, share, groups, size // groups).transpose(1, 2, 0, 3)
        return whole.reshape(share, ctx * size).astype(f32)

    norm_pieces, result_sent = sync(norm_pieces, result_sent)
    result_pieces = result_pieces + [swap(result_sent[s], s) for s in shifts[2:]]
    grad_inputs, final_rows = make_final(peers, by_column, tokens, grad_hidden, norm_pieces)
    final_rows = pin(sum_last.move(final_rows), sum_last)
    final_rows, sum_dense.arrived, sum_first.arrived = sync(
        final_rows, sum_dense.arrived, sum_first.arrived
    )
    sum_dense.close()
    sum_first.close()

    small_rows = jnp.concatenate(
        [middle_rows[:10], final_rows, grad_b_qkv, jnp.zeros((2, width), f32)], 0
    )
    small_rows, result_pieces = sync(small_rows, result_pieces)
    small_pieces = gather_ctx(small_rows)

    small_pieces = sum_last.receive(sum_second.receive(small_pieces))
    sum_last.close()
    (last_sum,) = sum_last.sent
    qkv_part, out_sums = last_sum[:, : 3 * own_width], last_sum[:, 3 * own_width :]
    out_sums = out_sums.reshape(ctx, share, own_width).transpose(1, 0, 2).reshape(share, width)
    late_pieces = trade(cut_columns([qkv_part]))
    up_rows = jnp.concatenate([gb_dense, gb_first, gb_second, jnp.zeros((5, own_hidden), f32)], 0)
    up_rows = jnp.pad(up_rows, ((0, 0), (0, width - own_hidden)))
    small_sum = jnp.concatenate([sum(small_pieces), up_rows], 0)
    small_sum, late_pieces = sync(small_sum + swap_core(small_sum), late_pieces)
    pairs = [[(i, (i + 2 * t) % dp) for i in range(dp)] for t in range(depth)]
    small_sum = sum(
        [small_sum] + [lax.ppermute(small_sum, "dp", pairs[t]) for t in range(1, depth)]
    )
    sum_second.close()
    sums = [pair(one.sent) for one in (sum_dense, sum_first, sum_second)]
    early_sent, late_pieces = sync(cut_columns([one[0] for one in sums]), late_pieces)
    early_pieces = trade(early_sent)
    result = make_result(base, unsort, result_pieces)
    up_grads = [
        from_columns(early_pieces, which * own_hidden, own_hidden, dp)
        for which in range(experts + 1)
    ]
    qkv_grad = from_columns(late_pieces, 0, 3 * own_width, 3)
    down_sums = [one[1] for one in sums]
    owner = place_dp * ctx + me
    own = lax.dynamic_slice(small_sum, (0, owner * share), (12, share))
    own_qv = lax.dynamic_slice(small_sum[12:14].reshape(-1), (owner * 2 * share,), (2 * share,))
    own_up = lax.dynamic_slice(small_sum, (16, place_dp * unit), (3, unit))
    return (
        result[None],
        grad_inputs[None],
        own[10],
        own[11],
        qkv_grad,
        own_qv,
        out_sums,
        own[0],
        own[1],
        own[2],
        up_grads[0],
        own_up[0],
        down_sums[0],
        own[3],
        own[6:8].T,
        own[8:10].T,
        jnp.stack(up_grads[1:]),
        own_up[1:],
        jnp.stack(down_sums[1:]),
        own[4:6],
    )


def solution(mesh):
    both = ("dp", "ctx")
    data = P("dp", "ctx", None)
    vector = P(both)
    matrix = P(both, None)
    expert_matrix = P(None, both, None)
    expert_vector = P(None, both)
    weights = (
        vector,
        vector,
        matrix,
        vector,
        matrix,
        vector,
        vector,
        vector,
        matrix,
        vector,
        matrix,
        vector,
        matrix,
        matrix,
        expert_matrix,
        expert_vector,
        expert_matrix,
        expert_vector,
    )
    return jax.shard_map(
        functools.partial(layer, mesh.shape["dp"], mesh.shape["ctx"]),
        mesh=mesh,
        in_specs=(data, data, data) + weights,
        out_specs=(data, data) + weights,
        check_vma=False,
    )
```

```python
import functools

import jax
import jax.numpy as jnp
from jax import lax
from jax.experimental import pallas as pl
from jax.experimental.pallas import tpu as pltpu
from jax.sharding import PartitionSpec as P

HEAD_DIM = 64
EPSILON = 1e-05
ROOT = 0.7978845608028654
CUBE = 0.044715
LANES = 128
f32 = jnp.float32
bf16 = jnp.bfloat16

ROUTER, MIX, GAIN_ONE, SHIFT_ONE, QV, OUT_BIAS, GAIN_TWO, SHIFT_TWO = 0, 2, 12, 13, 14, 16, 17, 18
DOWN_BIAS, EXPERT_DOWN, COUNT, UP_BIAS = 19, 20, 22, 23
SMALL_ROWS = 32

anywhere = pl.BlockSpec(memory_space=pl.ANY)
inside = pl.BlockSpec(memory_space=pltpu.VMEM)
scalar = pl.BlockSpec(memory_space=pltpu.SMEM)


def product(left_op, right_op):
    return jnp.dot(left_op, right_op, preferred_element_type=f32)


def left_product(left_op, right_op):
    return lax.dot_general(left_op, right_op, (((0,), (0,)), ((), ())), preferred_element_type=f32)


def right_product(left_op, right_op):
    return lax.dot_general(left_op, right_op, (((1,), (1,)), ((), ())), preferred_element_type=f32)


def layer_stats(values):
    row_mean = jnp.mean(values, -1, keepdims=True)
    centred = values - row_mean
    inverse = lax.rsqrt(jnp.mean(centred * centred, -1, keepdims=True) + EPSILON)
    return (centred * inverse, inverse)


def norm_back(grad_norm, normed, inverse, gain):
    scaled = grad_norm * gain
    return inverse * (
        scaled
        - jnp.mean(scaled, -1, keepdims=True)
        - normed * jnp.mean(scaled * normed, -1, keepdims=True)
    )


def sigmoid_pair(low, high):
    return 1.0 / (1.0 + jnp.exp(high - low))


def three_parts(values):
    high = values.astype(bf16)
    rest = values - high.astype(f32)
    middle = rest.astype(bf16)
    return high, middle, (rest - middle.astype(f32)).astype(bf16)


def aligned(index, size):
    return pl.ds(pl.multiple_of(index * size, size), size)


def run(kernel, name, micros, inputs, specs, outs, out_specs, scratch, grid=()):
    return pl.pallas_call(
        kernel,
        grid=grid,
        in_specs=specs,
        out_specs=out_specs,
        out_shape=[jax.ShapeDtypeStruct(shape, kind) for shape, kind in outs],
        scratch_shapes=scratch,
        compiler_params=pltpu.CompilerParams(
            dimension_semantics=("arbitrary",) * len(grid), vmem_limit_bytes=56 * 1024 * 1024
        ),
        cost_estimate=pl.CostEstimate(
            flops=int(micros * 10**9), bytes_accessed=1024, transcendentals=0
        ),
        name=name,
    )(*inputs)


def gate_kernel(*refs):
    in_ref, out_ref = refs[0], refs[-1]
    for i in range(in_ref.shape[0]):
        out_ref[i] = in_ref[i]


def gate(scalars, *others):
    return pl.pallas_call(
        gate_kernel,
        in_specs=[scalar] + [anywhere] * len(others),
        out_specs=scalar,
        out_shape=jax.ShapeDtypeStruct(scalars.shape, scalars.dtype),
        cost_estimate=pl.CostEstimate(flops=3 * 10**10, bytes_accessed=1024, transcendentals=0),
        name="gate",
    )(scalars, *others)


def start_all(copies):
    for copy in copies:
        copy.start()
    return copies


def wait_all(copies):
    for copy in copies:
        copy.wait()


def unpack_kernel(plan, places, *refs):
    dp, ctx, share, own, experts = plan
    parts, (by_row, by_column, out_ref), (held, sems) = refs[:dp], refs[dp : dp + 3], refs[dp + 3 :]
    size = parts[0].shape[0]
    wait_all(
        start_all(
            [
                pltpu.make_async_copy(part, held.at[aligned(places[i], size)], sems.at[i])
                for i, part in enumerate(parts)
            ]
        )
    )
    small = held[:, 4 * own :]
    by_row[...] = small
    turned = jnp.transpose(small.astype(f32))
    by_column[...] = turned[:SMALL_ROWS]
    for block in range(dp):
        for piece in range(ctx):
            at = block * size + piece * share
            out_ref[block * share : (block + 1) * share, piece * own : (piece + 1) * own] = held[
                at : at + share, 3 * own : 4 * own
            ]


def unpack(places, parts, plan):
    dp, ctx, share, own, experts = plan
    size = parts[0].shape[0]
    width = dp * size
    return run(
        functools.partial(unpack_kernel, plan),
        "unpack",
        3,
        [places] + parts,
        [scalar] + [anywhere] * dp,
        [((width, LANES), bf16), ((SMALL_ROWS, width), f32), ((dp * share, ctx * own), bf16)],
        [inside] * 3,
        [pltpu.VMEM((width, 4 * own + LANES), bf16), pltpu.SemaphoreType.DMA((dp,))],
    )


def qkv_kernel(plan, scalars, small_ref, *refs):
    dp, ctx, rows, own, share = plan
    parts, tokens = refs[:dp], refs[dp : dp + ctx]
    qkv_ref, norm_ref, weight_ref, sems = refs[dp + ctx :]
    size = parts[0].shape[0]
    moves = [
        pltpu.make_async_copy(token, norm_ref.at[aligned(scalars[dp + i], rows)], sems.at[i])
        for i, token in enumerate(tokens)
    ] + [
        pltpu.make_async_copy(part, weight_ref.at[aligned(scalars[i], size)], sems.at[ctx + i])
        for i, part in enumerate(parts)
    ]
    start_all(moves)
    width = small_ref.shape[1]
    column = lax.broadcasted_iota(jnp.int32, (width, own), 1) + scalars[dp] * own
    source = lax.broadcasted_iota(jnp.int32, (width, own), 0)
    rank, inner = column // (2 * share), column % (2 * share)
    pair = small_ref[QV : QV + 2, :].astype(bf16)
    biases = []
    for part in range(2):
        picks = [
            (source == (rank + part * (width // (2 * share))) * share + inner - half * share)
            & (inner // share == half)
            for half in range(2)
        ]
        biases.append(
            sum(product(pair[half : half + 1], picks[half].astype(bf16)) for half in range(2))
        )
    bias = jnp.concatenate([biases[0], jnp.zeros_like(biases[0]), biases[1]], 1)
    gain, shift = small_ref[GAIN_ONE : GAIN_ONE + 1, :], small_ref[SHIFT_ONE : SHIFT_ONE + 1, :]
    wait_all(moves)
    tile = min(256, ctx * rows)
    for at in range(0, ctx * rows, tile):
        span = slice(at, at + tile)
        normed, _ = layer_stats(norm_ref[span, :].astype(f32))
        low = (normed * gain + shift).astype(bf16)
        norm_ref[span, :] = low
        qkv_ref[span, :] = (product(low, weight_ref[:, : 3 * own]) + bias).astype(bf16)


def make_qkv(scalars, small, parts, tokens, plan):
    dp, ctx, rows, own, share = plan
    width = tokens[0].shape[1]
    return run(
        functools.partial(qkv_kernel, plan),
        "norm_qkv",
        8,
        [scalars, small] + parts + tokens,
        [scalar, inside] + [anywhere] * (dp + ctx),
        [
            ((ctx * rows, 3 * own), bf16),
            ((ctx * rows, width), bf16),
            ((width, parts[0].shape[1]), bf16),
        ],
        [inside] * 3,
        [pltpu.SemaphoreType.DMA((dp + ctx,))],
    )


def score_parts(q_part, k_ref, column, step, block):
    scale = HEAD_DIM ** (-0.5)
    parts = []
    if step:
        parts.append(right_product(q_part, k_ref[0 : step * block, column]) * scale)
    diagonal = right_product(q_part, k_ref[step * block : (step + 1) * block, column]) * scale
    rows = lax.broadcasted_iota(jnp.int32, (block, block), 0)
    keys = lax.broadcasted_iota(jnp.int32, (block, block), 1)
    parts.append(jnp.where(keys <= rows, diagonal, -1e30))
    return parts


def softmax_of(parts):
    row_max = functools.reduce(jnp.maximum, [jnp.max(part, -1, keepdims=True) for part in parts])
    terms = [jnp.exp(part - row_max) for part in parts]
    total = functools.reduce(jnp.add, [jnp.sum(term, -1, keepdims=True) for term in terms])
    inverse = 1.0 / total
    return [term * inverse for term in terms]


def key_spans(step, block):
    spans = [slice(0, step * block)] if step else []
    return spans + [slice(step * block, (step + 1) * block)]


def attention_forward_kernel(heads, block, rows_each, scalars, q_ref, k_ref, v_ref, *refs):
    out_refs, (held, out_ref, sems) = refs[:-3], refs[-3:]
    for head in range(heads):
        column = slice(head * HEAD_DIM, (head + 1) * HEAD_DIM)
        for step in range(q_ref.shape[0] // block):
            rows = slice(step * block, (step + 1) * block)
            probs = softmax_of(score_parts(q_ref[rows, column], k_ref, column, step, block))
            mixed = functools.reduce(
                jnp.add,
                [
                    product(prob.astype(bf16), v_ref[span, column])
                    for prob, span in zip(probs, key_spans(step, block))
                ],
            )
            out_ref[rows, column] = mixed.astype(bf16)
    step_now, lanes = pl.program_id(0), out_ref.shape[1]
    if held.shape[1] == lanes:
        held[...] = out_ref[...]
    else:
        held[:, aligned(step_now, lanes)] = out_ref[...]

    @pl.when(step_now == pl.num_programs(0) - 1)
    def _():
        wait_all(
            start_all(
                [
                    pltpu.make_async_copy(held.at[aligned(scalars[i], rows_each)], ref, sems.at[i])
                    for i, ref in enumerate(out_refs)
                ]
            )
        )


def attention_backward_kernel(
    heads, block, rows, scalars, q_ref, k_ref, v_ref, *refs
):
    scale = HEAD_DIM ** (-0.5)
    pieces, (dq_ref, dk_ref, dv_ref, held, k_acc, v_acc, sems) = refs[:-7], refs[-7:]
    step_now, lanes = pl.program_id(0), dq_ref.shape[1]

    @pl.when(step_now == 0)
    def _():
        wait_all(
            start_all(
                [
                    pltpu.make_async_copy(piece, held.at[aligned(scalars[i], rows)], sems.at[i])
                    for i, piece in enumerate(pieces)
                ]
            )
        )

    grads = held[...] if held.shape[1] == lanes else held[:, aligned(step_now, lanes)]
    for head in range(heads):
        column = slice(head * HEAD_DIM, (head + 1) * HEAD_DIM)
        for step in reversed(range(q_ref.shape[0] // block)):
            span_rows = slice(step * block, (step + 1) * block)
            spans = key_spans(step, block)
            q_part, o_part = q_ref[span_rows, column], grads[span_rows, column]
            probs = softmax_of(score_parts(q_part, k_ref, column, step, block))
            prob_grads = [right_product(o_part, v_ref[span, column]) for span in spans]
            delta = functools.reduce(
                jnp.add,
                [jnp.sum(p * g, -1, keepdims=True) for p, g in zip(probs, prob_grads)],
            )
            score_grads = [(p * (g - delta)).astype(bf16) for p, g in zip(probs, prob_grads)]
            q_grad = functools.reduce(
                jnp.add,
                [product(s, k_ref[span, column]) for s, span in zip(score_grads, spans)],
            )
            dq_ref[span_rows, column] = (q_grad * scale).astype(bf16)
            first = step == q_ref.shape[0] // block - 1
            for span, score_grad, prob in zip(spans, score_grads, probs):
                key_grad = left_product(score_grad, q_part)
                value_grad = left_product(prob.astype(bf16), o_part)
                k_acc[span, column] = key_grad if first else k_acc[span, column] + key_grad
                v_acc[span, column] = value_grad if first else v_acc[span, column] + value_grad
    dk_ref[...] = (k_acc[...] * scale).astype(bf16)
    dv_ref[...] = v_acc[...].astype(bf16)


def attention_plan(qkv, width):
    length = qkv.shape[0]
    heads = min(2, width // HEAD_DIM)
    block = min(256, length)
    lanes = heads * HEAD_DIM
    steps = width // lanes
    whole = lanes % LANES == 0
    joined = [qkv] * 3 if whole else [qkv[:, i * width : (i + 1) * width] for i in range(3)]

    def spec(part):
        first = part * steps if whole else 0
        return pl.BlockSpec((length, lanes), lambda step: (0, first + step))

    return length, heads, block, lanes, steps, spec, joined


def attention_forward(scalars, qkv, width, rows):
    length, heads, block, lanes, steps, spec, joined = attention_plan(qkv, width)
    pieces = length // rows
    return run(
        functools.partial(attention_forward_kernel, heads, block, rows),
        "attention_forward",
        10,
        [scalars] + joined,
        [scalar, spec(0), spec(1), spec(2)],
        [((rows, width), bf16)] * pieces,
        [anywhere] * pieces,
        [
            pltpu.VMEM((length, width), bf16),
            pltpu.VMEM((length, lanes), bf16),
            pltpu.SemaphoreType.DMA((pieces,)),
        ],
        (steps,),
    )


def attention_backward(scalars, qkv, pieces, width):
    length, heads, block, lanes, steps, spec, joined = attention_plan(qkv, width)
    return run(
        functools.partial(attention_backward_kernel, heads, block, pieces[0].shape[0]),
        "attention_backward",
        18,
        [scalars] + joined + pieces,
        [scalar, spec(0), spec(1), spec(2)] + [anywhere] * len(pieces),
        [((length, width), bf16)] * 3,
        [spec(0)] * 3,
        [
            pltpu.VMEM((length, width), bf16),
            pltpu.VMEM((length, lanes), f32),
            pltpu.VMEM((length, lanes), f32),
            pltpu.SemaphoreType.DMA((len(pieces),)),
        ],
        (steps,),
    )


def hidden_kernel(ctx, scalars, small_ref, out_ref, tokens_ref, sort_ref, *refs):
    pieces, (hidden_ref, norm_ref, sorted_ref) = refs[:ctx], refs[ctx:]
    own = pieces[0].shape[1]
    hidden = tokens_ref[...].astype(f32) + (
        sum(
            product(piece[...], out_ref[aligned(scalars[i], own), :])
            for i, piece in enumerate(pieces)
        )
        + small_ref[OUT_BIAS : OUT_BIAS + 1, :]
    )
    hidden_ref[...] = hidden
    normed, _ = layer_stats(hidden)
    low = (
        normed * small_ref[GAIN_TWO : GAIN_TWO + 1, :] + small_ref[SHIFT_TWO : SHIFT_TWO + 1, :]
    ).astype(bf16)
    norm_ref[...] = low
    sorted_ref[...] = product(sort_ref[...], low).astype(bf16)


def make_hidden(scalars, small, full_out, tokens, sort, pieces):
    shape = tokens.shape
    return run(
        functools.partial(hidden_kernel, len(pieces)),
        "hidden",
        4,
        [scalars, small, full_out, tokens, sort] + pieces,
        [scalar] + [inside] * (4 + len(pieces)),
        [(shape, f32), (shape, bf16), (shape, bf16)],
        [inside] * 3,
        [],
    )


def mlp_kernel(plan, scalars, small_ref, by_column, *refs):
    dp, ctx, rows, start, count, expert, merged, last = plan
    base = 2 if expert == 1 else 0
    depth = dp // 2
    refs = list(refs)

    def take(number):
        taken = refs[:number]
        del refs[:number]
        return taken

    x_parts, g_parts = take(ctx), take(ctx)
    parts = take(dp if merged else 2 * dp)
    sums = take(6) if last else []
    if last:
        y_refs, gx_refs = take(ctx), take(ctx)
    else:
        y_ref, gx_ref, dots_out = take(3)
    (gb_ref,) = take(1)
    mine, other = take(1 if merged else 2), take(1 if merged else 2)
    up, down, x_all, x_turned, g_all, act_all, go_all, gu_all, up_grad, down_grad = take(10)
    pre_all, back_all = take(2)
    held = take(6) if last else take(2)
    in_sems, x_sems, out_sems, held_sems = take(4)
    width, hidden = up.shape
    up_rows, down_rows = width // dp, hidden // dp
    tile = min(256, hidden)
    tiles = [slice(at, at + tile) for at in range(0, hidden, tile)]
    total = ctx * count

    def loads(target, size, which):
        return [
            pltpu.make_async_copy(
                parts[i].at[base + which] if merged else parts[which * dp + i],
                target.at[aligned(scalars[i], size)],
                in_sems.at[which * dp + i],
            )
            for i in range(dp)
        ]

    def rows_of(block):
        return slice(block * count, (block + 1) * count)

    tokens = [
        pltpu.make_async_copy(
            part.at[start : start + count], x_all.at[rows_of(i)], x_sems.at[i]
        )
        for i, part in enumerate(x_parts)
    ]
    grads = [
        pltpu.make_async_copy(
            part.at[start : start + count], g_all.at[rows_of(i)], x_sems.at[ctx + i]
        )
        for i, part in enumerate(g_parts)
    ]
    ups, downs = loads(up, up_rows, 0), loads(down, down_rows, 1)
    start_all(tokens + ups + grads + downs)
    gathered = [
        pltpu.make_async_copy(ref, held[i], held_sems.at[i]) for i, ref in enumerate(sums)
    ]
    start_all(gathered)
    wait_all(tokens)
    logits = product(x_all[...], small_ref[...])
    route_zero, route_one = logits[:, ROUTER : ROUTER + 1], logits[:, ROUTER + 1 : ROUTER + 2]
    mix_zero, mix_one = logits[:, MIX : MIX + 1], logits[:, MIX + 1 : MIX + 2]
    if expert is None:
        mask = None
        coef = sigmoid_pair(mix_zero, mix_one)
    else:
        place = lax.broadcasted_iota(jnp.int32, (count, 1), 0) + start
        firsts = [place < scalars[dp + block] for block in range(ctx)]
        masks = [(first if expert == 0 else ~first).astype(f32) for first in firsts]
        mask = jnp.concatenate(masks, 0)
        gate = (
            sigmoid_pair(route_zero, route_one)
            if expert == 0
            else sigmoid_pair(route_one, route_zero)
        )
        coef = sigmoid_pair(mix_one, mix_zero) * gate * mask
    x_turned[...] = jnp.transpose(x_all[...])
    wait_all(grads)
    go_all[...] = (g_all[...].astype(f32) * coef).astype(bf16)
    wait_all(ups)

    piece = 64 if total % 64 == 0 else 16

    def activate(cut):
        bias = by_column[:, cut]
        column_sum = jnp.zeros((8, tile), f32)
        for at in range(0, total, piece):
            span = slice(at, at + piece)
            pre = pre_all[span, :] + bias
            square = pre * pre
            bend = jnp.tanh((ROOT * pre) * (1.0 + CUBE * square))
            half = 0.5 + 0.5 * bend
            act_all[span, cut] = (pre * half).astype(bf16)
            slope = half + ((0.5 * ROOT) * pre) * (1.0 - bend * bend) * (
                1.0 + (3.0 * CUBE) * square
            )
            grad_up = (back_all[span, :] * slope).astype(bf16)
            gu_all[span, cut] = grad_up
            column_sum = column_sum + jnp.sum(
                grad_up.astype(f32).reshape(piece // 8, 8, tile), 0
            )
        gb_ref[:, cut] = jnp.sum(column_sum, 0, keepdims=True)

    for number, cut in enumerate(tiles):
        pre_all[...] = product(x_all[...], up[:, cut])
        if number == 0:
            wait_all(downs)
        back_all[...] = right_product(go_all[...], down[cut, :])
        activate(cut)
        down_grad[cut, :] = left_product(act_all[:, cut], go_all[...]).astype(bf16)
        up_grad[:, cut] = product(x_turned[...], gu_all[:, cut]).astype(bf16)

    def stores(grad, size, which):
        targets = [
            (mine[0].at[i, which] if merged else mine[which].at[i])
            if i < depth
            else (other[0].at[i - depth, which] if merged else other[which].at[i - depth])
            for i in range(dp)
        ]
        return [
            pltpu.make_async_copy(
                grad.at[aligned(scalars[i], size)], target, out_sems.at[which * dp + i]
            )
            for i, target in enumerate(targets)
        ]

    saved = start_all(stores(up_grad, up_rows, 0) + stores(down_grad, down_rows, 1))
    wait_all(gathered)
    sums_sent = []
    for block in range(ctx):
        span = rows_of(block)
        out = product(act_all[span, :], down[...])
        grad_x = right_product(gu_all[span, :], up[...])
        dot = jnp.sum(g_all[span, :].astype(f32) * out, -1, keepdims=True)
        out = out * coef[span]
        if not last:
            held[0][span, :], held[1][span, :] = out, grad_x
            for number, target in enumerate((y_ref, gx_ref)):
                copy = pltpu.make_async_copy(
                    held[number].at[span], target.at[span], held_sems.at[2 * block + number]
                )
                copy.start()
                sums_sent.append(copy)
            dots_out[span, :] = dot if mask is None else dot * mask[span]
            continue
        y_dense, gx_dense, dots_dense, y_first, gx_first, dots_first = held
        whole = slice(block * rows, (block + 1) * rows)
        sets = ((y_dense, y_first, out, y_refs), (gx_dense, gx_first, grad_x, gx_refs))
        for dense, first, own, target in sets:
            early = dense[whole, :][:start] + first[span, :][:start]
            middle = dense[whole, :][start:count] + (first[span, :][start:] + own[: count - start])
            late = dense[whole, :][count:] + own[count - start :]
            target[block][0:start, 0:width] = early.astype(bf16)
            target[block][start:count, 0:width] = middle.astype(bf16)
            target[block][count:rows, 0:width] = late.astype(bf16)
        own_dot = dot * mask[span]
        first_dot = dots_first[span, :]
        moe = jnp.concatenate(
            [
                first_dot[:start],
                first_dot[start:] + own_dot[: count - start],
                own_dot[count - start :],
            ],
            0,
        )
        lane = lax.broadcasted_iota(jnp.int32, (rows, LANES), 1)
        both = jnp.where(lane % 2 == 0, dots_dense[whole, :], moe)
        high, middle, low = three_parts(both)
        extra = jnp.where(lane < 2, high.astype(f32), jnp.where(lane < 4, middle.astype(f32), low.astype(f32)))
        gx_refs[block][:, width:] = jnp.where(lane < 6, extra, 0.0).astype(bf16)
    wait_all(saved + sums_sent)


def mlp(scalars, small, bias, x, g, parts, expert, merged, sums):
    ctx = len(x)
    rows, width = x[0].shape
    dp = len(parts) if merged else len(parts) // 2
    depth = dp // 2
    hidden = bias.shape[1]
    count = rows if expert is None else rows * 5 // 8
    start = 0 if expert in (None, 0) else rows - count
    total = ctx * count
    last = expert == 1
    if merged:
        halves = [((depth, 2) + parts[0].shape[1:], bf16)]
    else:
        halves = [((depth,) + parts[0].shape, bf16), ((depth,) + parts[dp].shape, bf16)]
    if last:
        outs = [((rows, width), bf16)] * ctx + [((rows, width + LANES), bf16)] * ctx
    else:
        outs = [((total, width), f32), ((total, width), f32), ((total, 1), f32)]
    outs = outs + [((1, hidden), f32)] + halves + halves
    small_outs = len(outs) - 2 * len(halves)
    held = [pltpu.VMEM(ref.shape, f32) for ref in sums] or [pltpu.VMEM((total, width), f32)] * 2
    tile = min(256, hidden)
    return run(
        functools.partial(mlp_kernel, (dp, ctx, rows, start, count, expert, merged, last)),
        "mlp",
        20 if total % LANES == 0 and expert is None else 18,
        [scalars, small, bias] + x + g + parts + sums,
        [scalar, inside, inside] + [anywhere] * (2 * ctx + len(parts) + len(sums)),
        outs,
        ([] if last else [anywhere] * 2)
        + [inside] * (small_outs if last else small_outs - 2)
        + [anywhere] * (2 * len(halves)),
        [
            pltpu.VMEM((width, hidden), bf16),
            pltpu.VMEM((hidden, width), bf16),
            pltpu.VMEM((total, width), bf16),
            pltpu.VMEM((width, total), bf16),
            pltpu.VMEM((total, width), bf16),
            pltpu.VMEM((total, hidden), bf16),
            pltpu.VMEM((total, width), bf16),
            pltpu.VMEM((total, hidden), bf16),
            pltpu.VMEM((width, hidden), bf16),
            pltpu.VMEM((hidden, width), bf16),
            pltpu.VMEM((total, tile), f32),
            pltpu.VMEM((total, tile), f32),
        ]
        + held
        + [
            pltpu.SemaphoreType.DMA((2 * dp,)),
            pltpu.SemaphoreType.DMA((2 * ctx,)),
            pltpu.SemaphoreType.DMA((2 * dp,)),
            pltpu.SemaphoreType.DMA((max(2 * ctx, len(sums)),)),
        ],
    )


def middle_kernel(
    ctx, scalars, by_row, by_column, out_ref, hidden_ref, norm_ref, g_ref, first_ref, unsort_ref, *refs
):
    gx, pieces = refs[:ctx], refs[ctx : 2 * ctx]
    outs = refs[2 * ctx :]
    base_ref, grad_hidden_ref, rows_ref = outs[:3]
    out_grads, grad_pieces = outs[3 : 3 + ctx], outs[3 + ctx : 3 + 2 * ctx]
    out_all, sems = outs[3 + 2 * ctx :]
    rows, width = hidden_ref.shape
    own = pieces[0].shape[1]
    unsort = unsort_ref[...]
    gathered = sum(product(unsort, piece[...]) for piece in gx)
    grad_norm = gathered[:, :width]
    extra = gathered[:, width:]
    dense_dot = extra[:, 0:1] + (extra[:, 2:3] + extra[:, 4:5])
    moe_dot = extra[:, 1:2] + (extra[:, 3:4] + extra[:, 5:6])
    grad_out = g_ref[...].astype(f32)
    first = first_ref[...]
    down_bias = by_column[DOWN_BIAS : DOWN_BIAS + 1, :]
    moe_bias = jnp.where(
        first > 0.5,
        by_column[EXPERT_DOWN : EXPERT_DOWN + 1, :],
        by_column[EXPERT_DOWN + 1 : EXPERT_DOWN + 2, :],
    )
    dense_dot = dense_dot + jnp.sum(grad_out * down_bias, -1, keepdims=True)
    moe_dot = moe_dot + jnp.sum(grad_out * moe_bias, -1, keepdims=True)
    norm = norm_ref[...]
    logits = product(norm, by_row[...])
    route = [
        sigmoid_pair(logits[:, a : a + 1], logits[:, b : b + 1])
        for a, b in ((ROUTER, ROUTER + 1), (ROUTER + 1, ROUTER))
    ]
    mix = [
        sigmoid_pair(logits[:, a : a + 1], logits[:, b : b + 1])
        for a, b in ((MIX, MIX + 1), (MIX + 1, MIX))
    ]
    hot = [first, 1.0 - first]
    gate = route[0] * hot[0] + route[1] * hot[1]
    branch = mix[1] * gate
    hidden = hidden_ref[...]
    base_ref[...] = hidden + (mix[0] * down_bias + branch * moe_bias)
    grad_mix = [dense_dot, moe_dot * gate]
    mean_mix = mix[0] * grad_mix[0] + mix[1] * grad_mix[1]
    grad_gate = moe_dot * mix[1]
    grad_route = [hot[0] * grad_gate, hot[1] * grad_gate]
    mean_route = route[0] * grad_route[0] + route[1] * grad_route[1]
    lane = lax.broadcasted_iota(jnp.int32, (rows, LANES), 1)
    columns = [route[i] * (grad_route[i] - mean_route) for i in range(2)]
    columns += [mix[i] * (grad_mix[i] - mean_mix) for i in range(2)]
    logit_grads = jnp.zeros((rows, LANES), f32)
    for i, column in enumerate(columns):
        logit_grads = jnp.where((lane % 4 == i) & (lane < 12), column, logit_grads)
    high, middle, rest = [part.astype(f32) for part in three_parts(logit_grads)]
    split = jnp.where(lane < 4, high, jnp.where(lane < 8, middle, rest)).astype(bf16)
    grad_norm = grad_norm + right_product(split, by_row[...])
    small_grads = left_product(split, norm)
    small_grads = small_grads[0:4] + (small_grads[4:8] + small_grads[8:12])
    grad_dense = (grad_out * mix[0]).astype(bf16).astype(f32)
    grad_moe = (grad_out * branch).astype(bf16).astype(f32)
    normed, inverse = layer_stats(hidden)
    gain = by_column[GAIN_TWO : GAIN_TWO + 1, :]
    grad_hidden = grad_out + norm_back(grad_norm, normed, inverse, gain)
    grad_hidden_ref[...] = grad_hidden
    low = grad_hidden.astype(bf16)

    def total(values):
        return jnp.sum(values, 0, keepdims=True)

    sums = [
        total(low.astype(f32)),
        total(grad_norm * normed),
        total(grad_norm),
        total(grad_dense),
        total(grad_moe * hot[0]),
        total(grad_moe * hot[1]),
    ]
    rows_ref[...] = jnp.concatenate(sums + [small_grads, jnp.zeros((6, width), f32)], 0)
    for i, (piece, target) in enumerate(zip(pieces, grad_pieces)):
        span = aligned(scalars[i], own)
        target[...] = right_product(low, out_ref[span, :]).astype(bf16)
        part = left_product(piece[...], low).astype(bf16)
        share = out_all.shape[3]
        many = own // (ctx * share)
        for c in range(ctx):
            columns = part[:, c * own : (c + 1) * own].reshape(many, ctx, share, own)
            out_all[aligned(scalars[i], many), :, c] = columns
    wait_all(
        start_all(
            [
                pltpu.make_async_copy(out_all.at[:, scalars[i]], target, sems.at[i])
                for i, target in enumerate(out_grads)
            ]
        )
    )


def make_middle(
    scalars, by_row, by_column, full_out, hidden, norm, g, first, unsort, gx, pieces, dp
):
    ctx = len(gx)
    rows, width = hidden.shape
    own = pieces[0].shape[1]
    return run(
        functools.partial(middle_kernel, ctx),
        "middle",
        11,
        [scalars, by_row, by_column, full_out, hidden, norm, g, first, unsort] + gx + pieces,
        [scalar] + [inside] * (8 + 2 * ctx),
        [
            ((rows, width), f32),
            ((rows, width), f32),
            ((16, width), f32),
        ]
        + [((dp, ctx, width // (dp * ctx), own), bf16)] * ctx
        + [((rows, own), bf16)] * ctx,
        [inside] * 3 + [anywhere] * ctx + [inside] * ctx,
        [
            pltpu.VMEM((dp, ctx, ctx, width // (dp * ctx), own), bf16),
            pltpu.SemaphoreType.DMA((ctx,)),
        ],
    )


def qkv_back_kernel(plan, scalars, norm_ref, dq_ref, dk_ref, dv_ref, weight_ref, *refs):
    dp, ctx, rows, own = plan
    depth = dp // 2
    out_pieces, gn_refs = refs[:ctx], refs[ctx : 2 * ctx]
    mine, other, bias_ref, grad, weight_grad, gn, sems, gn_sems = refs[2 * ctx :]
    width = norm_ref.shape[1]
    size = width // dp
    for part, ref in enumerate((dq_ref, dk_ref, dv_ref)):
        grad[:, part * own : (part + 1) * own] = ref[...]
    tile = min(256, ctx * rows)
    weight = weight_ref[:, : 3 * own]
    for at in range(0, ctx * rows, tile):
        gn[at : at + tile, :] = right_product(grad[at : at + tile, :], weight).astype(bf16)
    sent = start_all(
        [
            pltpu.make_async_copy(gn.at[aligned(scalars[dp + i], rows)], ref, gn_sems.at[i])
            for i, ref in enumerate(gn_refs)
        ]
    )
    step = min(256, width)
    for at in range(0, width, step):
        weight_grad[at : at + step, : 3 * own] = left_product(
            norm_ref[:, at : at + step], grad[...]
        ).astype(bf16)
    weight_grad[:, 3 * own :] = sum(piece[...].astype(f32) for piece in out_pieces).astype(bf16)
    saved = start_all(
        [
            pltpu.make_async_copy(
                weight_grad.at[aligned(scalars[i], size)],
                mine.at[i] if i < depth else other.at[i - depth],
                sems.at[i],
            )
            for i in range(dp)
        ]
    )
    bias = jnp.sum(grad[...].astype(f32), 0, keepdims=True)
    here = lax.broadcasted_iota(jnp.int32, (1, width), 1) // own == scalars[dp]
    for row, at in enumerate((0, 2 * own)):
        spread = jnp.concatenate([bias[:, at : at + own]] * ctx, 1)
        bias_ref[row : row + 1, :] = jnp.where(here, spread, 0.0)
    wait_all(sent + saved)


def qkv_back(scalars, norm, grads, weight, out_pieces, plan):
    dp, ctx, rows, own = plan
    length, width = norm.shape
    half = ((dp // 2, width // dp, 4 * own), bf16)
    return run(
        functools.partial(qkv_back_kernel, plan),
        "qkv_back",
        8,
        [scalars, norm] + list(grads) + [weight] + list(out_pieces),
        [scalar] + [inside] * (5 + ctx),
        [((rows, width), bf16)] * ctx + [half, half, ((2, width), f32)],
        [anywhere] * (ctx + 2) + [inside],
        [
            pltpu.VMEM((length, 3 * own), bf16),
            pltpu.VMEM((width, 4 * own), bf16),
            pltpu.VMEM((length, width), bf16),
            pltpu.SemaphoreType.DMA((dp,)),
            pltpu.SemaphoreType.DMA((ctx,)),
        ],
    )


def final_kernel(ctx, order, by_column, tokens_ref, grad_hidden_ref, *refs):
    pieces, (grad_ref, rows_ref) = refs[:ctx], refs[ctx:]
    grad_norm = sum(piece[...].astype(f32) for piece in pieces)
    normed, inverse = layer_stats(tokens_ref[...].astype(f32))
    gain = by_column[GAIN_ONE : GAIN_ONE + 1, :]
    grad_ref[...] = grad_hidden_ref[...] + norm_back(grad_norm, normed, inverse, gain)
    rows_ref[0:1, :] = jnp.sum(grad_norm * normed, 0, keepdims=True)
    rows_ref[1:2, :] = jnp.sum(grad_norm, 0, keepdims=True)


def make_final(order, by_column, tokens, grad_hidden, pieces):
    return run(
        functools.partial(final_kernel, len(pieces)),
        "final",
        4,
        [order, by_column, tokens, grad_hidden] + pieces,
        [scalar] + [inside] * (3 + len(pieces)),
        [(tokens.shape, f32), ((2, tokens.shape[1]), f32)],
        [inside] * 2,
        [],
    )


def result_kernel(ctx, base_ref, unsort_ref, *refs):
    pieces, (out_ref,) = refs[:ctx], refs[ctx:]
    unsort = unsort_ref[...]
    out_ref[...] = base_ref[...] + sum(product(unsort, piece[...]) for piece in pieces)


def make_result(base, unsort, pieces):
    return run(
        functools.partial(result_kernel, len(pieces)),
        "result",
        3.5,
        [base, unsort] + pieces,
        [inside] * (2 + len(pieces)),
        [(base.shape, f32)],
        [inside],
        [],
    )[0]


def layer(
    dp,
    ctx,
    tokens,
    cotangent,
    routes,
    ln1_gain,
    ln1_bias,
    qkv_weight,
    qv_bias,
    out_weight,
    out_bias,
    ln2_gain,
    ln2_bias,
    up_weight,
    up_bias,
    down_weight,
    down_bias,
    router_weight,
    mix_weight,
    expert_up,
    expert_up_bias,
    expert_down,
    expert_down_bias,
):
    rows, width = tokens.shape[0] * tokens.shape[1], tokens.shape[2]
    experts, share, hidden = expert_up.shape
    own_hidden = hidden // ctx
    own_width = width // ctx
    unit = hidden // (dp * ctx)
    me = lax.axis_index("ctx")
    place_dp = lax.axis_index("dp")
    core = place_dp % 2
    depth = dp // 2
    shifts = range(1, ctx)
    ring_pairs = [(i, (i + 2) % dp) for i in range(dp)]
    core_pairs = [(i, i ^ 1) for i in range(dp)]
    places = jnp.stack(
        [
            ((place_dp // 2 + depth - t) % depth) * 2 + c
            for c in (core, 1 - core)
            for t in range(depth)
        ]
    ).astype(jnp.int32)
    peers = jnp.stack([me ^ s for s in range(ctx)]).astype(jnp.int32)

    def swap(array, shift):
        return lax.ppermute(array, "ctx", [(i, i ^ shift) for i in range(ctx)])

    def gather_ctx(array):
        return [array] + [swap(array, s) for s in shifts]

    def trade(pieces):
        return [pieces[0]] + [swap(pieces[s], s) for s in shifts]

    def by_peer(pieces):
        return [lax.dynamic_index_in_dim(pieces, me ^ s, 0, keepdims=False) for s in range(ctx)]

    def natural(pieces):
        whole = jnp.zeros((ctx,) + pieces[0].shape, pieces[0].dtype)
        for s, piece in enumerate(pieces):
            whole = lax.dynamic_update_slice_in_dim(whole, piece[None], me ^ s, 0)
        return whole

    def ring(array):
        return lax.ppermute(array, "dp", ring_pairs)

    def swap_core(array):
        return lax.ppermute(array, "dp", core_pairs)

    def sync(*trees):
        return lax.optimization_barrier(trees)

    class Rings:
        def __init__(self, arrays):
            self.parts = [list(arrays)]

        def move(self):
            self.parts.append([ring(array) for array in self.parts[-1]])

        def rest(self):
            while len(self.parts) < depth:
                self.move()

        def pieces(self, others, which):
            return [part[which] for part in self.parts] + [part[which] for part in others]

    def swap_cores(part):
        return [swap_core(array) for array in part]

    class Scatter:
        def __init__(self, *halves):
            half = len(halves) // 2
            self.mine, self.step = list(halves[:half]), 0
            self.got = [swap_core(other) for other in halves[half:]]
            self.arrived = self.sent = None

        def receive(self, others):
            if self.sent is None:
                self.got, others = sync(self.got, others)
            else:
                self.arrived, others = sync([ring(part) for part in self.sent], others)
            return others

        def add(self):
            self.step += 1
            at = self.step % depth
            parts = [m[at].astype(f32) + g[at].astype(f32) for m, g in zip(self.mine, self.got)]
            if self.arrived is not None:
                parts = [p + c.astype(f32) for p, c in zip(parts, self.arrived)]
            self.sent = [part.astype(bf16) if at else part for part in parts]

        def move(self, others):
            others = self.receive(others)
            self.add()
            return others

        def close(self):
            self.add()
            while self.step < depth:
                self.arrived = [ring(part) for part in self.sent]
                self.add()

    def pin(value, *sums):
        value, sent = sync(value, [one.sent for one in sums])
        for one, parts in zip(sums, sent):
            one.sent = parts
        return value

    def pair(sums):
        return sums if len(sums) == 2 else [sums[0][0], sums[0][1]]

    tokens = tokens.reshape(rows, width)
    cotangent = cotangent.reshape(rows, width)
    first_hot = routes.reshape(rows) == 0
    first_float = first_hot.astype(f32)
    first_count = jnp.sum(first_float)

    def column(vector):
        return vector.reshape(-1, share).T

    def bias_column(vector):
        return jnp.pad(vector.reshape(unit, 1), ((0, ctx * share - unit), (0, 0)))

    small = jnp.concatenate(
        [
            jnp.concatenate([router_weight, mix_weight] * 3, 1),
            column(ln1_gain),
            column(ln1_bias),
            column(qv_bias),
            column(out_bias),
            column(ln2_gain),
            column(ln2_bias),
            column(down_bias),
            expert_down_bias.T,
            jnp.broadcast_to(first_count.astype(bf16), (share, 1)),
        ],
        1,
    )
    small = jnp.pad(small, ((0, 0), (0, LANES - small.shape[1])))
    qkv_cut = qkv_weight.reshape(share, 3, ctx, own_width).transpose(2, 0, 1, 3)
    first_cut = jnp.concatenate(
        [
            qkv_cut.reshape(ctx, share, 3 * own_width),
            jnp.broadcast_to(small[None], (ctx, share, LANES)),
        ],
        -1,
    )
    ups = jnp.concatenate([up_weight[None], expert_up], 0)
    ups_cut = ups.reshape(experts + 1, share, dp, ctx, unit).transpose(3, 0, 1, 2, 4)
    ups_sent = by_peer(ups_cut.reshape(ctx, experts + 1, share, own_hidden))
    first_rows, ups_sent = sync(trade(by_peer(first_cut)), ups_sent)
    first_rows = natural(first_rows).reshape(ctx * share, 3 * own_width + LANES)
    qkv_rows = first_rows[:, : 3 * own_width]
    small_rows = first_rows[:, 3 * own_width :]
    counts = small_rows[::share, COUNT]
    bias_lanes = jnp.concatenate(
        [bias_column(up_bias)] + [bias_column(expert_up_bias[e]) for e in range(experts)], 1
    )
    lane = jnp.arange(LANES)[None, :]
    bias_lanes = jnp.pad(bias_lanes, ((0, 0), (UP_BIAS, LANES - UP_BIAS - bias_lanes.shape[1])))
    small_rows = jnp.where((lane >= UP_BIAS) & (lane < UP_BIAS + experts + 1), bias_lanes, small_rows)
    out_rows = out_weight.reshape(share, ctx, own_width).transpose(1, 0, 2)
    out_rows = out_rows.reshape(ctx * share, own_width)
    first = Rings([jnp.concatenate([qkv_rows, out_rows, small_rows], 1)])

    first.move()
    first_others = [swap_cores(first.parts[0])]
    token_parts = gather_ctx(tokens)
    first.parts[1], first_others[0] = sync(first.parts[1], first_others[0])
    first.move()
    first_others.append(swap_cores(first.parts[1]))
    token_parts, first.parts[2], first_others[1], ups_sent = sync(
        token_parts, first.parts[2], first_others[1], ups_sent
    )
    first.rest()
    first_others += [swap_cores(part) for part in first.parts[2:-1]]
    ups_rows, first.parts[-1], first_others = sync(trade(ups_sent), first.parts[-1], first_others)
    ups_rows = natural(ups_rows).transpose(1, 0, 2, 3)
    ups_rows = ups_rows.reshape(experts + 1, ctx * share, own_hidden)
    downs = [down_weight] + [expert_down[e] for e in range(experts)]
    merged = downs[0].shape == ups_rows.shape[1:]
    if merged:
        dense_weights = [jnp.stack([ups_rows[0], downs[0]])]
        expert_weights = [jnp.stack([ups_rows[1], downs[1], ups_rows[2], downs[2]])]
    else:
        dense_weights = [ups_rows[0], downs[0]]
        expert_weights = [ups_rows[1], downs[1], ups_rows[2], downs[2]]
    dense_ring = Rings(dense_weights)
    dense_ring.move()
    first_others.append(swap_cores(first.parts[-1]))
    first_parts = first.pieces(first_others, 0)
    plan = (dp, ctx, share, own_width, experts)
    by_row, by_column, out_own = unpack(places, first_parts, plan)
    expert_weights, by_row = sync(expert_weights, by_row)
    expert_ring = Rings(expert_weights)
    expert_ring.move()
    out_pieces = gather_ctx(out_own)

    order = jnp.arange(rows).astype(f32)
    counted = jnp.cumsum(first_float)
    place = jnp.where(first_hot, counted - 1.0, first_count + order - counted)
    unsort = (place[:, None] == order[None, :]).astype(bf16)
    sort = (place[None, :] == order[:, None]).astype(bf16)
    sorted_grad = product(sort, cotangent).astype(bf16)

    scalars = jnp.concatenate([places, peers])
    qkv, attn_in, own_qkv = make_qkv(
        scalars, by_column, first_parts, token_parts, (dp, ctx, rows, own_width, share)
    )
    qkv, dense_ring.parts[1] = sync(qkv, dense_ring.parts[1])
    dense_ring.move()
    attended_heads = list(attention_forward(peers, qkv, own_width, rows))
    attended_heads, out_pieces = sync(attended_heads, out_pieces)
    attended = trade(attended_heads)
    full_out = natural(out_pieces).reshape(ctx, dp, share, width).transpose(1, 0, 2, 3)
    full_out = full_out.reshape(width, width)
    hidden_state, ffn_in, sorted_in = make_hidden(
        peers, by_column, full_out, tokens, sort, attended
    )
    sorted_in, expert_ring.parts[1] = sync(sorted_in, expert_ring.parts[1])
    expert_ring.move()
    ffn_parts = gather_ctx(sorted_in)
    late_columns, late_counts, _ = sync(by_column, counts, sorted_in)
    row_counts = jnp.stack([late_counts[me ^ s] for s in range(ctx)]).astype(jnp.int32)
    mlp_scalars = jnp.concatenate([places, row_counts])
    up_biases = late_columns[UP_BIAS : UP_BIAS + experts + 1]
    up_biases = up_biases.reshape(experts + 1, dp, -1)[:, :, :unit].reshape(experts + 1, own_hidden)

    mlp_scalars = gate(mlp_scalars, *dense_ring.parts[2])
    ffn_parts, dense_ring.parts[2], sorted_grad, up_biases, mlp_scalars = sync(
        ffn_parts, dense_ring.parts[2], sorted_grad, up_biases, mlp_scalars
    )
    dense_ring.rest()
    grad_parts = [sorted_grad] + [swap(sorted_grad, s) for s in shifts[:2]]
    expert_ring.parts[2], late_grad = sync(expert_ring.parts[2], sorted_grad)
    expert_ring.rest()
    grad_parts += [swap(late_grad, s) for s in shifts[2:]]
    grad_parts, dense_ring.parts = sync(grad_parts, dense_ring.parts)
    dense_others = [swap_cores(part) for part in dense_ring.parts]
    dense_others, early = sync(dense_others, expert_ring.parts[:-1])
    expert_others = [swap_cores(part) for part in early]

    def run_mlp(which, held, parts, sums):
        return mlp(
            held,
            by_row,
            up_biases[which][None],
            ffn_parts,
            grad_parts,
            parts,
            which - 1 if which else None,
            merged,
            list(sums),
        )

    def weights_of(rings, others, first_array):
        if merged:
            return rings.pieces(others, 0)
        return rings.pieces(others, first_array) + rings.pieces(others, first_array + 1)

    dense = run_mlp(0, mlp_scalars, weights_of(dense_ring, dense_others, 0), [])
    sum_dense = Scatter(*dense[4:])
    expert_last, expert_others, gb_dense = sync(expert_ring.parts[-1], expert_others, dense[3])
    expert_ring.parts[-1] = expert_last
    expert_others = expert_others + [swap_cores(expert_last)]
    gb_dense = sum_dense.move(gb_dense)
    first_mlp = run_mlp(
        1,
        pin(gate(mlp_scalars), sum_dense),
        weights_of(expert_ring, expert_others, 0),
        [],
    )
    sum_first = Scatter(*first_mlp[4:])
    gb_first = sum_dense.move(first_mlp[3])
    second_mlp = run_mlp(
        2,
        pin(mlp_scalars, sum_dense),
        weights_of(expert_ring, expert_others, 2),
        dense[:3] + first_mlp[:3],
    )
    gb_second = sum_first.move(sum_dense.move(second_mlp[2 * ctx]))
    grad_sent = list(second_mlp[ctx : 2 * ctx])
    grad_pieces = trade(grad_sent[:3] + pin(grad_sent[3:], sum_dense, sum_first))
    grad_pieces, halves, result_sent = sync(
        grad_pieces, second_mlp[2 * ctx + 1 :], second_mlp[:ctx]
    )
    grad_pieces = sum_dense.receive(sum_first.move(grad_pieces))
    sum_second = Scatter(*halves)
    result_pieces = [result_sent[0]] + [swap(result_sent[s], s) for s in shifts[:2]]

    middle_peers, sum_dense.arrived = sync(peers, sum_dense.arrived)
    base, grad_hidden, middle_rows, *rest = make_middle(
        pin(middle_peers, sum_first),
        by_row,
        by_column,
        full_out,
        hidden_state,
        ffn_in,
        cotangent,
        first_float[:, None],
        unsort,
        grad_pieces,
        attended,
        dp,
    )
    out_sent, att_sent = rest[:ctx], rest[ctx:]
    result_pieces, att_sent = sync(result_pieces, att_sent)
    att_grads, out_sent = sync(trade(att_sent), out_sent)
    out_sent = [piece.reshape(width, own_width) for piece in out_sent]
    out_pieces = trade(out_sent)
    middle_rows = sum_second.move(sum_first.move(middle_rows))

    grad_heads = attention_backward(pin(peers, sum_first, sum_second), qkv, att_grads, own_width)
    grad_heads = sum_second.move(sum_first.receive(grad_heads))
    back_scalars, sum_first.arrived = sync(pin(scalars, sum_second), sum_first.arrived)
    *norm_grads, last_mine, last_other, grad_b_qkv = qkv_back(
        back_scalars,
        attn_in,
        grad_heads,
        own_qkv,
        out_pieces,
        (dp, ctx, rows, own_width),
    )
    sum_last = Scatter(last_mine, last_other)
    norm_pieces = [norm_grads[0]] + [swap(norm_grads[s], s) for s in shifts[:2]]
    late_pieces = [swap(norm_grads[s], s) for s in shifts[2:]]
    grad_b_qkv = sum_last.move(grad_b_qkv)
    norm_pieces[1] = sum_last.move(sum_second.move(norm_pieces[1]))
    small_sources = (grad_b_qkv, middle_rows, gb_dense, gb_first, gb_second)
    norm_pieces, small_sources, sum_dense.arrived, sum_first.arrived = pin(
        (norm_pieces, small_sources, sum_dense.arrived, sum_first.arrived), sum_last, sum_second
    )
    grad_b_qkv, middle_rows, gb_dense, gb_first, gb_second = small_sources
    norm_pieces += late_pieces

    def cut_columns(parts):
        joined = jnp.concatenate([part.astype(bf16) for part in parts], 1)
        return by_peer(joined.reshape(ctx, share, joined.shape[1]))

    def from_columns(pieces, at, size, groups):
        whole = natural([piece[:, at : at + size] for piece in pieces])
        whole = whole.reshape(ctx, share, groups, size // groups).transpose(1, 2, 0, 3)
        return whole.reshape(share, ctx * size).astype(f32)

    norm_pieces, result_sent = sync(norm_pieces, result_sent)
    result_pieces = result_pieces + [swap(result_sent[s], s) for s in shifts[2:]]
    grad_inputs, final_rows = make_final(peers, by_column, tokens, grad_hidden, norm_pieces)
    final_rows = pin(sum_last.move(final_rows), sum_last)
    final_rows, sum_dense.arrived, sum_first.arrived = sync(
        final_rows, sum_dense.arrived, sum_first.arrived
    )
    sum_dense.close()
    sum_first.close()

    small_rows = jnp.concatenate(
        [middle_rows[:10], final_rows, grad_b_qkv, jnp.zeros((2, width), f32)], 0
    )
    small_rows, result_pieces = sync(small_rows, result_pieces)
    small_pieces = gather_ctx(small_rows)

    small_pieces = sum_last.receive(sum_second.receive(small_pieces))
    sum_last.close()
    (last_sum,) = sum_last.sent
    qkv_part, out_sums = last_sum[:, : 3 * own_width], last_sum[:, 3 * own_width :]
    out_sums = out_sums.reshape(ctx, share, own_width).transpose(1, 0, 2).reshape(share, width)
    late_pieces = trade(cut_columns([qkv_part]))
    up_rows = jnp.concatenate([gb_dense, gb_first, gb_second, jnp.zeros((5, own_hidden), f32)], 0)
    up_rows = jnp.pad(up_rows, ((0, 0), (0, width - own_hidden)))
    small_sum = jnp.concatenate([sum(small_pieces), up_rows], 0)
    small_sum, late_pieces = sync(small_sum + swap_core(small_sum), late_pieces)
    pairs = [[(i, (i + 2 * t) % dp) for i in range(dp)] for t in range(depth)]
    small_sum = sum(
        [small_sum] + [lax.ppermute(small_sum, "dp", pairs[t]) for t in range(1, depth)]
    )
    sum_second.close()
    sums = [pair(one.sent) for one in (sum_dense, sum_first, sum_second)]
    early_sent, late_pieces = sync(cut_columns([one[0] for one in sums]), late_pieces)
    early_pieces = trade(early_sent)
    result = make_result(base, unsort, result_pieces)
    up_grads = [
        from_columns(early_pieces, which * own_hidden, own_hidden, dp)
        for which in range(experts + 1)
    ]
    qkv_grad = from_columns(late_pieces, 0, 3 * own_width, 3)
    down_sums = [one[1] for one in sums]
    owner = place_dp * ctx + me
    own = lax.dynamic_slice(small_sum, (0, owner * share), (12, share))
    own_qv = lax.dynamic_slice(small_sum[12:14].reshape(-1), (owner * 2 * share,), (2 * share,))
    own_up = lax.dynamic_slice(small_sum, (16, place_dp * unit), (3, unit))
    return (
        result[None],
        grad_inputs[None],
        own[10],
        own[11],
        qkv_grad,
        own_qv,
        out_sums,
        own[0],
        own[1],
        own[2],
        up_grads[0],
        own_up[0],
        down_sums[0],
        own[3],
        own[6:8].T,
        own[8:10].T,
        jnp.stack(up_grads[1:]),
        own_up[1:],
        jnp.stack(down_sums[1:]),
        own[4:6],
    )


def solution(mesh):
    both = ("dp", "ctx")
    data = P("dp", "ctx", None)
    vector = P(both)
    matrix = P(both, None)
    expert_matrix = P(None, both, None)
    expert_vector = P(None, both)
    weights = (
        vector,
        vector,
        matrix,
        vector,
        matrix,
        vector,
        vector,
        vector,
        matrix,
        vector,
        matrix,
        vector,
        matrix,
        matrix,
        expert_matrix,
        expert_vector,
        expert_matrix,
        expert_vector,
    )
    return jax.shard_map(
        functools.partial(layer, mesh.shape["dp"], mesh.shape["ctx"]),
        mesh=mesh,
        in_specs=(data, data, data) + weights,
        out_specs=(data, data) + weights,
        check_vma=False,
    )
```
